32 devices in a mesh: dp: 8 (over z, core), tensor: 4 (over y, x).
Axes of the slice: x: 2, y: 2, z: 4, core: 2. Of those that a mesh axis runs over, the one named last changes fastest.
Arguments:
- tokens: bfloat16 [2, 4096, 2048], P(None, ('dp', 'tensor')), may hold values from -6 to 6
- cotangent: bfloat16 [2, 4096, 2048], P(None, ('dp', 'tensor')), may hold values from -6 to 6
- mixer: bfloat16 [2048, 6144], P('dp', 'tensor'), may hold values from -0.125 to 0.125
- merger: bfloat16 [2048, 2048], P('tensor', 'dp'), may hold values from -1.5 to 1.5
- expand: bfloat16 [2048, 8192], P('dp', 'tensor'), may hold values from -0.125 to 0.125
- shrink: bfloat16 [8192, 2048], P('tensor', 'dp'), may hold values from -0.0625 to 0.0625
- attend_gain: bfloat16 [2048], replicated, may hold values from 0.5 to 1.5
- attend_bias: bfloat16 [2048], replicated, may hold values from -0.59765625 to 0.59765625
- feed_gain: bfloat16 [2048], replicated, may hold values from 0.5 to 1.5
- feed_bias: bfloat16 [2048], replicated, may hold values from -0.59765625 to 0.59765625
- width_router: bfloat16 [2048, 4], replicated, may hold values from -0.09375 to 0.09375
- head_router: bfloat16 [2048, 4], replicated, may hold values from -0.8984375 to 0.8984375
- lengths: int32 [2, 32], P(None, 'dp'), may hold values from 0 to 512, as said below
- head_choice: int32 [2, 32], P(None, 'dp'), may hold values from 0 to 3
- width_bucket: int32 [2, 4096], P(None, 'dp'), may hold values from 0 to 3
Outputs:
- block_output: bfloat16 [2, 4096, 2048], P(None, ('dp', 'tensor'))
- tokens_gradient: float32 [2, 4096, 2048], P(None, ('dp', 'tensor'))
- mixer_gradient: float32 [2048, 6144], P('dp', 'tensor')
- merger_gradient: float32 [2048, 2048], P('tensor', 'dp')
- expand_gradient: float32 [2048, 8192], P('dp', 'tensor')
- shrink_gradient: float32 [8192, 2048], P('tensor', 'dp')
- attend_gain_gradient: float32 [2048], replicated
- attend_bias_gradient: float32 [2048], replicated
- feed_gain_gradient: float32 [2048], replicated
- feed_bias_gradient: float32 [2048], replicated
- width_router_gradient: float32 [2048, 4], replicated
- head_router_gradient: float32 [2048, 4], replicated
- width_usage: float32 [4], replicated
- head_usage: float32 [4], replicated
The draws below stay inside these ranges and needn't reach their ends.
Inputs may be any that keep to these rules, and one draw needn't show every extreme that they name: For each micro-batch and each of the 8 buffers the 4 lengths sum to between 256 and 512; in each micro-batch one buffer holds a single sequence of 512 tokens.
All inputs are finite; a program needn't handle non-finite values.
Results may differ from the reference program's by a relative error of at most 0.012.
The reference program's roundings to bfloat16 on the way count: a program that leaves them out, or rounds other values in their place, can miss the bound.
Values may be sent and summed in bfloat16 or wider, within the bound.
A program may use at most 256 MiB of HBM per device.

```python
import jax
import jax.numpy as jnp
from jax import lax

D = 2048
H = 16
HD = 128
FF = 8192
NB = 4
NHC = 4
MB = 2
SEQ_DEV = 4
CAP = 512
TOKENS = 4096
SEQS = 32
N_DP = 8


def draw_lengths(key, part):
    key = jax.random.fold_in(key, 17)
    count_key, pick_key, cut_key = jax.random.split(key, 3)
    filled = jax.random.randint(count_key, (MB, N_DP), CAP // 2, CAP + 1)
    pick = jax.random.randint(pick_key, (MB, 1), 0, N_DP)
    whole = jnp.arange(N_DP)[None, :] == pick
    filled = jnp.where(whole, CAP, filled)
    cuts = jax.random.randint(cut_key, (MB, N_DP, SEQ_DEV - 1), 0, CAP + 1)
    cuts = jnp.minimum(cuts, filled[:, :, None])
    cuts = jnp.where(whole[:, :, None], filled[:, :, None], cuts)
    cuts = jnp.sort(cuts, axis=-1)
    edges = jnp.concatenate([jnp.zeros((MB, N_DP, 1), jnp.int32), cuts.astype(jnp.int32), filled[:, :, None].astype(jnp.int32)], axis=-1)
    return (edges[:, :, 1:] - edges[:, :, :-1]).reshape(MB, N_DP * SEQ_DEV).astype(jnp.int32)


def place_ends(drawn, stream_key, least, top_value):
    longest = drawn.shape.index(max(drawn.shape))
    spots = []
    for shift in (0, 1):
        where = [jax.random.randint(jax.random.fold_in(stream_key, axis), (), 0, length) for axis, length in enumerate(drawn.shape)]
        where[longest] = (where[longest] + shift) % drawn.shape[longest]
        spots.append(tuple(where))
    return drawn.at[spots[0]].set(least).at[spots[1]].set(top_value)


def levels(own_key, extent, cuts, smallest, largest):
    level, own = 1.0, jax.random.fold_in(own_key, 6)
    for position, shards_of in cuts:
        heights = jnp.exp(jax.random.uniform(jax.random.fold_in(own, position), (shards_of,), jnp.float32, smallest / len(cuts), largest / len(cuts)))
        level = level * jnp.repeat(heights, extent[position] // shards_of).reshape([-1 if axis == position else 1 for axis in range(len(extent))])
    return level


def bell_draw(own_key, extent, deviation, most, cuts=(), kind=jnp.bfloat16):
    loudness = levels(own_key, extent, cuts, -0.22, 0.18) if cuts else 1.0
    drawn = jax.random.normal(own_key, extent, jnp.float32) * deviation * loudness
    return jnp.minimum(jnp.maximum(drawn, -most), most).astype(kind)


def setup_inputs(seed: int = 0) -> dict:
    seeds = jax.random.split(jax.random.key(seed), 16)
    tokens = bell_draw(seeds[0], (MB, TOKENS, D), 1.0, 6.0, ((1, 32),))
    cotangent = bell_draw(seeds[1], (MB, TOKENS, D), 1.0, 6.0, ((1, 32),))
    mixer = bell_draw(seeds[2], (D, 3 * H * HD), D ** -0.5, 0.125, ((0, 8), (1, 4)))
    merger = bell_draw(seeds[3], (H * HD, D), (H * HD * 4 // CAP) ** -0.5, 1.5, ((0, 4), (1, 8)))
    expand = bell_draw(seeds[4], (D, FF), D ** -0.5, 0.125, ((0, 8), (1, 4)))
    shrink = bell_draw(seeds[5], (FF, D), FF ** -0.5, 0.0625, ((0, 4), (1, 8)))
    attend_gain = jnp.clip(1.0 + 0.1 * jax.random.normal(seeds[6], (D,), jnp.float32), 0.5, 1.5).astype(jnp.bfloat16)
    attend_bias = bell_draw(seeds[7], (D,), 0.1, 0.59765625)
    feed_gain = jnp.clip(1.0 + 0.1 * jax.random.normal(seeds[8], (D,), jnp.float32), 0.5, 1.5).astype(jnp.bfloat16)
    feed_bias = bell_draw(seeds[9], (D,), 0.1, 0.59765625)
    width_router = bell_draw(seeds[10], (D, NB), (2 * D) ** -0.5, 0.09375)
    head_router = bell_draw(seeds[11], (D, NHC), 0.15, 0.8984375)
    lengths = draw_lengths(jax.random.fold_in(seeds[15], 71), 0)
    head_choice = place_ends(jax.random.randint(seeds[13], (MB, SEQS), 0, NHC), jax.random.fold_in(seeds[13], 1), 0, NHC - 1).astype(jnp.int32)
    width_bucket = place_ends(jax.random.randint(seeds[14], (MB, TOKENS), 0, NB), jax.random.fold_in(seeds[14], 1), 0, NB - 1).astype(jnp.int32)
    return dict(tokens=tokens, cotangent=cotangent, mixer=mixer, merger=merger, expand=expand, shrink=shrink, attend_gain=attend_gain, attend_bias=attend_bias, feed_gain=feed_gain, feed_bias=feed_bias, width_router=width_router, head_router=head_router, lengths=lengths, head_choice=head_choice, width_bucket=width_bucket)


@jax.custom_vjp
def low(v):
    return lax.optimization_barrier(v.astype(jnp.bfloat16)).astype(jnp.float32)

@jax.custom_vjp
def low_back(v):
    return v

def low_keep(v):
    return (low(v), None)

def low_pass(kept, grad):
    return (grad,)

def back_keep(v):
    return (v, None)

def back_low(kept, grad):
    return (low(grad),)
low.defvjp(low_keep, low_pass)
low_back.defvjp(back_keep, back_low)
EPSILON = 1e-05
HIGHEST = lax.Precision.HIGHEST
MASKED = -1e+30

def layout(lengths):
    ends = jnp.cumsum(lengths, dtype=jnp.int32)
    starts = ends - lengths
    filled = ends[-1]
    slots = jnp.arange(CAP, dtype=jnp.int32)
    member = lax.optimization_barrier(jnp.sum((ends[None, :] <= slots[:, None]).astype(jnp.int32), axis=1, dtype=jnp.int32))
    begins = jnp.concatenate([starts, filled[None]])
    onehot = member[:, None] == jnp.arange(SEQ_DEV + 1, dtype=jnp.int32)[None, :]
    place = slots - lax.optimization_barrier(jnp.sum(jnp.where(onehot, begins[None, :], 0), axis=1, dtype=jnp.int32))
    return (member, place, slots < filled, onehot[:, :SEQ_DEV])

def layer_norm(value, gain, bias):
    centred = value - lax.optimization_barrier(jnp.mean(value, axis=-1, keepdims=True))
    return centred * lax.rsqrt(lax.optimization_barrier(jnp.mean(centred * centred, axis=-1, keepdims=True)) + EPSILON) * gain + bias

def rotary_tables(place):
    half = HD // 2
    rates = jnp.power(10000.0, -2.0 * jnp.arange(half, dtype=jnp.float32) / HD)
    angles = place.astype(jnp.float32)[:, None] * rates[None, :]
    cosine = jnp.cos(angles)
    sine = jnp.sin(angles)
    return (jnp.concatenate([cosine, cosine], axis=1), jnp.concatenate([sine, sine], axis=1))

def rotate(value, cosine, sine):
    half = value.shape[-1] // 2
    turned = jnp.concatenate([-value[..., half:], value[..., :half]], axis=-1)
    return value * cosine + turned * sine

def softmax_rows(logits):
    powers = jnp.exp(logits - lax.optimization_barrier(jnp.max(logits, axis=-1, keepdims=True)))
    return powers / lax.optimization_barrier(jnp.sum(powers, axis=-1, keepdims=True))

def buffer_forward(params, tokens, lengths, choices, buckets):
    mixer, merger, expand, shrink, attend_gain, attend_bias, feed_gain, feed_bias, width_router, head_router = params
    member, place, live, seqmask = layout(lengths)
    seq_float = seqmask.astype(jnp.float32)
    normed = low(layer_norm(tokens, attend_gain, attend_bias))
    divisor = jnp.maximum(lax.optimization_barrier(jnp.sum(seq_float, axis=0)), 1.0)
    means = jnp.dot(seq_float.T, normed, precision=HIGHEST) / divisor[:, None]
    head_share = softmax_rows(jnp.dot(means, head_router, precision=HIGHEST))
    choice_hot = (choices[:, None] == jnp.arange(NHC, dtype=jnp.int32)[None, :]).astype(jnp.float32)
    seq_gate = NHC * lax.optimization_barrier(jnp.sum(head_share * choice_hot, axis=1))
    token_gate = jnp.dot(seq_float, seq_gate, precision=HIGHEST)
    heads_used = lax.optimization_barrier(jnp.sum(jnp.where(seqmask, H // NHC * (choices[None, :] + 1), 0), axis=1, dtype=jnp.int32))
    head_on = (jnp.arange(H, dtype=jnp.int32)[None, :] < heads_used[:, None]).astype(jnp.float32)
    mixed = low_back(jnp.dot(normed, mixer, precision=HIGHEST)).reshape(CAP, H, 3, HD)
    cosine, sine = rotary_tables(place)
    query = low(rotate(mixed[:, :, 0], cosine[:, None], sine[:, None]))
    keys = low(rotate(mixed[:, :, 1], cosine[:, None], sine[:, None]))
    values = low(mixed[:, :, 2])
    block = min(512, CAP)
    slots = jnp.arange(CAP, dtype=jnp.int32)

    def attend(index):
        start = index * block
        rows = lax.dynamic_slice_in_dim(query, start, block, 0)
        row_member = lax.dynamic_slice_in_dim(member, start, block, 0)
        row_slot = start + jnp.arange(block, dtype=jnp.int32)
        scores = low_back(jnp.einsum('qhd,khd->hqk', rows, keys, precision=HIGHEST) * HD ** (-0.5))
        allowed = (row_member[:, None] == member[None, :]) & (row_slot[:, None] >= slots[None, :])
        scores = jnp.where(allowed[None], scores, MASKED)
        share = low(softmax_rows(scores))
        return jnp.einsum('hqk,khd->qhd', share, values, precision=HIGHEST)
    heads_out = lax.map(jax.checkpoint(attend), jnp.arange(CAP // block, dtype=jnp.int32)).reshape(CAP, H, HD)
    heads_out = low_back(low(heads_out)) * head_on[:, :, None]
    attended = low_back(jnp.dot(heads_out.reshape(CAP, H * HD), merger, precision=HIGHEST))
    hidden = tokens + token_gate[:, None] * attended
    second = low(layer_norm(hidden, feed_gain, feed_bias))
    width_share = softmax_rows(jnp.dot(second, width_router, precision=HIGHEST))
    bucket_hot = (buckets[:, None] == jnp.arange(NB, dtype=jnp.int32)[None, :]).astype(jnp.float32)
    width_gate = NB * lax.optimization_barrier(jnp.sum(width_share * bucket_hot, axis=1))
    before = low_back(jnp.dot(second, expand, precision=HIGHEST))
    unit_on = (jnp.arange(FF, dtype=jnp.int32)[None, :] < FF // NB * (buckets[:, None] + 1)).astype(jnp.float32)
    rectified = jnp.maximum(before, 0.0)
    active = low(rectified * rectified * unit_on)
    branch = low_back(jnp.dot(active, shrink, precision=HIGHEST))
    return live.astype(jnp.float32)[:, None] * (hidden + width_gate[:, None] * branch)

def reference(tokens, cotangent, mixer, merger, expand, shrink, attend_gain, attend_bias, feed_gain, feed_bias, width_router, head_router, lengths, head_choice, width_bucket):
    buffers = MB * N_DP
    inputs = tokens.astype(jnp.float32).reshape(buffers, CAP, D)
    backs = cotangent.astype(jnp.float32).reshape(buffers, CAP, D)
    length_rows = lengths.reshape(buffers, SEQ_DEV)
    choice_rows = head_choice.reshape(buffers, SEQ_DEV)
    bucket_rows = width_bucket.reshape(buffers, CAP)
    params = tuple((piece.astype(jnp.float32) for piece in (mixer, merger, expand, shrink, attend_gain, attend_bias, feed_gain, feed_bias, width_router, head_router)))
    stepper = jax.checkpoint(buffer_forward)

    def forward(inputs, params):

        def scan_step(carry, pieces):
            return (carry, stepper(params, *pieces))
        return lax.scan(scan_step, jnp.zeros((), jnp.float32), (inputs, length_rows, choice_rows, bucket_rows))[1]
    outputs, pullback = jax.vjp(forward, inputs, params)
    input_back, param_back = pullback(backs)
    member_all, place_all, live_all, seq_all = jax.vmap(layout)(length_rows)
    live_float = live_all.astype(jnp.float32)
    bucket_hot = (bucket_rows[..., None] == jnp.arange(NB, dtype=jnp.int32)).astype(jnp.float32)
    width_usage = lax.optimization_barrier(jnp.sum(live_float[..., None] * bucket_hot, axis=(0, 1)))
    token_choice = lax.optimization_barrier(jnp.sum(jnp.where(seq_all, choice_rows[:, None, :], 0), axis=2, dtype=jnp.int32))
    choice_hot = (token_choice[..., None] == jnp.arange(NHC, dtype=jnp.int32)).astype(jnp.float32)
    head_usage = lax.optimization_barrier(jnp.sum(live_float[..., None] * choice_hot, axis=(0, 1)))
    return (outputs.reshape(MB, TOKENS, D).astype(jnp.bfloat16), input_back.reshape(MB, TOKENS, D), param_back[0], param_back[1], param_back[2], param_back[3], param_back[4], param_back[5], param_back[6], param_back[7], param_back[8], param_back[9], width_usage, head_usage)
```

```python
import jax
import jax.numpy as jnp
from jax import lax
from jax.sharding import PartitionSpec as P

H = 16
HD = 128
FF = 8192
NB = 4
NHC = 4


EPSILON = 1e-05
HIGHEST = lax.Precision.HIGHEST
MASKED = -1e30
BF16 = jnp.bfloat16
F32 = jnp.float32


def contract_rows(left, right):
    return lax.dot_general(left, right, (((0,), (0,)), ((), ())), preferred_element_type=F32)


def contract_cols(left, right):
    return lax.dot_general(left, right, (((1,), (1,)), ((), ())), preferred_element_type=F32)


def swap_low(value, size):
    return lax.ppermute(value, "tensor", [(i, i ^ 1) for i in range(size)])


def from_high(value, size, step):
    high = size // 2
    pairs = [(((h + step) % high) * 2 + l, h * 2 + l) for h in range(high) for l in range(2)]
    return lax.ppermute(value, "tensor", pairs)


def to_high(value, size, step):
    high = size // 2
    pairs = [(h * 2 + l, ((h + step) % high) * 2 + l) for h in range(high) for l in range(2)]
    return lax.ppermute(value, "tensor", pairs)


def arrival_parts(rank, size):
    high = size // 2
    hi, lo = rank // 2, rank % 2
    first = [((hi + s) % high) * 2 + (lo + l) % 2 for s in range(high) for l in range(2)]
    second = [((hi + s) % high) * 2 + (lo + l) % 2 for l in range(2) for s in range(high)]
    return first, second


def gather_rows(own, size):
    half = own.shape[0] // 2
    high = size // 2
    first, second = own[:half], own[half:]
    first = jnp.concatenate([first, swap_low(first, size)], axis=0)
    second = jnp.concatenate(
        [second] + [from_high(second, size, s) for s in range(1, high)], axis=0
    )
    blocks = [first] + [from_high(first, size, s) for s in range(1, high)]
    blocks += [second, swap_low(second, size)]
    return jnp.concatenate(blocks, axis=0)


def scatter_rows(part, size):
    half = part.shape[0] // (2 * size)
    high = size // 2
    first, second = part[: half * size], part[half * size :]
    first_sum = first[: 2 * half].astype(F32)
    for s in range(1, high):
        sent = to_high(first[2 * half * s : 2 * half * (s + 1)], size, s)
        first_sum = first_sum + sent.astype(F32)
    second_sum = second[: high * half].astype(F32)
    second_sum = second_sum + swap_low(second[high * half :], size).astype(F32)
    first_own = first_sum[:half] + swap_low(first_sum[half:].astype(BF16), size).astype(F32)
    second_own = second_sum[:half]
    for s in range(1, high):
        sent = to_high(second_sum[half * s : half * (s + 1)].astype(BF16), size, s)
        second_own = second_own + sent.astype(F32)
    return jnp.concatenate([first_own, second_own], axis=0)


def butterfly(value, axis, size):
    step = 1
    while step < size:
        value = value + lax.ppermute(value, axis, [(i, i ^ step) for i in range(size)])
        step *= 2
    return value


def normalize(value):
    centred = value - jnp.mean(value, axis=-1, keepdims=True)
    inverse = lax.rsqrt(jnp.mean(centred * centred, axis=-1, keepdims=True) + EPSILON)
    return (centred * inverse, inverse)


def norm_back(back, normed, inverse, gain):
    scaled = back * gain
    inner = jnp.mean(scaled, axis=-1, keepdims=True)
    along = jnp.mean(scaled * normed, axis=-1, keepdims=True)
    return inverse * (scaled - inner - normed * along)


def rotary_tables(place, width):
    half = width // 2
    rates = jnp.power(10000.0, -2.0 * jnp.arange(half, dtype=F32) / width)
    angles = place.astype(F32)[:, None] * rates[None, :]
    cosine = jnp.cos(angles)
    sine = jnp.sin(angles)
    return (jnp.concatenate([cosine, cosine], axis=1), jnp.concatenate([sine, sine], axis=1))


def rotate(value, cosine, sine):
    half = value.shape[-1] // 2
    turned = jnp.concatenate([-value[..., half:], value[..., :half]], axis=-1)
    return value * cosine + turned * sine


def rotate_back(grad_value, cosine, sine):
    moved = grad_value * sine
    half = moved.shape[-1] // 2
    return grad_value * cosine + jnp.concatenate([moved[..., half:], -moved[..., :half]], axis=-1)


def softmax_rows(logits):
    powers = jnp.exp(logits - jnp.max(logits, axis=-1, keepdims=True))
    return powers / jnp.sum(powers, axis=-1, keepdims=True)


def place_rows(lengths, slots):
    slot_count = lengths.shape[0]
    ends = jnp.cumsum(lengths, dtype=jnp.int32)
    starts = ends - lengths
    filled = ends[-1]
    member = jnp.sum((ends[None, :] <= slots[:, None]).astype(jnp.int32), axis=1, dtype=jnp.int32)
    begins = jnp.concatenate([starts, filled[None]])
    onehot = member[:, None] == jnp.arange(slot_count + 1, dtype=jnp.int32)[None, :]
    place = slots - jnp.sum(jnp.where(onehot, begins[None, :], 0), axis=1, dtype=jnp.int32)
    return (member, place, slots < filled, onehot[:, :slot_count])


def block_scores(query, keys, member, slots):
    scale = query.shape[-1] ** (-0.5)
    seen = (member[:, None] == member[None, :]) & (slots[:, None] >= slots[None, :])
    scores = jnp.einsum("qhd,khd->hqk", query, keys, preferred_element_type=F32) * scale
    return jnp.where(seen[None], scores, MASKED)


def attend_forward(query, keys, values, member, slots):
    scores = block_scores(query, keys, member, slots)
    peak = jnp.max(scores, axis=-1, keepdims=True)
    powers = jnp.exp(scores - peak)
    mass = jnp.sum(powers, axis=-1, keepdims=True)
    share = (powers / mass).astype(BF16)
    pieces = jnp.einsum("hqk,khd->qhd", share, values, preferred_element_type=F32)
    return (pieces, peak + jnp.log(mass))


def attend_backward(query, keys, values, member, slots, log_total, heads_back):
    scale = query.shape[-1] ** (-0.5)
    scores = block_scores(query, keys, member, slots)
    share = jnp.exp(scores - log_total)
    share_back = jnp.einsum("qhd,khd->hqk", heads_back, values, preferred_element_type=F32)
    inner = jnp.sum(share * share_back, axis=-1, keepdims=True)
    score_back = (share * (share_back - inner)).astype(BF16)
    query_back = jnp.einsum("hqk,khd->qhd", score_back, keys, preferred_element_type=F32) * scale
    keys_back = jnp.einsum("hqk,qhd->khd", score_back, query, preferred_element_type=F32) * scale
    values_back = jnp.einsum(
        "hqk,qhd->khd", share.astype(BF16), heads_back, preferred_element_type=F32
    )
    return (query_back, keys_back, values_back)


def after(value, *others):
    return lax.optimization_barrier((value,) + others)[0]


def gather_weights(piece):
    return lax.all_gather(piece, "dp", axis=0, tiled=False)


def local(
    dp_size,
    size,
    tokens,
    cotangent,
    mixer,
    merger,
    expand,
    shrink,
    attend_gain,
    attend_bias,
    feed_gain,
    feed_bias,
    width_router,
    head_router,
    lengths,
    head_choice,
    width_bucket,
):
    rank = lax.axis_index("tensor")
    micro, rows, width = tokens.shape
    total = width_bucket.shape[1]
    half = rows // 2
    heads_local = merger.shape[0] // HD
    units_local = expand.shape[1]
    head_ids = rank * heads_local + jnp.arange(heads_local, dtype=jnp.int32)
    unit_ids = rank * units_local + jnp.arange(units_local, dtype=jnp.int32)
    gain_one = attend_gain.astype(F32)
    bias_one = attend_bias.astype(F32)
    gain_two = feed_gain.astype(F32)
    bias_two = feed_bias.astype(F32)
    router_width = width_router.astype(F32)
    router_head = head_router.astype(F32)

    mix_weight = gather_weights(mixer)
    out_weight = gather_weights(after(merger, mix_weight))
    up_weight = gather_weights(after(expand, out_weight))
    down_weight = gather_weights(after(shrink, up_weight))
    mix_weight = mix_weight.reshape(width, -1)
    up_weight = up_weight.reshape(width, -1)

    first_ranks, second_ranks = arrival_parts(rank, size)
    row_starts = [r * rows for r in first_ranks] + [r * rows + half for r in second_ranks]
    slots = jnp.concatenate([start + jnp.arange(half, dtype=jnp.int32) for start in row_starts])
    own_slots = rank * rows + jnp.arange(rows, dtype=jnp.int32)

    state = []
    for m in range(micro):
        s = {}
        state.append(s)
        s["member"], s["place"], _, s["seqmask"] = place_rows(lengths[m], slots)
        _, _, own_live, own_seq = place_rows(lengths[m], own_slots)
        s["own_live"] = own_live.astype(F32)
        s["own_seq"] = own_seq.astype(F32)
        s["buckets"] = jnp.concatenate(
            [lax.dynamic_slice_in_dim(width_bucket[m], start, half, 0) for start in row_starts]
        )
        own_buckets = lax.dynamic_slice_in_dim(width_bucket[m], rank * rows, rows, 0)
        s["bucket_hot"] = (
            own_buckets[:, None] == jnp.arange(NB, dtype=jnp.int32)[None, :]
        ).astype(F32)
        choices = head_choice[m]
        s["choice_hot"] = (
            choices[:, None] == jnp.arange(NHC, dtype=jnp.int32)[None, :]
        ).astype(F32)
        s["cosine"], s["sine"] = [t[:, None, :] for t in rotary_tables(s["place"], HD)]
        heads_used = jnp.sum(
            jnp.where(s["seqmask"], H // NHC * (choices[None, :] + 1), 0), axis=1, dtype=jnp.int32
        )
        s["head_on"] = (head_ids[None, :] < heads_used[:, None]).astype(BF16)
        s["unit_on"] = (unit_ids[None, :] < FF // NB * (s["buckets"][:, None] + 1)).astype(F32)
        s["inputs"] = tokens[m].astype(F32)
        s["outer"] = cotangent[m].astype(F32) * s["own_live"][:, None]
        s["first_normed"], s["first_inverse"] = normalize(s["inputs"])
        s["first_low"] = (s["first_normed"] * gain_one + bias_one).astype(BF16)

    for s in state:
        s["first_rows"] = gather_rows(s["first_low"], size)

    for s in state:
        seq_float = s["seqmask"].astype(F32)
        s["divisor"] = jnp.maximum(jnp.sum(seq_float, axis=0), 1.0)
        sums = jnp.dot(seq_float.T.astype(BF16), s["first_rows"], preferred_element_type=F32)
        means = sums / s["divisor"][:, None]
        s["head_share"] = softmax_rows(jnp.dot(means, router_head, precision=HIGHEST))
        s["picked_head"] = jnp.sum(s["head_share"] * s["choice_hot"], axis=1)
        s["own_gate"] = jnp.sum(s["own_seq"] * (NHC * s["picked_head"])[None, :], axis=1)

    for s in state:
        mixed = jnp.dot(s["first_rows"], mix_weight, preferred_element_type=F32).reshape(
            total, heads_local, 3, HD
        )
        s["query"] = rotate(mixed[:, :, 0], s["cosine"], s["sine"]).astype(BF16)
        s["keys"] = rotate(mixed[:, :, 1], s["cosine"], s["sine"]).astype(BF16)
        s["values"] = mixed[:, :, 2].astype(BF16)
        attended, s["log_total"] = attend_forward(
            s["query"], s["keys"], s["values"], s["member"], slots
        )
        s["head_rows"] = (attended.astype(BF16) * s["head_on"][:, :, None]).reshape(
            total, heads_local * HD
        )
        part = lax.dot_general(
            s["head_rows"], out_weight, (((1,), (1,)), ((), ())), preferred_element_type=F32
        )
        s["attention_own"] = scatter_rows(part.astype(BF16).reshape(total, width), size)

    for s in state:
        hidden = s["inputs"] + s["own_gate"][:, None] * s["attention_own"]
        s["hidden"] = hidden
        s["second_normed"], s["second_inverse"] = normalize(hidden)
        s["second_low"] = (s["second_normed"] * gain_two + bias_two).astype(BF16)
        s["width_share"] = softmax_rows(
            jnp.dot(s["second_low"], width_router, preferred_element_type=F32)
        )
        s["picked_width"] = jnp.sum(s["width_share"] * s["bucket_hot"], axis=1)
        s["width_gate"] = NB * s["picked_width"]
        s["second_rows"] = gather_rows(s["second_low"], size)
    for s in state:
        branch_back = (s["width_gate"][:, None] * s["outer"]).astype(BF16)
        s["branch_rows"] = gather_rows(branch_back, size)

    for s in state:
        before = jnp.dot(s["second_rows"], up_weight, preferred_element_type=F32)
        s["rectified"] = jnp.maximum(before, 0.0) * s["unit_on"]
        s["active"] = (s["rectified"] * s["rectified"]).astype(BF16)

    def over_micro(left, right):
        return sum(contract_rows(s[left], s[right]) for s in state).astype(BF16)

    def columns_first(term):
        return jnp.swapaxes(term.reshape(term.shape[0], dp_size, -1), 0, 1)

    def share_out(term):
        return lax.psum_scatter(term, "dp", scatter_dimension=0, tiled=False).astype(F32)

    down_sum = share_out(columns_first(over_micro("active", "branch_rows")))

    outputs = []
    for s in state:
        part = lax.dot_general(
            s["active"], down_weight, (((1,), (1,)), ((), ())), preferred_element_type=F32
        )
        branch_own = scatter_rows(part.astype(BF16).reshape(total, width), size)
        outputs.append(
            (
                s["own_live"][:, None] * (s["hidden"] + s["width_gate"][:, None] * branch_own)
            ).astype(BF16)
        )
        s["width_gate_back"] = jnp.sum(s["outer"] * branch_own, axis=1)
    for s in state:
        branch_rows = s["branch_rows"].reshape(total, dp_size, -1)
        active_back = lax.dot_general(
            branch_rows, down_weight, (((1, 2), (0, 2)), ((), ())), preferred_element_type=F32
        )
        s["before_back"] = (2.0 * s["rectified"] * active_back).astype(BF16)
    up_sum = share_out(
        after(over_micro("second_rows", "before_back"), down_sum).reshape(dp_size, -1, units_local)
    )

    gain_two_sum = 0.0
    bias_two_sum = 0.0
    width_router_sum = 0.0
    for s in state:
        second_part = contract_cols(s["before_back"], up_weight)
        second_back = scatter_rows(second_part.astype(BF16), size)
        width_logit_back = (
            NB
            * s["picked_width"][:, None]
            * (s["bucket_hot"] - s["width_share"])
            * s["width_gate_back"][:, None]
        )
        width_router_sum = width_router_sum + jnp.dot(
            width_logit_back.T, s["second_low"].astype(F32), precision=HIGHEST
        )
        second_back = second_back + jnp.dot(width_logit_back, router_width.T, precision=HIGHEST)
        gain_two_sum = gain_two_sum + jnp.sum(second_back * s["second_normed"], axis=0)
        bias_two_sum = bias_two_sum + jnp.sum(second_back, axis=0)
        s["hidden_back"] = s["outer"] + norm_back(
            second_back, s["second_normed"], s["second_inverse"], gain_two
        )
        gate_back = jnp.sum(s["hidden_back"] * s["attention_own"], axis=1)
        seq_gate_part = jnp.sum(s["own_seq"] * gate_back[:, None], axis=0)
        s["seq_gate_back"] = butterfly(seq_gate_part, "tensor", size)
        attention_back = (s["own_gate"][:, None] * s["hidden_back"]).astype(BF16)
        s["attention_rows_back"] = gather_rows(attention_back, size)

    out_sum = share_out(after(columns_first(over_micro("head_rows", "attention_rows_back")), up_sum))

    for s in state:
        rows_back = s["attention_rows_back"].reshape(total, dp_size, -1)
        heads_back = lax.dot_general(
            rows_back, out_weight, (((1, 2), (0, 2)), ((), ())), preferred_element_type=F32
        )
        heads_back = (
            heads_back.reshape(total, heads_local, HD) * s["head_on"][:, :, None]
        ).astype(BF16)
        query_back, keys_back, values_back = attend_backward(
            s["query"], s["keys"], s["values"], s["member"], slots, s["log_total"], heads_back
        )
        mixed_back = jnp.stack(
            [
                rotate_back(query_back, s["cosine"], s["sine"]),
                rotate_back(keys_back, s["cosine"], s["sine"]),
                values_back,
            ],
            axis=2,
        )
        s["mixed_back"] = mixed_back.reshape(total, 3 * heads_local * HD).astype(BF16)

    mix_sum = share_out(
        after(over_micro("first_rows", "mixed_back"), out_sum).reshape(dp_size, -1, mixer.shape[1])
    )

    input_backs = []
    gain_one_sum = 0.0
    bias_one_sum = 0.0
    head_router_sum = 0.0
    width_use = 0.0
    head_use = 0.0
    for s in state:
        first_part = contract_cols(s["mixed_back"], mix_weight)
        first_back = scatter_rows(first_part.astype(BF16), size)
        head_logit_back = (
            NHC
            * s["picked_head"][:, None]
            * (s["choice_hot"] - s["head_share"])
            * s["seq_gate_back"][:, None]
        )
        own_spread = jnp.dot(
            s["own_seq"], head_logit_back / s["divisor"][:, None], precision=HIGHEST
        )
        first_back = first_back + jnp.dot(own_spread, router_head.T, precision=HIGHEST)
        head_router_sum = head_router_sum + jnp.dot(
            own_spread.T, s["first_low"].astype(F32), precision=HIGHEST
        )
        gain_one_sum = gain_one_sum + jnp.sum(first_back * s["first_normed"], axis=0)
        bias_one_sum = bias_one_sum + jnp.sum(first_back, axis=0)
        input_backs.append(
            s["hidden_back"] + norm_back(first_back, s["first_normed"], s["first_inverse"], gain_one)
        )
        width_use = width_use + jnp.sum(s["bucket_hot"] * s["own_live"][:, None], axis=0)
        head_use = head_use + jnp.sum(
            s["own_seq"][:, :, None] * s["choice_hot"][None, :, :], axis=(0, 1)
        )

    use_row = jnp.zeros((1, width), F32)
    use_row = use_row.at[0, :NB].set(width_use).at[0, NB : NB + NHC].set(head_use)
    stats = jnp.concatenate(
        [
            gain_one_sum[None],
            bias_one_sum[None],
            gain_two_sum[None],
            bias_two_sum[None],
            width_router_sum,
            head_router_sum,
            use_row,
        ],
        axis=0,
    )
    stats = butterfly(butterfly(stats, "tensor", size), "dp", dp_size)
    return (
        jnp.stack(outputs, axis=0),
        jnp.stack(input_backs, axis=0),
        mix_sum,
        out_sum,
        up_sum,
        down_sum,
        stats[0],
        stats[1],
        stats[2],
        stats[3],
        stats[4 : 4 + NB].T,
        stats[4 + NB : 4 + NB + NHC].T,
        stats[4 + NB + NHC, :NB],
        stats[4 + NB + NHC, NB : NB + NHC],
    )


def solution(mesh):
    def run(*args):
        return local(mesh.shape["dp"], mesh.shape["tensor"], *args)

    rows = P(None, ("dp", "tensor"), None)
    tall, wide = P("dp", "tensor"), P("tensor", "dp")
    weights = (tall, wide, tall, wide)
    return jax.shard_map(
        run,
        mesh=mesh,
        in_specs=(rows, rows) + weights + (P(),) * 6 + (P(None, "dp"),) * 3,
        out_specs=(rows, rows) + weights + (P(),) * 8,
        check_vma=False,
    )
```

```python
import functools
import types

import jax
import jax.numpy as jnp
from jax import lax
from jax.experimental import pallas as pl
from jax.experimental.pallas import tpu as pltpu
from jax.sharding import PartitionSpec as P

H = 16
HD = 128
FF = 8192
NB = 4
NHC = 4

EPSILON = 1e-05
HIGHEST = lax.Precision.HIGHEST
MASKED = -1e30
BF16 = jnp.bfloat16
F32 = jnp.float32
MESH = pl.DeviceIdType.MESH
MIB = 1024 * 1024
LANES = 128
STEP = 16

GATE = 4
LIVE = 5
SEQ = 8


def dot(left, right):
    return jnp.dot(left, right, preferred_element_type=F32)


def dot_nt(left, right):
    return lax.dot_general(left, right, (((1,), (1,)), ((), ())), preferred_element_type=F32)


def dot_tn(left, right):
    return lax.dot_general(left, right, (((0,), (0,)), ((), ())), preferred_element_type=F32)


def at(start, size=STEP):
    return pl.ds(pl.multiple_of(start, STEP), size)


class Links:
    def __init__(self, size, rows, send_sems, recv_sems):
        me = lax.axis_index("tensor")
        hi, lo = me // 2, me % 2
        self.me, self.size, self.high, self.half = me, size, size // 2, rows // 2
        self.near = hi * 2 + (1 - lo)
        self.ahead = [lax.rem(hi + s, self.high) * 2 + lo for s in range(self.high)]
        self.behind = [
            lax.rem(hi + self.high - s, self.high) * 2 + lo for s in range(self.high)
        ]
        self.send_sems, self.recv_sems, self.used = send_sems, recv_sems, 0
        self.second = self.half * size

    def greet(self, others=()):
        barrier = pltpu.get_barrier_semaphore()
        peers = [self.near] + self.ahead[1:] + list(others)
        for peer in peers:
            pl.semaphore_signal(
                barrier, inc=1, device_id={"tensor": peer}, device_id_type=MESH
            )
        pl.semaphore_wait(barrier, len(peers))

    def copy(self, src, dst, to):
        made = pltpu.make_async_remote_copy(
            src_ref=src,
            dst_ref=dst,
            send_sem=self.send_sems.at[self.used],
            recv_sem=self.recv_sems.at[self.used],
            device_id={"tensor": to},
            device_id_type=MESH,
        )
        self.used += 1
        made.start()
        return made


def transfers(size):
    return 2 * (size // 2)


class Gather:
    def __init__(self, links, buf, base):
        self.links, self.buf, self.base = links, buf, base

    def rows(self, start, count):
        return self.buf.at[pl.ds(self.base + start, count)]

    def start(self):
        k, half, second = self.links, self.links.half, self.links.second
        self.first_near = k.copy(self.rows(0, half), self.rows(half, half), k.near)
        self.second_far = [
            k.copy(self.rows(second, half), self.rows(second + s * half, half), k.behind[s])
            for s in range(1, k.high)
        ]

    def middle(self):
        k, half, second = self.links, self.links.half, self.links.second
        self.first_near.wait_recv()
        self.first_far = [
            k.copy(self.rows(0, 2 * half), self.rows(2 * half * s, 2 * half), k.behind[s])
            for s in range(1, k.high)
        ]
        for made in self.second_far:
            made.wait_recv()
        block = k.high * half
        self.second_near = k.copy(self.rows(second, block), self.rows(second + block, block), k.near)

    def finish(self):
        for made in self.first_far + [self.second_near]:
            made.wait_recv()
        for made in [self.first_near, self.second_near] + self.first_far + self.second_far:
            made.wait_send()


class Scatter:
    def __init__(self, links, part, base, landing, staged, last, total):
        self.links, self.part, self.base = links, part, base
        self.landing, self.staged, self.last, self.total = landing, staged, last, total

    def start(self):
        k, half = self.links, self.links.half
        block = k.high * half
        self.first_far = [
            k.copy(
                self.part.at[pl.ds(self.base + 2 * half * s, 2 * half)],
                self.landing.at[pl.ds(2 * half * (s - 1), 2 * half)],
                k.ahead[s],
            )
            for s in range(1, k.high)
        ]
        self.second_near = k.copy(
            self.part.at[pl.ds(self.base + k.second + block, block)],
            self.landing.at[pl.ds(2 * half * (k.high - 1), block)],
            k.near,
        )

    def middle(self):
        k, half, base = self.links, self.links.half, self.base
        steps = half // STEP
        for made in self.first_far:
            made.wait_recv()

        def first(i, _):
            for where in range(2):
                row = where * half + i * STEP
                value = self.part[at(base + row), :].astype(F32)
                for s in range(1, k.high):
                    value = value + self.landing[at(2 * half * (s - 1) + row), :].astype(F32)
                if where == 0:
                    self.total[at(i * STEP), :] = value
                else:
                    self.staged[at(i * STEP), :] = value.astype(BF16)
            return 0

        lax.fori_loop(0, steps, first, 0)
        self.first_near = k.copy(
            self.staged.at[pl.ds(0, half)], self.last.at[pl.ds(0, half)], k.near
        )
        self.second_near.wait_recv()
        landed = 2 * half * (k.high - 1)

        def second(i, _):
            for s in range(k.high):
                row = s * half + i * STEP
                value = self.part[at(base + k.second + row), :].astype(F32)
                value = value + self.landing[at(landed + row), :].astype(F32)
                if s == 0:
                    self.total[at(half + i * STEP), :] = value
                else:
                    self.staged[at(row), :] = value.astype(BF16)
            return 0

        lax.fori_loop(0, steps, second, 0)
        self.second_far = [
            k.copy(
                self.staged.at[pl.ds(half * s, half)], self.last.at[pl.ds(half * s, half)], k.ahead[s]
            )
            for s in range(1, k.high)
        ]
        for made in self.first_far + [self.second_near]:
            made.wait_send()

    def finish(self):
        for made in [self.first_near] + self.second_far:
            made.wait_recv()
            made.wait_send()

    def chunk(self, where, i):
        k, half = self.links, self.links.half
        value = self.total[at(where * half + i * STEP), :]
        if where == 0:
            return value + self.last[at(i * STEP), :].astype(F32)
        for s in range(1, k.high):
            value = value + self.last[at(half * s + i * STEP), :].astype(F32)
        return value


def over_rows(half, body):
    for where in range(2):

        def inner(i, _, where=where):
            body(where, i, where * half + i * STEP)
            return 0

        lax.fori_loop(0, half // STEP, inner, 0)


class Loads:
    def __init__(self, sems):
        self.sems, self.used = sems, 0

    def copy(self, src, dst):
        made = pltpu.make_async_copy(src, dst, self.sems.at[self.used])
        self.used += 1
        made.start()
        return made


def wait_all(*groups):
    for group in groups:
        for made in group if isinstance(group, list) else [group]:
            made.wait()


def columns_in(loads, blocks, flat):
    count, _, width = blocks.shape
    return [loads.copy(blocks.at[j], flat.at[:, pl.ds(j * width, width)]) for j in range(count)]


def tiles_out(count, make, tile, sems, target):
    def one(c, slot, wait):
        copy = pltpu.make_async_copy(tile.at[slot], target(c), sems.at[slot])
        if wait is not None:

            @pl.when(wait)
            def _():
                copy.wait()

        make(c, tile.at[slot])
        copy.start()

    if count == 1:
        one(0, 0, None)
    else:

        def pair(i, _):
            one(2 * i, 0, i > 0)
            one(2 * i + 1, 1, i > 0)
            return 0

        lax.fori_loop(0, count // 2, pair, 0)
    for slot in range(min(count, 2)):
        pltpu.make_async_copy(tile.at[slot], target(slot), sems.at[slot]).wait()


def normalized(value):
    centred = value - jnp.mean(value, axis=-1, keepdims=True)
    inverse = lax.rsqrt(jnp.mean(centred * centred, axis=-1, keepdims=True) + EPSILON)
    return centred * inverse, inverse


def norm_back(back, normed, inverse, gain):
    scaled = back * gain
    inner = jnp.mean(scaled, axis=-1, keepdims=True)
    along = jnp.mean(scaled * normed, axis=-1, keepdims=True)
    return inverse * (scaled - inner - normed * along)


def turned(value, cosine, sine):
    return value * cosine + pltpu.roll(value, HD // 2, 1) * sine


def first_norm_kernel(size, tokens, gain, bias, rows_out, buf, send, recv, out_sems):
    micro, rows, _ = tokens.shape
    links = Links(size, rows, send, recv)
    total = rows * size
    links.greet()
    gathers, loads = [], Loads(out_sems)
    for m in range(micro):

        def body(where, i, row, m=m):
            value = tokens[m, at(row), :].astype(F32)
            low = (normalized(value)[0] * gain[...] + bias[...]).astype(BF16)
            buf[at(m * total + where * links.second + i * STEP), :] = low

        over_rows(links.half, body)
        gathers.append(Gather(links, buf, m * total))
        gathers[m].start()
    for g in gathers:
        g.middle()
    outs = []
    for m, g in enumerate(gathers):
        g.finish()
        here = pl.ds(m * total, total)
        outs.append(loads.copy(buf.at[here], rows_out.at[here]))
    wait_all(outs)


def attend_kernel(
    size,
    heads,
    rows_hbm,
    mix_hbm,
    out_hbm,
    mask_hbm,
    cosine,
    sine,
    row_info,
    own,
    tokens,
    cotangent,
    gain,
    bias,
    router,
    qkv_out,
    heads_out,
    attention_out,
    second_out,
    share_out,
    branch_out,
    rows_buf,
    mix,
    out,
    mask,
    qkv,
    head_rows,
    part,
    landing,
    staged,
    last,
    second_buf,
    send,
    recv,
    load_sems,
):
    micro, rows, width = tokens.shape
    total = rows * size
    links = Links(size, rows, send, recv)
    half = links.half
    loads = Loads(load_sems)
    mix_copy = loads.copy(mix_hbm, mix)
    row_copies = [
        loads.copy(rows_hbm.at[pl.ds(m * total, total)], rows_buf.at[pl.ds(m * total, total)])
        for m in range(micro)
    ]
    mask_copy = loads.copy(mask_hbm, mask)
    out_copies = columns_in(loads, out_hbm, out)
    links.greet()
    mix_copy.wait()
    scale = HD ** (-0.5)
    span = 3 * HD
    chunk = min(128, total)
    tile = min(512, width)
    saves = []

    def project(m):
        base = m * total
        cos, sin = cosine[m], sine[m]

        def head(h, _):
            mixed = dot(
                rows_buf[pl.ds(base, total), :], mix[:, pl.ds(pl.multiple_of(h * span, HD), span)]
            )
            here = pl.ds(pl.multiple_of(h * HD, HD), HD)
            qkv[m, 0, :, here] = turned(mixed[:, :HD], cos, sin).astype(BF16)
            qkv[m, 1, :, here] = turned(mixed[:, HD : 2 * HD], cos, sin).astype(BF16)
            qkv[m, 2, :, here] = mixed[:, 2 * HD :].astype(BF16)
            return 0

        lax.fori_loop(0, heads, head, 0)

    def attend(m):
        base = m * total

        def some(c, _):
            rows_here = pl.ds(pl.multiple_of(c * chunk, chunk), chunk)
            bias_here = mask[m, rows_here, :]
            info = row_info[m, rows_here, :]
            for h in range(heads):
                here = pl.ds(h * HD, HD)
                scores = dot_nt(qkv[m, 0, rows_here, here], qkv[m, 1, :, here]) * scale + bias_here
                peak = jnp.max(scores, axis=-1, keepdims=True)
                powers = jnp.exp(scores - peak)
                share = powers / jnp.sum(powers, axis=-1, keepdims=True)
                value = dot(share.astype(BF16), qkv[m, 2, :, here]).astype(BF16)
                value = value.astype(F32) * info[:, h : h + 1]
                head_rows[pl.ds(pl.multiple_of(base + c * chunk, chunk), chunk), here] = value.astype(
                    BF16
                )
            return 0

        lax.fori_loop(0, total // chunk, some, 0)

    def merge(m):
        base = m * total

        def body(j, _):
            here = pl.ds(pl.multiple_of(j * tile, tile), tile)
            part[pl.ds(base, total), here] = dot(
                head_rows[pl.ds(base, total), :], out[:, here]
            ).astype(BF16)
            return 0

        lax.fori_loop(0, width // tile, body, 0)

    scatters = [
        Scatter(
            links,
            part,
            m * total,
            landing.at[m],
            staged.at[m],
            last.at[m],
            attention_out.at[m],
        )
        for m in range(micro)
    ]
    gathers = [Gather(links, second_buf, m * total) for m in range(micro)]

    def second_norm(m):
        scatter = scatters[m]

        def body(where, i, row):
            attended = scatter.chunk(where, i)
            info = own[m, at(row), :]
            hidden = tokens[m, at(row), :].astype(F32) + info[:, GATE : GATE + 1] * attended
            attention_out[m, at(row), :] = attended
            low = (normalized(hidden)[0] * gain[...] + bias[...]).astype(BF16)
            second_buf[at(m * total + where * links.second + i * STEP), :] = low
            logits = dot(low, router[...])
            lane = lax.broadcasted_iota(jnp.int32, logits.shape, 1)
            logits = jnp.where(lane < NB, logits, MASKED)
            powers = jnp.exp(logits - jnp.max(logits, axis=-1, keepdims=True))
            share = powers / jnp.sum(powers, axis=-1, keepdims=True)
            share = jnp.where(lane < NB, share, 0.0)
            share_out[m, at(row), :] = share
            gate = NB * jnp.sum(share * info, axis=-1, keepdims=True)
            outer = cotangent[m, at(row), :].astype(F32) * info[:, LIVE : LIVE + 1]
            branch_out[m, at(row), :] = (gate * outer).astype(BF16)

        over_rows(half, body)

    for m in range(micro):
        row_copies[m].wait()
        project(m)
        if m > 0:
            scatters[m - 1].middle()
        if m == 0:
            mask_copy.wait()
        attend(m)
        if m == 0:
            wait_all(out_copies)
        merge(m)
        scatters[m].start()
    for m in range(micro):
        if m == micro - 1:
            scatters[m].middle()
        scatters[m].finish()
        second_norm(m)
        gathers[m].start()
        if m > 0:
            gathers[m - 1].middle()
    saves.append(loads.copy(qkv, qkv_out))
    saves.append(loads.copy(head_rows, heads_out))
    gathers[micro - 1].middle()
    for m in range(micro):
        gathers[m].finish()
        here = pl.ds(m * total, total)
        saves.append(loads.copy(second_buf.at[here], second_out.at[here]))
    wait_all(saves)


def widen_kernel(
    size,
    unit_lane,
    second_hbm,
    up_hbm,
    branch,
    row_info,
    rect_out,
    active_out,
    branch_out,
    down_out,
    second_rows,
    up,
    branch_buf,
    rect,
    active,
    tile,
    send,
    recv,
    load_sems,
    tile_sems,
):
    micro, rows, width = branch.shape
    total = rows * size
    units = up.shape[1]
    links = Links(size, rows, send, recv)
    loads = Loads(load_sems)
    up_copy = loads.copy(up_hbm, up)
    second_copies = [
        loads.copy(second_hbm.at[pl.ds(m * total, total)], second_rows.at[pl.ds(m * total, total)])
        for m in range(micro)
    ]
    half = links.half
    own_copies = []
    for m in range(micro):
        for where in range(2):
            own_copies.append(
                loads.copy(
                    branch.at[m, pl.ds(where * half, half)],
                    branch_buf.at[pl.ds(m * total + where * links.second, half)],
                )
            )
    links.greet()
    wait_all(own_copies)
    gathers = [Gather(links, branch_buf, m * total) for m in range(micro)]
    for g in gathers:
        g.start()
    up_copy.wait()
    step = min(512, units)
    saves = []
    for m in range(micro):
        second_copies[m].wait()

        def body(j, _, m=m):
            here = pl.ds(pl.multiple_of(j * step, step), step)
            before = dot(second_rows[pl.ds(m * total, total), :], up[:, here])
            kept = jnp.maximum(before, 0.0) * row_info[m, :, unit_lane : unit_lane + 1]
            rect[pl.ds(m * total, total), here] = kept.astype(BF16)
            active[pl.ds(m * total, total), here] = (kept * kept).astype(BF16)
            return 0

        lax.fori_loop(0, units // step, body, 0)
        gathers[m].middle()
        here = pl.ds(m * total, total)
        saves.append(loads.copy(rect.at[here], rect_out.at[here]))
        saves.append(loads.copy(active.at[here], active_out.at[here]))
    for m, g in enumerate(gathers):
        g.finish()
        here = pl.ds(m * total, total)
        saves.append(loads.copy(branch_buf.at[here], branch_out.at[here]))
    count, _, block = down_out.shape
    wide = tile.shape[2]

    def make(c, slot):
        value = dot_tn(active[:, pl.ds(pl.multiple_of(c * wide, wide), wide)], branch_buf[...])
        for j in range(count):
            slot[j] = value[:, j * block : (j + 1) * block].astype(BF16)

    tiles_out(
        units // wide,
        make,
        tile,
        tile_sems,
        lambda c: down_out.at[:, pl.ds(pl.multiple_of(c * wide, wide), wide), :],
    )
    wait_all(saves)


def narrow_kernel(
    size,
    down_hbm,
    up_hbm,
    active_hbm,
    rect_hbm,
    branch_hbm,
    second_hbm,
    tokens,
    cotangent,
    attention,
    share,
    own,
    gain,
    router,
    block_out,
    up_out,
    hidden_out,
    back_out,
    stats_out,
    gate_out,
    down,
    up,
    active,
    rect,
    shared_rows,
    part,
    landing,
    staged,
    last,
    total_rows,
    gate_back,
    tile,
    send,
    recv,
    load_sems,
    tile_sems,
):
    micro, rows, width = tokens.shape
    total = rows * size
    units = up.shape[1]
    links = Links(size, rows, send, recv)
    half = links.half
    loads = Loads(load_sems)
    here = [pl.ds(m * total, total) for m in range(micro)]
    down_copies = columns_in(loads, down_hbm, down)
    active_copies = [loads.copy(active_hbm.at[h], active.at[h]) for h in here]
    branch_copies = [loads.copy(branch_hbm.at[h], shared_rows.at[h]) for h in here]
    rect_copies = [loads.copy(rect_hbm.at[h], rect.at[h]) for h in here]
    up_copy = loads.copy(up_hbm, up)
    stats_out[...] = jnp.zeros_like(stats_out)
    gate_out[...] = jnp.zeros_like(gate_out)
    links.greet()
    step = min(512, units)
    tile_cols = min(512, width)
    outs = [
        Scatter(
            links, part, m * total, landing.at[m], staged.at[m], last.at[m], total_rows.at[m]
        )
        for m in range(micro)
    ]
    backs = [
        Scatter(
            links,
            part,
            m * total,
            landing.at[micro + m],
            staged.at[micro + m],
            last.at[micro + m],
            hidden_out.at[m],
        )
        for m in range(micro)
    ]
    wait_all(down_copies)
    for m in range(micro):
        active_copies[m].wait()

        def body(j, _, m=m):
            cols = pl.ds(pl.multiple_of(j * tile_cols, tile_cols), tile_cols)
            part[here[m], cols] = dot(active[here[m], :], down[:, cols]).astype(BF16)
            return 0

        lax.fori_loop(0, width // tile_cols, body, 0)
        outs[m].start()
    for m in range(micro):
        branch_copies[m].wait()
        rect_copies[m].wait()

        def body(j, _, m=m):
            cols = pl.ds(pl.multiple_of(j * step, step), step)
            back = dot_nt(shared_rows[here[m], :], down[cols, :])
            active[here[m], cols] = (2.0 * rect[here[m], cols].astype(F32) * back).astype(BF16)
            return 0

        lax.fori_loop(0, units // step, body, 0)
        if m == 0:
            up_copy.wait()
    second_copies = [loads.copy(second_hbm.at[h], shared_rows.at[h]) for h in here]
    for m in range(micro):
        outs[m].middle()

        def body(j, _, m=m):
            cols = pl.ds(pl.multiple_of(j * tile_cols, tile_cols), tile_cols)
            part[here[m], cols] = dot_nt(active[here[m], :], up[cols, :]).astype(BF16)
            return 0

        lax.fori_loop(0, width // tile_cols, body, 0)
        backs[m].start()

    def finish_out(m):
        outs[m].finish()

        def body(where, i, row):
            branch = outs[m].chunk(where, i)
            info = own[m, at(row), :]
            live = info[:, LIVE : LIVE + 1]
            outer = cotangent[m, at(row), :].astype(F32) * live
            hidden = tokens[m, at(row), :].astype(F32)
            hidden = hidden + info[:, GATE : GATE + 1] * attention[m, at(row), :]
            gate = NB * jnp.sum(share[m, at(row), :] * info, axis=-1, keepdims=True)
            block_out[m, at(row), :] = (live * (hidden + gate * branch)).astype(BF16)
            value = jnp.sum(outer * branch, axis=-1, keepdims=True)
            gate_back[m, at(row), :] = jnp.broadcast_to(value, (STEP, LANES))

        over_rows(half, body)

    def finish_back(m):
        backs[m].finish()

        def body(where, i, row):
            back = backs[m].chunk(where, i)
            info = own[m, at(row), :]
            portions = share[m, at(row), :]
            live = info[:, LIVE : LIVE + 1]
            outer = cotangent[m, at(row), :].astype(F32) * live
            hidden = tokens[m, at(row), :].astype(F32)
            attended = attention[m, at(row), :]
            hidden = hidden + info[:, GATE : GATE + 1] * attended
            normed, inverse = normalized(hidden)
            low = (normed * gain[0:1, :] + gain[1:2, :]).astype(BF16).astype(F32)
            picked = jnp.sum(portions * info, axis=-1, keepdims=True)
            logit_back = NB * picked * (info - portions) * gate_back[m, at(row), :]
            for b in range(NB):
                column = logit_back[:, b : b + 1]
                back = back + column * router[b : b + 1, :]
                stats_out[2 + b : 3 + b, :] += jnp.sum(column * low, axis=0, keepdims=True)
            stats_out[0:1, :] += jnp.sum(back * normed, axis=0, keepdims=True)
            stats_out[1:2, :] += jnp.sum(back, axis=0, keepdims=True)
            hidden_back = outer + norm_back(back, normed, inverse, gain[0:1, :])
            hidden_out[m, at(row), :] = hidden_back
            back_out[m, at(row), :] = (info[:, GATE : GATE + 1] * hidden_back).astype(BF16)
            gate_part = jnp.sum(hidden_back * attended, axis=-1, keepdims=True)
            gate_out[m : m + 1, :] += jnp.sum(info * gate_part, axis=0, keepdims=True)

        over_rows(half, body)

    for m in range(micro):
        finish_out(m)
    wait_all(second_copies)
    block = up_out.shape[1]

    def make(c, slot):
        slot[...] = dot_tn(
            shared_rows[:, pl.ds(pl.multiple_of(c * block, block), block)], active[...]
        ).astype(BF16)

    tiles_out(up_out.shape[0], make, tile, tile_sems, lambda c: up_out.at[c])
    for m in range(micro):
        backs[m].middle()
    for m in range(micro):
        finish_back(m)


def attend_back_kernel(
    size,
    heads,
    _before,
    back,
    gate,
    out_hbm,
    qkv_hbm,
    heads_hbm,
    rows_hbm,
    mask_hbm,
    cosine,
    sine,
    row_info,
    mixed_out,
    out_term,
    mix_term,
    gate_out,
    buf,
    out,
    qkv,
    head_rows,
    rows_buf,
    mask,
    heads_back,
    mixed_back,
    score_back,
    shares,
    out_tile,
    mix_tile,
    gates,
    send,
    recv,
    load_sems,
    out_sems,
    mix_sems,
):
    micro, rows, width = back.shape
    total = rows * size
    links = Links(size, rows, send, recv)
    half = links.half
    loads = Loads(load_sems)
    own_copies = []
    for m in range(micro):
        for where in range(2):
            own_copies.append(
                loads.copy(
                    back.at[m, pl.ds(where * half, half)],
                    buf.at[pl.ds(m * total + where * links.second, half)],
                )
            )
    out_copies = columns_in(loads, out_hbm, out)
    qkv_copy = loads.copy(qkv_hbm, qkv)
    mask_copy = loads.copy(mask_hbm, mask)
    heads_copy = loads.copy(heads_hbm, head_rows)
    rows_copy = loads.copy(rows_hbm, rows_buf)
    gates[links.me] = gate[...]
    others = [lax.rem(links.me + s, size) for s in range(1, size)]
    barrier = pltpu.get_barrier_semaphore()
    for peer in others:
        pl.semaphore_signal(barrier, inc=1, device_id={"tensor": peer}, device_id_type=MESH)
    pl.semaphore_wait(barrier, size - 1)
    wait_all(own_copies)
    gathers = [Gather(links, buf, m * total) for m in range(micro)]
    for g in gathers:
        g.start()
    gate_copies = [links.copy(gate, gates.at[links.me], peer) for peer in others]
    wait_all(out_copies)
    qkv_copy.wait()
    mask_copy.wait()
    scale = HD ** (-0.5)
    chunk = min(128, total)
    for g in gathers:
        g.middle()
    for m in range(micro):
        gathers[m].finish()
        base = m * total
        every = pl.ds(base, total)
        value = dot_nt(buf[every, :], out[...])
        for h in range(heads):
            here = pl.ds(h * HD, HD)
            heads_back[:, here] = (
                value[:, h * HD : (h + 1) * HD] * row_info[m, :, h : h + 1]
            ).astype(BF16)
        for h in range(heads):
            here = pl.ds(h * HD, HD)

            def some(c, _, m=m, here=here):
                rows_here = pl.ds(pl.multiple_of(c * chunk, chunk), chunk)
                scores = dot_nt(qkv[m, 0, rows_here, here], qkv[m, 1, :, here]) * scale
                scores = scores + mask[m, rows_here, :]
                powers = jnp.exp(scores - jnp.max(scores, axis=-1, keepdims=True))
                share = powers / jnp.sum(powers, axis=-1, keepdims=True)
                share_back = dot_nt(heads_back[rows_here, here], qkv[m, 2, :, here])
                inner = jnp.sum(share * share_back, axis=-1, keepdims=True)
                score_back[rows_here, :] = (share * (share_back - inner)).astype(BF16)
                shares[rows_here, :] = share.astype(BF16)
                return 0

            lax.fori_loop(0, total // chunk, some, 0)
            cos, sin = cosine[m], -sine[m]
            query_back = dot(score_back[...], qkv[m, 1, :, here]) * scale
            keys_back = dot_tn(score_back[...], qkv[m, 0, :, here]) * scale
            values_back = dot_tn(shares[...], heads_back[:, here])
            col = 3 * h * HD
            mixed_back[every, pl.ds(col, HD)] = turned(query_back, cos, sin).astype(BF16)
            mixed_back[every, pl.ds(col + HD, HD)] = turned(keys_back, cos, sin).astype(BF16)
            mixed_back[every, pl.ds(col + 2 * HD, HD)] = values_back.astype(BF16)
    mixed_save = loads.copy(mixed_back, mixed_out)
    heads_copy.wait()
    count, depth, block = out_term.shape
    wide = out_tile.shape[2]

    def make_out(c, slot):
        value = dot_tn(head_rows[:, pl.ds(pl.multiple_of(c * wide, wide), wide)], buf[...])
        for j in range(count):
            slot[j] = value[:, j * block : (j + 1) * block].astype(BF16)

    tiles_out(
        depth // wide,
        make_out,
        out_tile,
        out_sems,
        lambda c: out_term.at[:, pl.ds(pl.multiple_of(c * wide, wide), wide), :],
    )
    rows_copy.wait()

    def make_mix(c, slot):
        slot[...] = dot_tn(
            rows_buf[:, pl.ds(pl.multiple_of(c * block, block), block)], mixed_back[...]
        ).astype(BF16)

    tiles_out(count, make_mix, mix_tile, mix_sems, lambda c: mix_term.at[c])
    for made in gate_copies:
        made.wait()
    gate_sum = gates[0]
    for r in range(1, size):
        gate_sum = gate_sum + gates[r]
    gate_out[...] = gate_sum
    mixed_save.wait()


def first_back_kernel(
    size,
    micro,
    _before,
    mixed_hbm,
    mix_hbm,
    back_out,
    mixed_back,
    mix,
    part,
    landing,
    staged,
    last,
    send,
    recv,
    load_sems,
):
    total = mixed_back.shape[0] // micro
    rows = total // size
    width = mix.shape[0]
    links = Links(size, rows, send, recv)
    loads = Loads(load_sems)
    here = [pl.ds(m * total, total) for m in range(micro)]
    mix_copy = loads.copy(mix_hbm, mix)
    mixed_copies = [loads.copy(mixed_hbm.at[h], mixed_back.at[h]) for h in here]
    links.greet()
    scatters = [
        Scatter(links, part, m * total, landing.at[m], staged.at[m], last.at[m], back_out.at[m])
        for m in range(micro)
    ]
    mix_copy.wait()
    tile = min(512, width)
    for m in range(micro):
        mixed_copies[m].wait()

        def body(j, _, m=m):
            cols = pl.ds(pl.multiple_of(j * tile, tile), tile)
            part[here[m], cols] = dot_nt(mixed_back[here[m], :], mix[cols, :]).astype(BF16)
            return 0

        lax.fori_loop(0, width // tile, body, 0)
        scatters[m].start()
    for s in scatters:
        s.middle()
    for m, s in enumerate(scatters):
        s.finish()

        def body(where, i, row, m=m, s=s):
            back_out[m, at(row), :] = s.chunk(where, i)

        over_rows(links.half, body)


def butterfly(value, axis, size):
    step = 1
    while step < size:
        value = value + lax.ppermute(value, axis, [(i, i ^ step) for i in range(size)])
        step *= 2
    return value


def norm_rows(value):
    centred = value - jnp.mean(value, axis=-1, keepdims=True)
    inverse = lax.rsqrt(jnp.mean(centred * centred, axis=-1, keepdims=True) + EPSILON)
    return centred * inverse, inverse


def rotary_tables(place):
    half = HD // 2
    rates = jnp.power(10000.0, -2.0 * jnp.arange(half, dtype=F32) / HD)
    angles = place.astype(F32)[:, None] * rates[None, :]
    cosine, sine = jnp.cos(angles), jnp.sin(angles)
    return jnp.concatenate([cosine, cosine], axis=1), jnp.concatenate([-sine, sine], axis=1)


def softmax_rows(logits):
    powers = jnp.exp(logits - jnp.max(logits, axis=-1, keepdims=True))
    return powers / jnp.sum(powers, axis=-1, keepdims=True)


def place_rows(lengths, slots):
    slot_count = lengths.shape[0]
    ends = jnp.cumsum(lengths, dtype=jnp.int32)
    starts = ends - lengths
    filled = ends[-1]
    member = jnp.sum((ends[None, :] <= slots[:, None]).astype(jnp.int32), axis=1, dtype=jnp.int32)
    begins = jnp.concatenate([starts, filled[None]])
    onehot = member[:, None] == jnp.arange(slot_count + 1, dtype=jnp.int32)[None, :]
    place = slots - jnp.sum(jnp.where(onehot, begins[None, :], 0), axis=1, dtype=jnp.int32)
    return member, place, slots < filled, onehot[:, :slot_count]


def gather_weights(piece):
    return lax.all_gather(piece, "dp", axis=0, tiled=False)


def share_out(term):
    return lax.psum_scatter(term, "dp", scatter_dimension=0, tiled=False)


ANY = pl.BlockSpec(memory_space=pl.ANY)
VMEM = pl.BlockSpec(memory_space=pltpu.VMEM)


def call(kernel, ident, ins, outs, scratch, copies, loads, extra=(), flops=0, limit=56):
    dma = pltpu.SemaphoreType.DMA
    sems = [dma((copies,)), dma((copies,)), dma((loads,))] + [dma((n,)) for n in extra]
    moved = sum(a.size * a.dtype.itemsize for a, _ in ins)
    return pl.pallas_call(
        kernel,
        out_shape=[jax.ShapeDtypeStruct(shape, kind) for shape, kind, _ in outs],
        in_specs=[VMEM if near else ANY for _, near in ins],
        out_specs=[VMEM if near else ANY for _, _, near in outs],
        scratch_shapes=[pltpu.VMEM(shape, kind) for shape, kind in scratch] + sems,
        compiler_params=pltpu.CompilerParams(
            collective_id=ident, has_side_effects=True, vmem_limit_bytes=limit * MIB
        ),
        cost_estimate=pl.CostEstimate(flops=flops, bytes_accessed=moved, transcendentals=0),
    )(*[a for a, _ in ins])


def local(
    dp_size,
    size,
    tokens,
    cotangent,
    mixer,
    merger,
    expand,
    shrink,
    attend_gain,
    attend_bias,
    feed_gain,
    feed_bias,
    width_router,
    head_router,
    lengths,
    head_choice,
    width_bucket,
):
    rank = lax.axis_index("tensor")
    micro, rows, width = tokens.shape
    total = width_bucket.shape[1]
    every = micro * total
    half = rows // 2
    high = size // 2
    heads = merger.shape[0] // HD
    units = expand.shape[1]
    block = width // dp_size
    gain_one = attend_gain.astype(F32)[None]
    bias_one = attend_bias.astype(F32)[None]
    gain_two = feed_gain.astype(F32)[None]
    bias_two = feed_bias.astype(F32)[None]
    router_width = width_router.astype(F32)
    router_head = head_router.astype(F32)

    mix_weight = gather_weights(mixer).reshape(width, -1)
    out_weight = gather_weights(merger)
    up_weight = gather_weights(expand).reshape(width, -1)
    down_weight = gather_weights(shrink)

    few = transfers(size)
    first_rows = call(
        functools.partial(first_norm_kernel, size),
        1,
        [(tokens, True), (gain_one, True), (bias_one, True)],
        [((every, width), BF16, False)],
        [((every, width), BF16)],
        micro * few,
        micro,
    )[0]

    hi, lo = rank // 2, rank % 2
    first_ranks = [((hi + s) % high) * 2 + (lo + l) % 2 for s in range(high) for l in range(2)]
    second_ranks = [((hi + s) % high) * 2 + (lo + l) % 2 for l in range(2) for s in range(high)]
    starts = [r * rows for r in first_ranks] + [r * rows + half for r in second_ranks]
    slots = jnp.concatenate([start + jnp.arange(half, dtype=jnp.int32) for start in starts])
    own_slots = rank * rows + jnp.arange(rows, dtype=jnp.int32)

    def columns(parts, count):
        joined = jnp.concatenate(parts, axis=1)
        return jnp.pad(joined, ((0, 0), (0, count - joined.shape[1])))

    infos, owns, masks, cosines, sines, micros = [], [], [], [], [], []
    for m in range(micro):
        member, place, _, seqmask = place_rows(lengths[m], slots)
        _, _, own_live, own_seq = place_rows(lengths[m], own_slots)
        choices = head_choice[m]
        buckets = jnp.concatenate(
            [lax.dynamic_slice_in_dim(width_bucket[m], start, half, 0) for start in starts]
        )
        own_buckets = lax.dynamic_slice_in_dim(width_bucket[m], rank * rows, rows, 0)
        bucket_hot = (own_buckets[:, None] == jnp.arange(NB, dtype=jnp.int32)[None, :]).astype(F32)
        choice_hot = (choices[:, None] == jnp.arange(NHC, dtype=jnp.int32)[None, :]).astype(F32)
        heads_used = jnp.sum(
            jnp.where(seqmask, H // NHC * (choices[None, :] + 1), 0), axis=1, dtype=jnp.int32
        )
        head_ids = rank * heads + jnp.arange(heads, dtype=jnp.int32)
        head_on = (head_ids[None, :] < heads_used[:, None]).astype(F32)
        unit_on = (rank * units < FF // NB * (buckets[:, None] + 1)).astype(F32)
        infos.append(columns([head_on, unit_on], LANES))
        seen = (member[:, None] == member[None, :]) & (slots[:, None] >= slots[None, :])
        masks.append(jnp.where(seen, 0.0, MASKED).astype(F32))
        cosine, sine = rotary_tables(place)
        cosines.append(cosine)
        sines.append(sine)
        seq_float = seqmask.astype(F32)
        own_seq = own_seq.astype(F32)
        own_live = own_live.astype(F32)
        divisor = jnp.maximum(jnp.sum(seq_float, axis=0), 1.0)
        sums = dot(seq_float.T.astype(BF16), first_rows[m * total : (m + 1) * total])
        means = sums / divisor[:, None]
        head_share = softmax_rows(jnp.dot(means, router_head, precision=HIGHEST))
        picked_head = jnp.sum(head_share * choice_hot, axis=1)
        own_gate = jnp.sum(own_seq * (NHC * picked_head)[None, :], axis=1, keepdims=True)
        pad = jnp.zeros((rows, SEQ - LIVE - 1), F32)
        owns.append(columns([bucket_hot, own_gate, own_live[:, None], pad, own_seq], LANES))
        micros.append(
            types.SimpleNamespace(
                divisor=divisor,
                head_share=head_share,
                picked_head=picked_head,
                choice_hot=choice_hot,
                own_seq=own_seq,
                width_use=jnp.sum(bucket_hot * own_live[:, None], axis=0),
                head_use=jnp.sum(own_seq[:, :, None] * choice_hot[None, :, :], axis=(0, 1)),
            )
        )
    row_info, own, mask = jnp.stack(infos), jnp.stack(owns), jnp.stack(masks)
    cosine, sine = jnp.stack(cosines), jnp.stack(sines)
    router_lanes = jnp.pad(width_router, ((0, 0), (0, LANES - NB)))
    router_rows = jnp.pad(router_width.T, ((0, 8 - NB), (0, 0)))
    gains_two = jnp.concatenate([gain_two, bias_two, jnp.zeros((6, width), F32)], axis=0)

    lands = half * (2 * (high - 1) + high)
    stages = half * high
    wide_heads = heads * HD
    span = 3 * wide_heads
    buffers = [((micro, lands, width), BF16), ((micro, stages, width), BF16), ((micro, stages, width), BF16)]
    qkv, head_rows, attention, second_rows, width_share, branch_own = call(
        functools.partial(attend_kernel, size, heads),
        2,
        [
            (first_rows, False),
            (mix_weight, False),
            (out_weight, False),
            (mask, False),
            (cosine, True),
            (sine, True),
            (row_info, True),
            (own, True),
            (tokens, True),
            (cotangent, True),
            (gain_two, True),
            (bias_two, True),
            (router_lanes, True),
        ],
        [
            ((micro, 3, total, wide_heads), BF16, False),
            ((every, wide_heads), BF16, False),
            ((micro, rows, width), F32, True),
            ((every, width), BF16, False),
            ((micro, rows, LANES), F32, True),
            ((micro, rows, width), BF16, True),
        ],
        [
            ((every, width), BF16),
            ((width, span), BF16),
            ((wide_heads, width), BF16),
            ((micro, total, total), F32),
            ((micro, 3, total, wide_heads), BF16),
            ((every, wide_heads), BF16),
            ((every, width), BF16),
        ]
        + buffers
        + [((every, width), BF16)],
        2 * micro * few,
        2 + micro + dp_size + 2 + micro,
        flops=2 * every * width * (span + wide_heads) + 8 * heads * micro * total * total * HD,
    )

    unit_tile = 256
    rect, active, branch_rows, down_term = call(
        functools.partial(widen_kernel, size, heads),
        3,
        [(second_rows, False), (up_weight, False), (branch_own, False), (row_info, True)],
        [
            ((every, units), BF16, False),
            ((every, units), BF16, False),
            ((every, width), BF16, False),
            ((dp_size, units, block), BF16, False),
        ],
        [
            ((every, width), BF16),
            ((width, units), BF16),
            ((every, width), BF16),
            ((every, units), BF16),
            ((every, units), BF16),
            ((2, dp_size, unit_tile, block), BF16),
        ],
        micro * few,
        1 + 6 * micro,
        (2,),
        flops=4 * every * width * units,
    )
    down_sum = share_out(down_term)

    block_output, up_term, hidden_back, back_own, stats_two, gate_part = call(
        functools.partial(narrow_kernel, size),
        4,
        [
            (down_weight, False),
            (up_weight, False),
            (active, False),
            (rect, False),
            (branch_rows, False),
            (second_rows, False),
            (tokens, True),
            (cotangent, True),
            (attention, True),
            (width_share, True),
            (own, True),
            (gains_two, True),
            (router_rows, True),
        ],
        [
            ((micro, rows, width), BF16, True),
            ((dp_size, block, units), BF16, False),
            ((micro, rows, width), F32, True),
            ((micro, rows, width), BF16, True),
            ((8, width), F32, True),
            ((8, LANES), F32, True),
        ],
        [
            ((units, width), BF16),
            ((width, units), BF16),
            ((every, units), BF16),
            ((every, units), BF16),
            ((every, width), BF16),
            ((every, width), BF16),
            ((2 * micro, lands, width), BF16),
            ((2 * micro, stages, width), BF16),
            ((2 * micro, stages, width), BF16),
            ((micro, rows, width), F32),
            ((micro, rows, LANES), F32),
            ((2, block, units), BF16),
        ],
        2 * micro * few,
        dp_size + 4 * micro + 1,
        (2,),
        flops=8 * every * width * units,
        limit=62,
    )
    up_sum = share_out(up_term)

    out_tile = min(256, wide_heads)
    mixed_back, out_term, mix_term, gate_total = call(
        functools.partial(attend_back_kernel, size, heads),
        5,
        [
            (down_sum, False),
            (back_own, False),
            (gate_part, True),
            (out_weight, False),
            (qkv, False),
            (head_rows, False),
            (first_rows, False),
            (mask, False),
            (cosine, True),
            (sine, True),
            (row_info, True),
        ],
        [
            ((every, span), BF16, False),
            ((dp_size, wide_heads, block), BF16, False),
            ((dp_size, block, span), BF16, False),
            ((8, LANES), F32, True),
        ],
        [
            ((every, width), BF16),
            ((wide_heads, width), BF16),
            ((micro, 3, total, wide_heads), BF16),
            ((every, wide_heads), BF16),
            ((every, width), BF16),
            ((micro, total, total), F32),
            ((total, wide_heads), BF16),
            ((every, span), BF16),
            ((total, total), BF16),
            ((total, total), BF16),
            ((2, dp_size, out_tile, block), BF16),
            ((2, block, span), BF16),
            ((size, 8, LANES), F32),
        ],
        micro * few + size - 1,
        2 * micro + dp_size + 5,
        (2, 2),
        flops=2 * every * width * (2 * wide_heads + span) + 20 * heads * micro * total * total * HD,
    )
    out_sum = share_out(out_term)
    mix_sum = share_out(mix_term)

    first_back = call(
        functools.partial(first_back_kernel, size, micro),
        6,
        [(up_sum, False), (mixed_back, False), (mix_weight, False)],
        [((micro, rows, width), F32, True)],
        [((every, span), BF16), ((width, span), BF16), ((every, width), BF16)] + buffers,
        micro * few,
        1 + micro,
        flops=2 * every * width * span,
    )[0]

    input_backs = []
    gain_one_sum = 0.0
    bias_one_sum = 0.0
    head_router_sum = 0.0
    for m, s in enumerate(micros):
        normed, inverse = norm_rows(tokens[m].astype(F32))
        low = (normed * gain_one + bias_one).astype(BF16)
        seq_gate_back = gate_total[m, SEQ : SEQ + s.own_seq.shape[1]]
        head_logit_back = (
            NHC * s.picked_head[:, None] * (s.choice_hot - s.head_share) * seq_gate_back[:, None]
        )
        spread = jnp.dot(s.own_seq, head_logit_back / s.divisor[:, None], precision=HIGHEST)
        back = first_back[m] + jnp.dot(spread, router_head.T, precision=HIGHEST)
        head_router_sum = head_router_sum + jnp.dot(spread.T, low.astype(F32), precision=HIGHEST)
        gain_one_sum = gain_one_sum + jnp.sum(back * normed, axis=0)
        bias_one_sum = bias_one_sum + jnp.sum(back, axis=0)
        input_backs.append(hidden_back[m] + norm_back(back, normed, inverse, gain_one))

    use = jnp.concatenate([sum(s.width_use for s in micros), sum(s.head_use for s in micros)])
    use_row = jnp.pad(use[None], ((0, 0), (0, width - NB - NHC)))
    stats = jnp.concatenate(
        [stats_two[: 2 + NB], gain_one_sum[None], bias_one_sum[None], head_router_sum, use_row],
        axis=0,
    )
    stats = butterfly(butterfly(stats, "tensor", size), "dp", dp_size)
    after = 4 + NB
    return (
        block_output,
        jnp.stack(input_backs, axis=0),
        mix_sum.astype(F32),
        out_sum.astype(F32),
        up_sum.astype(F32),
        down_sum.astype(F32),
        stats[2 + NB],
        stats[3 + NB],
        stats[0],
        stats[1],
        stats[2 : 2 + NB].T,
        stats[after : after + NHC].T,
        stats[after + NHC, :NB],
        stats[after + NHC, NB : NB + NHC],
    )


def solution(mesh):
    def run(*args):
        return local(mesh.shape["dp"], mesh.shape["tensor"], *args)

    rows = P(None, ("dp", "tensor"), None)
    tall, wide = P("dp", "tensor"), P("tensor", "dp")
    weights = (tall, wide, tall, wide)
    return jax.shard_map(
        run,
        mesh=mesh,
        in_specs=(rows, rows) + weights + (P(),) * 6 + (P(None, "dp"),) * 3,
        out_specs=(rows, rows) + weights + (P(),) * 8,
        check_vma=False,
    )
```

```python
import functools

import jax
import jax.numpy as jnp
from jax import lax
from jax.experimental import pallas as pl
from jax.experimental.pallas import tpu as pltpu
from jax.sharding import PartitionSpec as P

H = 16
HD = 128
FF = 8192
NB = 4
NHC = 4

EPSILON = 1e-05
HIGHEST = lax.Precision.HIGHEST
MASKED = -1e30
BF16 = jnp.bfloat16
F32 = jnp.float32
MESH = pl.DeviceIdType.MESH
MIB = 1024 * 1024
LANES = 128
STEP = 16

GATE = 4
LIVE = 5
SEQ = 8
CHOICE = 16

PICKED = 4
DIVISOR = 5
CHOSEN = 6

ATTEND = 0
FEED = 2
WIDTH_ROUTER = 4
HEAD_ROUTER = 8


def dot(left, right):
    return jnp.dot(left, right, preferred_element_type=F32)


def dot_nt(left, right):
    return lax.dot_general(left, right, (((1,), (1,)), ((), ())), preferred_element_type=F32)


def dot_tn(left, right):
    return lax.dot_general(left, right, (((0,), (0,)), ((), ())), preferred_element_type=F32)


def at(start, size=STEP):
    return pl.ds(pl.multiple_of(start, STEP), size)


class Copies:
    def __init__(self, send_sems, recv_sems):
        self.send_sems, self.recv_sems, self.used = send_sems, recv_sems, 0

    def start(self, src, dst, axis, to):
        made = pltpu.make_async_remote_copy(
            src_ref=src,
            dst_ref=dst,
            send_sem=self.send_sems.at[self.used],
            recv_sem=self.recv_sems.at[self.used],
            device_id={axis: to},
            device_id_type=MESH,
        )
        self.used += 1
        made.start()
        return made


def greet(*peers):
    barrier = pltpu.get_barrier_semaphore()
    for axis, to in peers:
        pl.semaphore_signal(barrier, inc=1, device_id={axis: to}, device_id_type=MESH)
    pl.semaphore_wait(barrier, len(peers))


class Links:
    def __init__(self, size, rows, copies):
        me = lax.axis_index("tensor")
        hi, lo = me // 2, me % 2
        self.me, self.size, self.high, self.half = me, size, size // 2, rows // 2
        self.near = hi * 2 + (1 - lo)
        self.ahead = [lax.rem(hi + s, self.high) * 2 + lo for s in range(self.high)]
        self.behind = [
            lax.rem(hi + self.high - s, self.high) * 2 + lo for s in range(self.high)
        ]
        self.second = self.half * size
        self.copies = copies
        steps = range(self.high)
        grid = [[lax.rem(hi + s, self.high) * 2 + (lo + l) % 2 for l in range(2)] for s in steps]
        self.first_ranks = [grid[s][l] for s in steps for l in range(2)]
        self.second_ranks = [grid[s][l] for l in range(2) for s in steps]
        self.peers = [("tensor", to) for to in [self.near] + self.ahead[1:]]

    def copy(self, src, dst, to):
        return self.copies.start(src, dst, "tensor", to)


class Column:
    def __init__(self, size, copies):
        self.me, self.chips, self.copies = lax.axis_index("dp"), size // 2, copies
        self.chip, self.core = self.me // 2, self.me % 2
        self.twin = self.chip * 2 + 1 - self.core
        self.right = self.block(1)
        self.left = self.block(-1)
        self.ring = [("dp", self.left)]
        self.pair = [("dp", self.twin)]

    def chip_at(self, step):
        return lax.rem(self.chip + self.chips + step, self.chips)

    def block(self, step):
        return self.chip_at(step) * 2 + self.core

    def copy(self, src, dst, to):
        return self.copies.start(src, dst, "dp", to)


class WeightRing:
    def __init__(self, column, loads, own, slot):
        self.column, self.loads, self.own, self.slot = column, loads, own, slot

    def start(self):
        k = self.column
        here = self.slot(k.me)
        self.hops = [k.copy(self.own, here, k.right)]
        self.twins = [k.copy(self.own, here, k.twin)]
        self.local = self.loads.copy(self.own, here)

    def advance(self):
        k = self.column
        step = len(self.twins)
        self.hops[step - 1].wait_recv()
        here = self.slot(k.block(-step))
        if step < k.chips - 1:
            self.hops.append(k.copy(here, here, k.right))
        self.twins.append(k.copy(here, here, k.twin))

    def finish(self):
        while len(self.twins) < self.column.chips:
            self.advance()
        for made in self.twins:
            made.wait()
        for made in self.hops:
            made.wait_send()
        self.local.wait()


def ring_copies(size):
    return size // 2 * 2 - 1


class SumRing:
    def __init__(self, column, loads, mine, twin, target, own, other, landing, staged, tile, tile_sems):
        self.column, self.loads = column, loads
        self.mine, self.twin, self.target = mine, twin, target
        self.own, self.other, self.landing, self.staged = own, other, landing, staged
        self.tile, self.tile_sems = tile, tile_sems
        self.hops = []
        self.rows = tile.shape[1]

    def load(self):
        block = self.column.chip_at(-1 - len(self.hops))
        self.loading = [
            self.loads.copy(self.mine.at[block], self.own),
            self.loads.copy(self.twin.at[block], self.other),
        ]

    def send(self, landed):
        k, rows = self.column, self.rows

        def body(i, _):
            here = pl.ds(pl.multiple_of(i * rows, rows), rows)
            value = self.own[here, :].astype(F32) + self.other[here, :].astype(F32)
            if landed is not None:
                value = value + self.landing[landed, here, :].astype(F32)
            self.staged[here, :] = value.astype(BF16)
            return 0

        lax.fori_loop(0, self.own.shape[0] // rows, body, 0)
        self.hops.append(k.copy(self.staged, self.landing.at[len(self.hops)], k.right))
        self.load()

    def start(self):
        self.load()
        wait_all(self.loading)
        self.send(None)

    def advance(self):
        self.hops[-1].wait()
        wait_all(self.loading)
        self.send(len(self.hops) - 1)

    def finish(self):
        k, rows = self.column, self.rows
        while len(self.hops) < k.chips - 1:
            self.advance()
        self.hops[-1].wait()
        wait_all(self.loading)
        landed = k.chips - 2

        def body(i, _):
            here = pl.ds(pl.multiple_of(i * rows, rows), rows)
            slot = lax.rem(i, 2)
            copy = pltpu.make_async_copy(
                self.tile.at[slot], self.target.at[here], self.tile_sems.at[slot]
            )

            @pl.when(i >= 2)
            def _():
                copy.wait()

            value = self.own[here, :].astype(F32) + self.other[here, :].astype(F32)
            self.tile[slot] = value + self.landing[landed, here, :].astype(F32)
            copy.start()
            return 0

        count = self.own.shape[0] // rows
        lax.fori_loop(0, count, body, 0)
        for i in range(max(count - 2, 0), count):
            here = pl.ds(i * rows, rows)
            pltpu.make_async_copy(
                self.tile.at[i % 2], self.target.at[here], self.tile_sems.at[i % 2]
            ).wait()


def sum_rows(width):
    return 128 if width <= 256 else 16


def sum_scratch(chips, rows, width):
    return [
        ((rows, width), BF16),
        ((rows, width), BF16),
        ((chips - 1, rows, width), BF16),
        ((rows, width), BF16),
        ((2, sum_rows(width), width), F32),
    ]


def transfers(size):
    return 2 * (size // 2)


class Gather:
    def __init__(self, links, buf, base):
        self.links, self.buf, self.base = links, buf, base

    def rows(self, start, count):
        return self.buf.at[pl.ds(self.base + start, count)]

    def start(self):
        k, half, second = self.links, self.links.half, self.links.second
        self.first_near = k.copy(self.rows(0, half), self.rows(half, half), k.near)
        self.second_far = [
            k.copy(self.rows(second, half), self.rows(second + s * half, half), k.behind[s])
            for s in range(1, k.high)
        ]

    def middle(self):
        k, half, second = self.links, self.links.half, self.links.second
        self.first_near.wait_recv()
        self.first_far = [
            k.copy(self.rows(0, 2 * half), self.rows(2 * half * s, 2 * half), k.behind[s])
            for s in range(1, k.high)
        ]
        for made in self.second_far:
            made.wait_recv()
        block = k.high * half
        self.second_near = k.copy(self.rows(second, block), self.rows(second + block, block), k.near)

    def finish(self):
        for made in self.first_far + [self.second_near]:
            made.wait_recv()
        for made in [self.first_near, self.second_near] + self.first_far + self.second_far:
            made.wait_send()


class Scatter:
    def __init__(self, links, part, base, landing, staged, last, total):
        self.links, self.part, self.base = links, part, base
        self.landing, self.staged, self.last, self.total = landing, staged, last, total

    def start(self):
        k, half = self.links, self.links.half
        block = k.high * half
        self.first_far = [
            k.copy(
                self.part.at[pl.ds(self.base + 2 * half * s, 2 * half)],
                self.landing.at[pl.ds(2 * half * (s - 1), 2 * half)],
                k.ahead[s],
            )
            for s in range(1, k.high)
        ]
        self.second_near = k.copy(
            self.part.at[pl.ds(self.base + k.second + block, block)],
            self.landing.at[pl.ds(2 * half * (k.high - 1), block)],
            k.near,
        )

    def middle(self):
        k, half, base = self.links, self.links.half, self.base
        steps = half // STEP
        for made in self.first_far:
            made.wait_recv()

        def first(i, _):
            for where in range(2):
                row = where * half + i * STEP
                value = self.part[at(base + row), :].astype(F32)
                for s in range(1, k.high):
                    value = value + self.landing[at(2 * half * (s - 1) + row), :].astype(F32)
                if where == 0:
                    self.total[at(i * STEP), :] = value
                else:
                    self.staged[at(i * STEP), :] = value.astype(BF16)
            return 0

        lax.fori_loop(0, steps, first, 0)
        self.first_near = k.copy(
            self.staged.at[pl.ds(0, half)], self.last.at[pl.ds(0, half)], k.near
        )
        self.second_near.wait_recv()
        landed = 2 * half * (k.high - 1)

        def second(i, _):
            for s in range(k.high):
                row = s * half + i * STEP
                value = self.part[at(base + k.second + row), :].astype(F32)
                value = value + self.landing[at(landed + row), :].astype(F32)
                if s == 0:
                    self.total[at(half + i * STEP), :] = value
                else:
                    self.staged[at(row), :] = value.astype(BF16)
            return 0

        lax.fori_loop(0, steps, second, 0)
        self.second_far = [
            k.copy(
                self.staged.at[pl.ds(half * s, half)], self.last.at[pl.ds(half * s, half)], k.ahead[s]
            )
            for s in range(1, k.high)
        ]
        for made in self.first_far + [self.second_near]:
            made.wait_send()

    def finish(self):
        for made in [self.first_near] + self.second_far:
            made.wait_recv()
            made.wait_send()

    def chunk(self, where, i):
        k, half = self.links, self.links.half
        value = self.total[at(where * half + i * STEP), :]
        if where == 0:
            return value + self.last[at(i * STEP), :].astype(F32)
        for s in range(1, k.high):
            value = value + self.last[at(half * s + i * STEP), :].astype(F32)
        return value


def over_rows(half, body):
    for where in range(2):

        def inner(i, _, where=where):
            body(where, i, where * half + i * STEP)
            return 0

        lax.fori_loop(0, half // STEP, inner, 0)


class Loads:
    def __init__(self, sems):
        self.sems, self.used = sems, 0

    def copy(self, src, dst):
        made = pltpu.make_async_copy(src, dst, self.sems.at[self.used])
        self.used += 1
        made.start()
        return made


def wait_all(*groups):
    for group in groups:
        for made in group if isinstance(group, list) else [group]:
            made.wait()


def columns_in(loads, blocks, flat):
    count, _, width = blocks.shape
    return [loads.copy(blocks.at[j], flat.at[:, pl.ds(j * width, width)]) for j in range(count)]


def halves_out(column, count, make, tile, mine, twin, sems, twin_sem):
    wide = tile.shape[3]

    def outs(c, slot):
        here = pl.ds(pl.multiple_of(c * wide, wide), wide)
        local = pltpu.make_async_copy(tile.at[slot, 0], mine.at[:, here, :], sems.at[slot])
        away = pltpu.make_async_remote_copy(
            src_ref=tile.at[slot, 1],
            dst_ref=twin.at[:, here, :],
            send_sem=sems.at[2 + slot],
            recv_sem=twin_sem.at[0],
            device_id={"dp": column.twin},
            device_id_type=MESH,
        )
        return local, away

    def body(c, _):
        slot = lax.rem(c, 2)
        local, away = outs(c, slot)

        @pl.when(c >= 2)
        def _():
            local.wait()
            away.wait_send()

        def put(block, value):
            tile[slot, lax.rem(block + column.core, 2), block // 2] = value

        make(c, put)
        local.start()
        away.start()
        return 0

    lax.fori_loop(0, count, body, 0)
    for c in range(max(count - 2, 0), count):
        local, away = outs(c, c % 2)
        local.wait()
        away.wait_send()
    all_landed(column, twin, sems, twin_sem)


def blocks_out(column, make, tile, mine, twin, sems, twin_sem):
    def outs(i):
        local = pltpu.make_async_copy(tile.at[0], mine.at[i], sems.at[0])
        away = pltpu.make_async_remote_copy(
            src_ref=tile.at[1],
            dst_ref=twin.at[i],
            send_sem=sems.at[1],
            recv_sem=twin_sem.at[0],
            device_id={"dp": column.twin},
            device_id_type=MESH,
        )
        return local, away

    def body(i, _):
        local, away = outs(i)

        @pl.when(i > 0)
        def _():
            away.wait_send()

        make(2 * i + 1 - column.core, tile.at[1])
        away.start()

        @pl.when(i > 0)
        def _():
            local.wait()

        make(2 * i + column.core, tile.at[0])
        local.start()
        return 0

    lax.fori_loop(0, column.chips, body, 0)
    local, away = outs(column.chips - 1)
    local.wait()
    away.wait_send()
    all_landed(column, twin, sems, twin_sem)


def all_landed(column, twin, sems, twin_sem):
    pltpu.make_async_remote_copy(
        src_ref=twin,
        dst_ref=twin,
        send_sem=sems.at[0],
        recv_sem=twin_sem.at[0],
        device_id={"dp": column.twin},
        device_id_type=MESH,
    ).wait_recv()


def normalized(value):
    centred = value - jnp.mean(value, axis=-1, keepdims=True)
    inverse = lax.rsqrt(jnp.mean(centred * centred, axis=-1, keepdims=True) + EPSILON)
    return centred * inverse, inverse


def norm_back(back, normed, inverse, gain):
    scaled = back * gain
    inner = jnp.mean(scaled, axis=-1, keepdims=True)
    along = jnp.mean(scaled * normed, axis=-1, keepdims=True)
    return inverse * (scaled - inner - normed * along)


def softmax_lanes(logits, lanes):
    logits = jnp.where(lanes, logits, MASKED)
    powers = jnp.exp(logits - jnp.max(logits, axis=-1, keepdims=True))
    return jnp.where(lanes, powers / jnp.sum(powers, axis=-1, keepdims=True), 0.0)


def turned(value, cosine, sine):
    return value * cosine + pltpu.roll(value, HD // 2, 1) * sine


def first_norm_kernel(
    dp_size,
    size,
    heads,
    units,
    tokens,
    params,
    rates,
    bucket,
    lengths,
    choices,
    mixer,
    merger,
    rows_out,
    mix_out,
    out_out,
    mask,
    cosine,
    sine,
    row_info,
    own,
    seq_info,
    usage,
    buf,
    slot_col,
    member_col,
    bucket_col,
    send,
    recv,
    load_sems,
):
    micro, rows, _ = tokens.shape
    count = lengths.shape[1]
    copies, loads = Copies(send, recv), Loads(load_sems)
    links, column = Links(size, rows, copies), Column(dp_size, copies)
    total = rows * size
    greet(*links.peers, *column.ring, *column.pair)
    rings = [
        WeightRing(column, loads, mixer, lambda i: mix_out.at[i]),
        WeightRing(column, loads, merger, lambda i: out_out.at[i]),
    ]
    for ring in rings:
        ring.start()
    gathers = []
    for m in range(micro):

        def body(where, i, row, m=m):
            value = tokens[m, at(row), :].astype(F32)
            low = normalized(value)[0] * params[ATTEND : ATTEND + 1, :]
            low = (low + params[ATTEND + 1 : ATTEND + 2, :]).astype(BF16)
            buf[at(m * total + where * links.second + i * STEP), :] = low

        over_rows(links.half, body)
        gathers.append(Gather(links, buf, m * total))
        gathers[m].start()

    half = links.half
    starts = [r * rows for r in links.first_ranks] + [r * rows + half for r in links.second_ranks]

    def slots(shape, dimension):
        index = lax.broadcasted_iota(jnp.int32, shape, dimension)
        offset = jnp.full(shape, starts[0], jnp.int32)
        for k in range(1, len(starts)):
            offset = jnp.where(index >= k * half, starts[k] - k * half, offset)
        return index + offset

    def ends(m):
        found, end = [], 0
        for s in range(count):
            end = end + lengths[m, s]
            found.append(end)
        return found

    def members(m, slot):
        member = jnp.zeros(slot.shape, jnp.int32)
        begin = jnp.zeros(slot.shape, jnp.int32)
        for end in ends(m):
            member = member + jnp.where(slot >= end, 1, 0)
            begin = jnp.where(slot >= end, end, begin)
        return member, slot - begin

    def by_member(member, values, other):
        value = jnp.full(member.shape, other)
        for s in range(count):
            value = jnp.where(member == s, values[s], value)
        return value

    chunk = min(128, total)
    lane = lax.broadcasted_iota(jnp.int32, (chunk, LANES), 1)
    slot_row = slots((8, total), 1)
    slot_col[...] = slots((total, LANES), 0)
    member_rows = [members(m, slot_row)[0] for m in range(micro)]
    for m in range(micro):

        def table(c, _, m=m):
            here = pl.ds(pl.multiple_of(c * chunk, chunk), chunk)
            slot = slot_col[here, :]
            member, place = members(m, slot)
            member_col[m, here, :] = member
            seen = (member[:, :1] == member_rows[m][:1, :]) & (slot[:, :1] >= slot_row[:1, :])
            mask[m, here, :] = jnp.where(seen, 0.0, MASKED)
            angle = place.astype(F32) * rates[...]
            turn = jnp.sin(angle)
            cosine[m, here, :] = jnp.cos(angle)
            sine[m, here, :] = jnp.where(lane < HD // 2, -turn, turn)
            natural = lax.broadcasted_iota(jnp.int32, (chunk, total), 1)
            picked = jnp.where(slot[:, :1] == natural, bucket[m : m + 1, :].astype(F32), 0.0)
            bucket_here = jnp.sum(picked, axis=-1, keepdims=True)
            bucket_col[m, here, :] = jnp.broadcast_to(bucket_here, (chunk, LANES))
            used = by_member(member, [H // NHC * (choices[m, s] + 1) for s in range(count)], 0)
            head_on = jnp.where(links.me * heads + lane < used, 1.0, 0.0)
            first_unit = jnp.full(lane.shape, links.me * units, jnp.int32).astype(F32)
            unit_on = jnp.where(first_unit < FF // NB * (bucket_here + 1.0), 1.0, 0.0)
            row_info[m, here, :] = jnp.where(
                lane < heads, head_on, jnp.where(lane == heads, unit_on, 0.0)
            )
            return 0

        lax.fori_loop(0, total // chunk, table, 0)
    for g in gathers:
        g.middle()
    for ring in rings:
        ring.advance()
    outs = []
    usage[...] = jnp.zeros_like(usage)
    few = lax.broadcasted_iota(jnp.int32, (8, LANES), 1)
    which = lax.broadcasted_iota(jnp.int32, (8, LANES), 0)
    lane_own = lax.broadcasted_iota(jnp.int32, (half, LANES), 1)
    for m, g in enumerate(gathers):
        g.finish()
        here = pl.ds(m * total, total)
        outs.append(loads.copy(buf.at[here], rows_out.at[here]))
        sequence = lax.broadcasted_iota(jnp.int32, (8, total), 0)
        hot = jnp.where(member_rows[m] == sequence, 1.0, 0.0).astype(BF16)
        divisor = jnp.maximum(by_member(which, [lengths[m, s] for s in range(count)], 0), 1)
        divisor = divisor.astype(F32)
        chosen = by_member(which, [choices[m, s] for s in range(count)], 0)
        means = dot(hot, buf[here, :]) / divisor[:, :1]
        logits = jnp.full((8, LANES), MASKED)
        for c in range(NHC):
            router = params[HEAD_ROUTER + c : HEAD_ROUTER + c + 1, :]
            logit = jnp.sum(means * router, axis=-1, keepdims=True)
            logits = jnp.where(few == c, logit, logits)
        share = softmax_lanes(logits, few < NHC)
        picked = jnp.sum(jnp.where(few == chosen, share, 0.0), axis=-1, keepdims=True)
        table = jnp.where(few == PICKED, picked, share)
        table = jnp.where(few == DIVISOR, divisor, table)
        seq_info[m] = jnp.where(few == CHOSEN, chosen.astype(F32), table)
        for where in range(2):
            source = pl.ds(where * links.second, half)
            member = member_col[m, source, :]
            gate = by_member(member, [NHC * picked[s : s + 1, :] for s in range(count)], 0.0)
            choice = by_member(member, [choices[m, s] for s in range(count)], -NHC)
            live = jnp.where(member < count, 1.0, 0.0)
            kind = bucket_col[m, source, :].astype(jnp.int32)
            hot = (lane_own == kind) | (lane_own == CHOICE + choice)
            hot = hot | ((lane_own == SEQ + member) & (member < count))
            value = jnp.where(hot & (choice >= -NHC), 1.0, 0.0)
            value = jnp.where(lane_own == GATE, gate, value)
            value = jnp.where(lane_own == LIVE, live, value)
            own[m, pl.ds(where * half, half), :] = value
            usage[0:1, :] += jnp.sum(value * live, axis=0, keepdims=True)
    for step in range(column.chips - 2):
        for ring in rings:
            ring.advance()
    for ring in rings:
        ring.finish()
    wait_all(outs)


def attend_kernel(
    dp_size,
    size,
    heads,
    rows_hbm,
    mix_hbm,
    out_hbm,
    mask_hbm,
    cosine,
    sine,
    row_info,
    own,
    tokens,
    cotangent,
    params,
    expand,
    shrink,
    qkv_out,
    heads_out,
    attention_out,
    second_out,
    share_out,
    branch_out,
    up_out,
    down_out,
    rows_buf,
    mix,
    out,
    mask,
    qkv,
    head_rows,
    part,
    landing,
    staged,
    last,
    second_buf,
    send,
    recv,
    load_sems,
):
    micro, rows, width = tokens.shape
    total = rows * size
    copies, loads = Copies(send, recv), Loads(load_sems)
    links, column = Links(size, rows, copies), Column(dp_size, copies)
    half = links.half
    mix_copy = loads.copy(mix_hbm, mix)
    row_copies = [
        loads.copy(rows_hbm.at[pl.ds(m * total, total)], rows_buf.at[pl.ds(m * total, total)])
        for m in range(micro)
    ]
    mask_copy = loads.copy(mask_hbm, mask)
    out_copies = columns_in(loads, out_hbm, out)
    greet(*links.peers, *column.ring, *column.pair)
    early = shrink.shape[0] // 2
    rings = [
        WeightRing(column, loads, expand, lambda i: up_out.at[i]),
        WeightRing(column, loads, shrink.at[pl.ds(0, early)], lambda i: down_out.at[i]),
    ]
    for ring in rings:
        ring.start()
    mix_copy.wait()
    scale = HD ** (-0.5)
    span = 3 * HD
    chunk = min(128, total)
    tile = min(512, width)
    saves = []

    def project(m):
        base = m * total
        cos, sin = cosine[m], sine[m]

        def head(h, _):
            mixed = dot(
                rows_buf[pl.ds(base, total), :], mix[:, pl.ds(pl.multiple_of(h * span, HD), span)]
            )
            here = pl.ds(pl.multiple_of(h * HD, HD), HD)
            qkv[m, 0, :, here] = turned(mixed[:, :HD], cos, sin).astype(BF16)
            qkv[m, 1, :, here] = turned(mixed[:, HD : 2 * HD], cos, sin).astype(BF16)
            qkv[m, 2, :, here] = mixed[:, 2 * HD :].astype(BF16)
            return 0

        lax.fori_loop(0, heads, head, 0)

    def attend(m):
        base = m * total

        def some(c, _):
            rows_here = pl.ds(pl.multiple_of(c * chunk, chunk), chunk)
            bias_here = mask[m, rows_here, :]
            info = row_info[m, rows_here, :]
            for h in range(heads):
                here = pl.ds(h * HD, HD)
                scores = dot_nt(qkv[m, 0, rows_here, here], qkv[m, 1, :, here]) * scale + bias_here
                peak = jnp.max(scores, axis=-1, keepdims=True)
                powers = jnp.exp(scores - peak)
                share = powers / jnp.sum(powers, axis=-1, keepdims=True)
                value = dot(share.astype(BF16), qkv[m, 2, :, here]).astype(BF16)
                value = value.astype(F32) * info[:, h : h + 1]
                head_rows[pl.ds(pl.multiple_of(base + c * chunk, chunk), chunk), here] = value.astype(
                    BF16
                )
            return 0

        lax.fori_loop(0, total // chunk, some, 0)

    def merge(m):
        base = m * total

        def body(j, _):
            here = pl.ds(pl.multiple_of(j * tile, tile), tile)
            part[pl.ds(base, total), here] = dot(
                head_rows[pl.ds(base, total), :], out[:, here]
            ).astype(BF16)
            return 0

        lax.fori_loop(0, width // tile, body, 0)

    scatters = [
        Scatter(
            links,
            part,
            m * total,
            landing.at[m],
            staged.at[m],
            last.at[m],
            attention_out.at[m],
        )
        for m in range(micro)
    ]
    gathers = [Gather(links, second_buf, m * total) for m in range(micro)]

    def second_norm(m):
        scatter = scatters[m]

        def body(where, i, row):
            attended = scatter.chunk(where, i)
            info = own[m, at(row), :]
            hidden = tokens[m, at(row), :].astype(F32) + info[:, GATE : GATE + 1] * attended
            attention_out[m, at(row), :] = attended
            low = normalized(hidden)[0] * params[FEED : FEED + 1, :]
            low = (low + params[FEED + 1 : FEED + 2, :]).astype(BF16)
            second_buf[at(m * total + where * links.second + i * STEP), :] = low
            low = low.astype(F32)
            lane = lax.broadcasted_iota(jnp.int32, (STEP, LANES), 1)
            logits = jnp.full((STEP, LANES), MASKED)
            for b in range(NB):
                router = params[WIDTH_ROUTER + b : WIDTH_ROUTER + b + 1, :]
                logits = jnp.where(lane == b, jnp.sum(low * router, axis=-1, keepdims=True), logits)
            share = softmax_lanes(logits, lane < NB)
            share_out[m, at(row), :] = share
            gate = NB * jnp.sum(share * info, axis=-1, keepdims=True)
            outer = cotangent[m, at(row), :].astype(F32) * info[:, LIVE : LIVE + 1]
            branch_out[m, at(row), :] = (gate * outer).astype(BF16)

        over_rows(half, body)

    for m in range(micro):
        row_copies[m].wait()
        project(m)
        if m > 0:
            scatters[m - 1].middle()
            for ring in rings:
                ring.advance()
        if m == 0:
            mask_copy.wait()
        attend(m)
        if m == 0:
            wait_all(out_copies)
        merge(m)
        scatters[m].start()
    for m in range(micro):
        if m == micro - 1:
            scatters[m].middle()
        scatters[m].finish()
        second_norm(m)
        gathers[m].start()
        if m > 0:
            gathers[m - 1].middle()
        if m == 0:
            for ring in rings:
                ring.advance()
    saves.append(loads.copy(qkv, qkv_out))
    saves.append(loads.copy(head_rows, heads_out))
    gathers[micro - 1].middle()
    for m in range(micro):
        gathers[m].finish()
        here = pl.ds(m * total, total)
        saves.append(loads.copy(second_buf.at[here], second_out.at[here]))
    for ring in rings:
        ring.finish()
    wait_all(saves)


def widen_kernel(
    dp_size,
    size,
    unit_lane,
    second_hbm,
    up_hbm,
    branch,
    row_info,
    shrink,
    rect_out,
    active_out,
    branch_out,
    down_out,
    mine_out,
    twin_out,
    second_rows,
    up,
    branch_buf,
    rect,
    active,
    tile,
    send,
    recv,
    load_sems,
    tile_sems,
    twin_sem,
):
    micro, rows, width = branch.shape
    total = rows * size
    units = up.shape[1]
    copies, loads = Copies(send, recv), Loads(load_sems)
    links, column = Links(size, rows, copies), Column(dp_size, copies)
    up_copy = loads.copy(up_hbm, up)
    second_copies = [
        loads.copy(second_hbm.at[pl.ds(m * total, total)], second_rows.at[pl.ds(m * total, total)])
        for m in range(micro)
    ]
    half = links.half
    own_copies = []
    for m in range(micro):
        for where in range(2):
            own_copies.append(
                loads.copy(
                    branch.at[m, pl.ds(where * half, half)],
                    branch_buf.at[pl.ds(m * total + where * links.second, half)],
                )
            )
    greet(*links.peers, *column.ring, *column.pair)
    late = shrink.shape[0] // 2
    ring = WeightRing(column, loads, shrink.at[pl.ds(late, late)], lambda i: down_out.at[i])
    ring.start()
    wait_all(own_copies)
    gathers = [Gather(links, branch_buf, m * total) for m in range(micro)]
    for g in gathers:
        g.start()
    up_copy.wait()
    step = min(512, units)
    saves = []
    for m in range(micro):
        second_copies[m].wait()

        def body(j, _, m=m):
            here = pl.ds(pl.multiple_of(j * step, step), step)
            before = dot(second_rows[pl.ds(m * total, total), :], up[:, here])
            kept = jnp.maximum(before, 0.0) * row_info[m, :, unit_lane : unit_lane + 1]
            rect[pl.ds(m * total, total), here] = kept.astype(BF16)
            active[pl.ds(m * total, total), here] = (kept * kept).astype(BF16)
            return 0

        lax.fori_loop(0, units // step, body, 0)
        gathers[m].middle()
        if m < column.chips - 1:
            ring.advance()
        here = pl.ds(m * total, total)
        saves.append(loads.copy(rect.at[here], rect_out.at[here]))
        saves.append(loads.copy(active.at[here], active_out.at[here]))
    for m, g in enumerate(gathers):
        g.finish()
        here = pl.ds(m * total, total)
        saves.append(loads.copy(branch_buf.at[here], branch_out.at[here]))
    block, wide = mine_out.shape[2], tile.shape[3]

    def make(c, put):
        value = dot_tn(active[:, pl.ds(pl.multiple_of(c * wide, wide), wide)], branch_buf[...])
        for j in range(dp_size):
            put(j, value[:, j * block : (j + 1) * block].astype(BF16))

    halves_out(column, units // wide, make, tile, mine_out, twin_out, tile_sems, twin_sem)
    ring.finish()
    wait_all(saves)


def narrow_kernel(
    dp_size,
    size,
    down_early,
    down_late,
    up_hbm,
    active_hbm,
    rect_hbm,
    branch_hbm,
    second_hbm,
    tokens,
    cotangent,
    attention,
    share,
    own,
    params,
    mine_hbm,
    twin_hbm,
    block_out,
    mine_out,
    twin_out,
    hidden_out,
    back_out,
    stats_out,
    gate_out,
    sum_out,
    down,
    up,
    active,
    rect,
    shared_rows,
    part,
    landing,
    staged,
    last,
    total_rows,
    gate_back,
    tile,
    sum_own,
    sum_other,
    sum_landing,
    sum_staged,
    sum_tile,
    send,
    recv,
    load_sems,
    tile_sems,
    twin_sem,
    sum_sems,
):
    micro, rows, width = tokens.shape
    total = rows * size
    units = up.shape[1]
    copies, loads = Copies(send, recv), Loads(load_sems)
    links, column = Links(size, rows, copies), Column(dp_size, copies)
    half = links.half
    here = [pl.ds(m * total, total) for m in range(micro)]
    ring = SumRing(
        column,
        loads,
        mine_hbm,
        twin_hbm,
        sum_out,
        sum_own,
        sum_other,
        sum_landing,
        sum_staged,
        sum_tile,
        sum_sems,
    )
    early = down_early.shape[1]
    down_copies = columns_in(loads, down_early, down.at[pl.ds(0, early)])
    down_copies += columns_in(loads, down_late, down.at[pl.ds(early, early)])
    active_copies = [loads.copy(active_hbm.at[h], active.at[h]) for h in here]
    branch_copies = [loads.copy(branch_hbm.at[h], shared_rows.at[h]) for h in here]
    rect_copy = loads.copy(rect_hbm.at[here[0]], rect)
    up_copy = loads.copy(up_hbm, up)
    stats_out[...] = jnp.zeros_like(stats_out)
    gate_out[...] = jnp.zeros_like(gate_out)
    greet(*links.peers, *column.ring, *column.pair)
    ring.start()
    step = min(512, units)
    tile_cols = min(512, width)
    outs = [
        Scatter(
            links, part, m * total, landing.at[m], staged.at[m], last.at[m], total_rows.at[m]
        )
        for m in range(micro)
    ]
    backs = [
        Scatter(
            links,
            part,
            m * total,
            landing.at[micro + m],
            staged.at[micro + m],
            last.at[micro + m],
            hidden_out.at[m],
        )
        for m in range(micro)
    ]
    wait_all(down_copies)
    for m in range(micro):
        active_copies[m].wait()

        def body(j, _, m=m):
            cols = pl.ds(pl.multiple_of(j * tile_cols, tile_cols), tile_cols)
            part[here[m], cols] = dot(active[here[m], :], down[:, cols]).astype(BF16)
            return 0

        lax.fori_loop(0, width // tile_cols, body, 0)
        outs[m].start()
    for m in range(micro):
        branch_copies[m].wait()
        rect_copy.wait()

        def body(j, _, m=m):
            cols = pl.ds(pl.multiple_of(j * step, step), step)
            back = dot_nt(shared_rows[here[m], :], down[cols, :])
            active[here[m], cols] = (2.0 * rect[:, cols].astype(F32) * back).astype(BF16)
            return 0

        lax.fori_loop(0, units // step, body, 0)
        if m + 1 < micro:
            rect_copy = loads.copy(rect_hbm.at[here[m + 1]], rect)
        if m == 0:
            up_copy.wait()
    second_copies = [loads.copy(second_hbm.at[h], shared_rows.at[h]) for h in here]
    if column.chips > 2:
        ring.advance()
    for m in range(micro):
        outs[m].middle()

        def body(j, _, m=m):
            cols = pl.ds(pl.multiple_of(j * tile_cols, tile_cols), tile_cols)
            part[here[m], cols] = dot_nt(active[here[m], :], up[cols, :]).astype(BF16)
            return 0

        lax.fori_loop(0, width // tile_cols, body, 0)
        backs[m].start()

    def finish_out(m):
        outs[m].finish()

        def body(where, i, row):
            branch = outs[m].chunk(where, i)
            info = own[m, at(row), :]
            live = info[:, LIVE : LIVE + 1]
            outer = cotangent[m, at(row), :].astype(F32) * live
            hidden = tokens[m, at(row), :].astype(F32)
            hidden = hidden + info[:, GATE : GATE + 1] * attention[m, at(row), :]
            gate = NB * jnp.sum(share[m, at(row), :] * info, axis=-1, keepdims=True)
            block_out[m, at(row), :] = (live * (hidden + gate * branch)).astype(BF16)
            value = jnp.sum(outer * branch, axis=-1, keepdims=True)
            gate_back[m, at(row), :] = jnp.broadcast_to(value, (STEP, LANES))

        over_rows(half, body)

    def finish_back(m):
        backs[m].finish()

        def body(where, i, row):
            back = backs[m].chunk(where, i)
            info = own[m, at(row), :]
            portions = share[m, at(row), :]
            live = info[:, LIVE : LIVE + 1]
            outer = cotangent[m, at(row), :].astype(F32) * live
            hidden = tokens[m, at(row), :].astype(F32)
            attended = attention[m, at(row), :]
            hidden = hidden + info[:, GATE : GATE + 1] * attended
            normed, inverse = normalized(hidden)
            gain = params[FEED : FEED + 1, :]
            low = (normed * gain + params[FEED + 1 : FEED + 2, :]).astype(BF16).astype(F32)
            picked = jnp.sum(portions * info, axis=-1, keepdims=True)
            logit_back = NB * picked * (info - portions) * gate_back[m, at(row), :]
            for b in range(NB):
                column = logit_back[:, b : b + 1]
                back = back + column * params[WIDTH_ROUTER + b : WIDTH_ROUTER + b + 1, :]
                stats_out[2 + b : 3 + b, :] += jnp.sum(column * low, axis=0, keepdims=True)
            stats_out[0:1, :] += jnp.sum(back * normed, axis=0, keepdims=True)
            stats_out[1:2, :] += jnp.sum(back, axis=0, keepdims=True)
            hidden_back = outer + norm_back(back, normed, inverse, gain)
            hidden_out[m, at(row), :] = hidden_back
            back_out[m, at(row), :] = (info[:, GATE : GATE + 1] * hidden_back).astype(BF16)
            gate_part = jnp.sum(hidden_back * attended, axis=-1, keepdims=True)
            gate_out[m : m + 1, :] += jnp.sum(info * gate_part, axis=0, keepdims=True)

        over_rows(half, body)

    if column.chips > 3:
        ring.advance()
    for m in range(micro):
        finish_out(m)
    wait_all(second_copies)
    block = mine_out.shape[1]

    def make(c, ref):
        ref[...] = dot_tn(
            shared_rows[:, pl.ds(pl.multiple_of(c * block, block), block)], active[...]
        ).astype(BF16)

    blocks_out(column, make, tile, mine_out, twin_out, tile_sems, twin_sem)
    for m in range(micro):
        backs[m].middle()
    ring.finish()
    for m in range(micro):
        finish_back(m)


def attend_back_kernel(
    dp_size,
    size,
    heads,
    back,
    gate,
    out_hbm,
    qkv_hbm,
    heads_hbm,
    rows_hbm,
    mask_hbm,
    cosine,
    sine,
    row_info,
    mine_hbm,
    twin_hbm,
    mixed_out,
    out_mine,
    out_twin,
    mix_mine,
    mix_twin,
    gate_out,
    sum_out,
    buf,
    out,
    qkv,
    head_rows,
    rows_buf,
    mask,
    heads_back,
    mixed_back,
    score_back,
    shares,
    out_tile,
    mix_tile,
    gates,
    sum_own,
    sum_other,
    sum_landing,
    sum_staged,
    sum_tile,
    send,
    recv,
    load_sems,
    out_sems,
    out_twin_sem,
    mix_sems,
    mix_twin_sem,
    sum_sems,
):
    micro, rows, width = back.shape
    total = rows * size
    copies, loads = Copies(send, recv), Loads(load_sems)
    links, column = Links(size, rows, copies), Column(dp_size, copies)
    half = links.half
    ring = SumRing(
        column,
        loads,
        mine_hbm,
        twin_hbm,
        sum_out,
        sum_own,
        sum_other,
        sum_landing,
        sum_staged,
        sum_tile,
        sum_sems,
    )
    own_copies = []
    for m in range(micro):
        for where in range(2):
            own_copies.append(
                loads.copy(
                    back.at[m, pl.ds(where * half, half)],
                    buf.at[pl.ds(m * total + where * links.second, half)],
                )
            )
    out_copies = columns_in(loads, out_hbm, out)
    qkv_copy = loads.copy(qkv_hbm, qkv)
    mask_copy = loads.copy(mask_hbm, mask)
    heads_copy = loads.copy(heads_hbm, head_rows)
    rows_copy = loads.copy(rows_hbm, rows_buf)
    gates[links.me] = gate[...]
    others = [lax.rem(links.me + s, size) for s in range(1, size)]
    greet(*[("tensor", to) for to in others], *column.ring, *column.pair)
    wait_all(own_copies)
    gathers = [Gather(links, buf, m * total) for m in range(micro)]
    for g in gathers:
        g.start()
    ring.start()
    gate_copies = [links.copy(gate, gates.at[links.me], peer) for peer in others]
    wait_all(out_copies)
    qkv_copy.wait()
    mask_copy.wait()
    scale = HD ** (-0.5)
    chunk = min(128, total)
    for g in gathers:
        g.middle()
    for m in range(micro):
        gathers[m].finish()
        if m + 2 < column.chips:
            ring.advance()
        base = m * total
        every = pl.ds(base, total)
        value = dot_nt(buf[every, :], out[...])
        for h in range(heads):
            here = pl.ds(h * HD, HD)
            heads_back[:, here] = (
                value[:, h * HD : (h + 1) * HD] * row_info[m, :, h : h + 1]
            ).astype(BF16)
        for h in range(heads):
            here = pl.ds(h * HD, HD)

            def some(c, _, m=m, here=here):
                rows_here = pl.ds(pl.multiple_of(c * chunk, chunk), chunk)
                scores = dot_nt(qkv[m, 0, rows_here, here], qkv[m, 1, :, here]) * scale
                scores = scores + mask[m, rows_here, :]
                powers = jnp.exp(scores - jnp.max(scores, axis=-1, keepdims=True))
                share = powers / jnp.sum(powers, axis=-1, keepdims=True)
                share_back = dot_nt(heads_back[rows_here, here], qkv[m, 2, :, here])
                inner = jnp.sum(share * share_back, axis=-1, keepdims=True)
                score_back[rows_here, :] = (share * (share_back - inner)).astype(BF16)
                shares[rows_here, :] = share.astype(BF16)
                return 0

            lax.fori_loop(0, total // chunk, some, 0)
            cos, sin = cosine[m], -sine[m]
            query_back = dot(score_back[...], qkv[m, 1, :, here]) * scale
            keys_back = dot_tn(score_back[...], qkv[m, 0, :, here]) * scale
            values_back = dot_tn(shares[...], heads_back[:, here])
            col = 3 * h * HD
            mixed_back[every, pl.ds(col, HD)] = turned(query_back, cos, sin).astype(BF16)
            mixed_back[every, pl.ds(col + HD, HD)] = turned(keys_back, cos, sin).astype(BF16)
            mixed_back[every, pl.ds(col + 2 * HD, HD)] = values_back.astype(BF16)
    mixed_save = loads.copy(mixed_back, mixed_out)
    heads_copy.wait()
    block, wide = out_mine.shape[2], out_tile.shape[3]

    def make_out(c, put):
        value = dot_tn(head_rows[:, pl.ds(pl.multiple_of(c * wide, wide), wide)], buf[...])
        for j in range(dp_size):
            put(j, value[:, j * block : (j + 1) * block].astype(BF16))

    halves_out(
        column, heads * HD // wide, make_out, out_tile, out_mine, out_twin, out_sems, out_twin_sem
    )
    rows_copy.wait()

    def make_mix(c, ref):
        ref[...] = dot_tn(
            rows_buf[:, pl.ds(pl.multiple_of(c * block, block), block)], mixed_back[...]
        ).astype(BF16)

    blocks_out(column, make_mix, mix_tile, mix_mine, mix_twin, mix_sems, mix_twin_sem)
    ring.finish()
    for made in gate_copies:
        made.wait()
    gate_sum = gates[0]
    for r in range(1, size):
        gate_sum = gate_sum + gates[r]
    gate_out[...] = gate_sum
    mixed_save.wait()


STATS_ONE = 6
STATS_USE = 12
STATS_ROWS = 16
SEQ_COUNT = 4


def first_back_kernel(
    dp_size,
    size,
    micro,
    mixed_hbm,
    mix_hbm,
    mix_mine,
    mix_twin,
    out_mine,
    out_twin,
    tokens,
    hidden_back,
    own,
    seq_info,
    gates,
    params,
    stats_two,
    usage,
    back_out,
    mix_sum,
    out_sum,
    stats_out,
    mixed_back,
    mix,
    part,
    landing,
    staged,
    last,
    *rest,
):
    mix_bufs, out_bufs = rest[:5], rest[5:10]
    stats, share, pieces, sums, whole = rest[10:15]
    send, recv, load_sems, mix_sems, out_sems = rest[15:]
    total = mixed_back.shape[0] // micro
    rows = total // size
    width = mix.shape[0]
    copies, loads = Copies(send, recv), Loads(load_sems)
    links, column = Links(size, rows, copies), Column(dp_size, copies)
    here = [pl.ds(m * total, total) for m in range(micro)]
    rings = [
        SumRing(column, loads, mix_mine, mix_twin, mix_sum, *mix_bufs, mix_sems),
        SumRing(column, loads, out_mine, out_twin, out_sum, *out_bufs, out_sems),
    ]
    mix_copy = loads.copy(mix_hbm, mix)
    mixed_copies = [loads.copy(mixed_hbm.at[h], mixed_back.at[h]) for h in here]
    near = [lax.rem(links.me + s, size) for s in range(1, size)]
    far = [lax.rem(column.me + s, dp_size) for s in range(1, dp_size)]
    greet(*[("tensor", to) for to in near], *[("dp", to) for to in far])
    for ring in rings:
        ring.start()
    stats[...] = jnp.zeros_like(stats)
    stats[0:8, :] = stats_two[...]
    stats[STATS_USE : STATS_USE + 1, 0:LANES] = usage[0:1, :]
    scatters = [
        Scatter(links, part, m * total, landing.at[m], staged.at[m], last.at[m], back_out.at[m])
        for m in range(micro)
    ]
    mix_copy.wait()
    tile = min(512, width)
    for m in range(micro):
        mixed_copies[m].wait()

        def body(j, _, m=m):
            cols = pl.ds(pl.multiple_of(j * tile, tile), tile)
            part[here[m], cols] = dot_nt(mixed_back[here[m], :], mix[cols, :]).astype(BF16)
            return 0

        lax.fori_loop(0, width // tile, body, 0)
        scatters[m].start()
    if column.chips > 2:
        for ring in rings:
            ring.advance()
    for s in scatters:
        s.middle()
    if column.chips > 3:
        for ring in rings:
            ring.advance()
    for m, s in enumerate(scatters):
        s.finish()

        count = SEQ_COUNT
        lane = lax.broadcasted_iota(jnp.int32, (8, LANES), 1)
        which = lax.broadcasted_iota(jnp.int32, (8, LANES), 0)
        info = seq_info[m]
        gate_back = jnp.where(lane == SEQ + which, gates[m : m + 1, :], 0.0)
        gate_back = jnp.sum(gate_back, axis=-1, keepdims=True)
        chosen = jnp.where(lane == info[:, CHOSEN : CHOSEN + 1].astype(jnp.int32), 1.0, 0.0)
        logit_back = NHC * info[:, PICKED : PICKED + 1] * (chosen - info) * gate_back
        logit_back = logit_back / info[:, DIVISOR : DIVISOR + 1]

        def body(where, i, row, m=m, s=s, logit_back=logit_back):
            back = s.chunk(where, i)
            normed, inverse = normalized(tokens[m, at(row), :].astype(F32))
            gain = params[ATTEND : ATTEND + 1, :]
            low = (normed * gain + params[ATTEND + 1 : ATTEND + 2, :]).astype(BF16).astype(F32)
            rows_info = own[m, at(row), :]
            spread = jnp.zeros((STEP, LANES), F32)
            for q in range(count):
                spread = spread + rows_info[:, SEQ + q : SEQ + q + 1] * logit_back[q : q + 1, :]
            for c in range(NHC):
                column = spread[:, c : c + 1]
                back = back + column * params[HEAD_ROUTER + c : HEAD_ROUTER + c + 1, :]
                at_row = STATS_ONE + 2 + c
                stats[at_row : at_row + 1, :] += jnp.sum(column * low, axis=0, keepdims=True)
            at_row = STATS_ONE
            stats[at_row : at_row + 1, :] += jnp.sum(back * normed, axis=0, keepdims=True)
            stats[at_row + 1 : at_row + 2, :] += jnp.sum(back, axis=0, keepdims=True)
            value = norm_back(back, normed, inverse, gain)
            back_out[m, at(row), :] = hidden_back[m, at(row), :] + value

        over_rows(links.half, body)

    piece = width // size
    mine = pl.ds(pl.multiple_of(links.me * piece, piece), piece)
    sent = [
        links.copy(
            stats.at[:, pl.ds(pl.multiple_of(to * piece, piece), piece)], pieces.at[links.me], to
        )
        for to in near
    ]
    pieces[links.me] = stats[:, mine]
    wait_all(sent)
    value = pieces[0]
    for r in range(1, size):
        value = value + pieces[r]
    share[0] = value
    sums[column.me] = value
    wait_all([column.copy(share.at[0], sums.at[column.me], to) for to in far])
    value = sums[0]
    for r in range(1, dp_size):
        value = value + sums[r]
    share[1] = value
    whole[links.me] = value
    wait_all([links.copy(share.at[1], whole.at[links.me], to) for to in near])
    for r in range(size):
        stats_out[:, r * piece : (r + 1) * piece] = whole[r]
    for ring in rings:
        ring.finish()


ANY = pl.BlockSpec(memory_space=pl.ANY)
VMEM = pl.BlockSpec(memory_space=pltpu.VMEM)
SMEM = pl.BlockSpec(memory_space=pltpu.SMEM)


def call(kernel, ident, ins, outs, scratch, copies, loads, extra=(), flops=0, limit=56):
    dma = pltpu.SemaphoreType.DMA
    sems = [dma((copies,)), dma((copies,)), dma((loads,))] + [dma((n,)) for n in extra]
    moved = sum(a.size * a.dtype.itemsize for a, _ in ins)
    return pl.pallas_call(
        kernel,
        out_shape=[jax.ShapeDtypeStruct(shape, kind) for shape, kind, _ in outs],
        in_specs=[SMEM if near == "s" else VMEM if near else ANY for _, near in ins],
        out_specs=[VMEM if near else ANY for _, _, near in outs],
        scratch_shapes=[pltpu.VMEM(shape, kind) for shape, kind in scratch] + sems,
        compiler_params=pltpu.CompilerParams(
            collective_id=ident, has_side_effects=True, vmem_limit_bytes=limit * MIB
        ),
        cost_estimate=pl.CostEstimate(flops=flops, bytes_accessed=moved, transcendentals=0),
    )(*[a for a, _ in ins])


def local(
    dp_size,
    size,
    tokens,
    cotangent,
    mixer,
    merger,
    expand,
    shrink,
    attend_gain,
    attend_bias,
    feed_gain,
    feed_bias,
    width_router,
    head_router,
    lengths,
    head_choice,
    width_bucket,
):
    micro, rows, width = tokens.shape
    total = width_bucket.shape[1]
    every = micro * total
    half = rows // 2
    high = size // 2
    heads = merger.shape[0] // HD
    units = expand.shape[1]
    block = width // dp_size
    chips = dp_size // 2
    few = transfers(size)
    ringed = ring_copies(dp_size)

    vectors = jnp.stack([attend_gain, attend_bias, feed_gain, feed_bias])
    params = jnp.concatenate(
        [vectors, width_router.T, head_router.T, jnp.zeros((4, width), BF16)], axis=0
    ).astype(F32)
    rates = jnp.power(10000.0, -2.0 * jnp.arange(HD // 2, dtype=F32) / HD)
    rates = jnp.concatenate([rates, rates])[None]

    tables = (micro, total, LANES)
    first_rows, mix_weight, out_weight, mask, cosine, sine, row_info, own, seq_info, usage = call(
        functools.partial(first_norm_kernel, dp_size, size, heads, units),
        1,
        [
            (tokens, True),
            (params, True),
            (rates, True),
            (width_bucket, True),
            (lengths, "s"),
            (head_choice, "s"),
            (mixer, False),
            (merger, False),
        ],
        [
            ((every, width), BF16, False),
            ((dp_size,) + mixer.shape, BF16, False),
            ((dp_size,) + merger.shape, BF16, False),
            ((micro, total, total), F32, True),
            (tables, F32, True),
            (tables, F32, True),
            (tables, F32, True),
            ((micro, rows, LANES), F32, True),
            ((micro, 8, LANES), F32, True),
            ((8, LANES), F32, True),
        ],
        [
            ((every, width), BF16),
            ((total, LANES), jnp.int32),
            (tables, jnp.int32),
            (tables, F32),
        ],
        micro * few + 2 * ringed,
        micro + 2,
    )
    mix_weight = mix_weight.reshape(width, -1)

    lands = half * (2 * (high - 1) + high)
    stages = half * high
    wide_heads = heads * HD
    span = 3 * wide_heads
    buffers = [((micro, lands, width), BF16), ((micro, stages, width), BF16), ((micro, stages, width), BF16)]
    qkv, head_rows, attention, second_rows, width_share, branch_own, up_weight, down_early = call(
        functools.partial(attend_kernel, dp_size, size, heads),
        2,
        [
            (first_rows, False),
            (mix_weight, False),
            (out_weight, False),
            (mask, False),
            (cosine, True),
            (sine, True),
            (row_info, True),
            (own, True),
            (tokens, True),
            (cotangent, True),
            (params, True),
            (expand, False),
            (shrink, False),
        ],
        [
            ((micro, 3, total, wide_heads), BF16, False),
            ((every, wide_heads), BF16, False),
            ((micro, rows, width), F32, True),
            ((every, width), BF16, False),
            ((micro, rows, LANES), F32, True),
            ((micro, rows, width), BF16, True),
            ((dp_size,) + expand.shape, BF16, False),
            ((dp_size, units // 2, block), BF16, False),
        ],
        [
            ((every, width), BF16),
            ((width, span), BF16),
            ((wide_heads, width), BF16),
            ((micro, total, total), F32),
            ((micro, 3, total, wide_heads), BF16),
            ((every, wide_heads), BF16),
            ((every, width), BF16),
        ]
        + buffers
        + [((every, width), BF16)],
        2 * micro * few + 2 * ringed,
        2 + micro + dp_size + 2 + micro + 2,
        flops=2 * every * width * (span + wide_heads) + 8 * heads * micro * total * total * HD,
    )

    up_weight = up_weight.reshape(width, -1)
    unit_tile = 256
    rect, active, branch_rows, down_late, down_mine, down_twin = call(
        functools.partial(widen_kernel, dp_size, size, heads),
        3,
        [
            (second_rows, False),
            (up_weight, False),
            (branch_own, False),
            (row_info, True),
            (shrink, False),
        ],
        [
            ((every, units), BF16, False),
            ((every, units), BF16, False),
            ((every, width), BF16, False),
            ((dp_size, units // 2, block), BF16, False),
            ((chips, units, block), BF16, False),
            ((chips, units, block), BF16, False),
        ],
        [
            ((every, width), BF16),
            ((width, units), BF16),
            ((every, width), BF16),
            ((every, units), BF16),
            ((every, units), BF16),
            ((2, 2, chips, unit_tile, block), BF16),
        ],
        micro * few + ringed,
        2 + 6 * micro,
        (4, 1),
        flops=4 * every * width * units,
    )

    block_output, up_mine, up_twin, hidden_back, back_own, stats_two, gate_part, down_sum = call(
        functools.partial(narrow_kernel, dp_size, size),
        4,
        [
            (down_early, False),
            (down_late, False),
            (up_weight, False),
            (active, False),
            (rect, False),
            (branch_rows, False),
            (second_rows, False),
            (tokens, True),
            (cotangent, True),
            (attention, True),
            (width_share, True),
            (own, True),
            (params, True),
            (down_mine, False),
            (down_twin, False),
        ],
        [
            ((micro, rows, width), BF16, True),
            ((chips, block, units), BF16, False),
            ((chips, block, units), BF16, False),
            ((micro, rows, width), F32, True),
            ((micro, rows, width), BF16, True),
            ((8, width), F32, True),
            ((8, LANES), F32, True),
            ((units, block), F32, False),
        ],
        [
            ((units, width), BF16),
            ((width, units), BF16),
            ((every, units), BF16),
            ((total, units), BF16),
            ((every, width), BF16),
            ((every, width), BF16),
            ((2 * micro, lands, width), BF16),
            ((2 * micro, stages, width), BF16),
            ((2 * micro, stages, width), BF16),
            ((micro, rows, width), F32),
            ((micro, rows, LANES), F32),
            ((2, block, units), BF16),
        ]
        + sum_scratch(chips, units, block),
        2 * micro * few + chips - 1,
        2 * dp_size + 4 * micro + 1 + 2 * chips,
        (2, 1, 2),
        flops=8 * every * width * units,
        limit=63,
    )

    out_tile = min(256, wide_heads)
    mixed_back, out_mine, out_twin, mix_mine, mix_twin, gate_total, up_sum = call(
        functools.partial(attend_back_kernel, dp_size, size, heads),
        5,
        [
            (back_own, False),
            (gate_part, True),
            (out_weight, False),
            (qkv, False),
            (head_rows, False),
            (first_rows, False),
            (mask, False),
            (cosine, True),
            (sine, True),
            (row_info, True),
            (up_mine, False),
            (up_twin, False),
        ],
        [
            ((every, span), BF16, False),
            ((chips, wide_heads, block), BF16, False),
            ((chips, wide_heads, block), BF16, False),
            ((chips, block, span), BF16, False),
            ((chips, block, span), BF16, False),
            ((8, LANES), F32, True),
            ((block, units), F32, False),
        ],
        [
            ((every, width), BF16),
            ((wide_heads, width), BF16),
            ((micro, 3, total, wide_heads), BF16),
            ((every, wide_heads), BF16),
            ((every, width), BF16),
            ((micro, total, total), F32),
            ((total, wide_heads), BF16),
            ((every, span), BF16),
            ((total, total), BF16),
            ((total, total), BF16),
            ((2, 2, chips, out_tile, block), BF16),
            ((2, block, span), BF16),
            ((size, 8, LANES), F32),
        ]
        + sum_scratch(chips, block, units),
        micro * few + size - 1 + chips - 1,
        2 * micro + dp_size + 5 + 2 * chips,
        (4, 1, 2, 1, 2),
        flops=2 * every * width * (2 * wide_heads + span) + 20 * heads * micro * total * total * HD,
    )

    tokens_gradient, mix_sum, out_sum, stats = call(
        functools.partial(first_back_kernel, dp_size, size, micro),
        6,
        [
            (mixed_back, False),
            (mix_weight, False),
            (mix_mine, False),
            (mix_twin, False),
            (out_mine, False),
            (out_twin, False),
            (tokens, True),
            (hidden_back, True),
            (own, True),
            (seq_info, True),
            (gate_total, True),
            (params, True),
            (stats_two, True),
            (usage, True),
        ],
        [
            ((micro, rows, width), F32, True),
            ((block, span), F32, False),
            ((wide_heads, block), F32, False),
            ((STATS_ROWS, width), F32, True),
        ],
        [((every, span), BF16), ((width, span), BF16), ((every, width), BF16)]
        + buffers
        + sum_scratch(chips, block, span)
        + sum_scratch(chips, wide_heads, block)
        + [
            ((STATS_ROWS, width), F32),
            ((2, STATS_ROWS, width // size), F32),
            ((size, STATS_ROWS, width // size), F32),
            ((dp_size, STATS_ROWS, width // size), F32),
            ((size, STATS_ROWS, width // size), F32),
        ],
        micro * few + 2 * (chips - 1) + 2 * (size - 1) + dp_size - 1,
        1 + micro + 4 * chips,
        (2, 2),
        flops=2 * every * width * span,
    )
    return (
        block_output,
        tokens_gradient,
        mix_sum,
        out_sum,
        up_sum,
        down_sum,
        stats[STATS_ONE],
        stats[STATS_ONE + 1],
        stats[0],
        stats[1],
        stats[2 : 2 + NB].T,
        stats[STATS_ONE + 2 : STATS_ONE + 2 + NHC].T,
        stats[STATS_USE, :NB],
        stats[STATS_USE, CHOICE : CHOICE + NHC],
    )


def solution(mesh):
    def run(*args):
        return local(mesh.shape["dp"], mesh.shape["tensor"], *args)

    rows = P(None, ("dp", "tensor"), None)
    tall, wide = P("dp", "tensor"), P("tensor", "dp")
    weights = (tall, wide, tall, wide)
    return jax.shard_map(
        run,
        mesh=mesh,
        in_specs=(rows, rows) + weights + (P(),) * 6 + (P(None, "dp"),) * 3,
        out_specs=(rows, rows) + weights + (P(),) * 8,
        check_vma=False,
    )
```

```python
import functools

import jax
import jax.numpy as jnp
from jax import lax
from jax.experimental import pallas as pl
from jax.experimental.pallas import tpu as pltpu
from jax.sharding import PartitionSpec as P

H = 16
HD = 128
FF = 8192
NB = 4
NHC = 4

EPSILON = 1e-05
HIGHEST = lax.Precision.HIGHEST
MASKED = -1e30
BF16 = jnp.bfloat16
F32 = jnp.float32
MESH = pl.DeviceIdType.MESH
MIB = 1024 * 1024
LANES = 128
STEP = 16

GATE = 4
LIVE = 5
SEQ = 8
CHOICE = 16

PICKED = 4
DIVISOR = 5
CHOSEN = 6

ATTEND = 0
FEED = 2
WIDTH_ROUTER = 4
HEAD_ROUTER = 8


def dot(left, right):
    return jnp.dot(left, right, preferred_element_type=F32)


def dot_nt(left, right):
    return lax.dot_general(left, right, (((1,), (1,)), ((), ())), preferred_element_type=F32)


def dot_tn(left, right):
    return lax.dot_general(left, right, (((0,), (0,)), ((), ())), preferred_element_type=F32)


def at(start, size=STEP):
    return pl.ds(pl.multiple_of(start, STEP), size)


class Copies:
    def __init__(self, send_sems, recv_sems):
        self.send_sems, self.recv_sems, self.used = send_sems, recv_sems, 0

    def start(self, src, dst, axis, to):
        made = pltpu.make_async_remote_copy(
            src_ref=src,
            dst_ref=dst,
            send_sem=self.send_sems.at[self.used],
            recv_sem=self.recv_sems.at[self.used],
            device_id={axis: to},
            device_id_type=MESH,
        )
        self.used += 1
        made.start()
        return made


def greet(*peers):
    barrier = pltpu.get_barrier_semaphore()
    for axis, to in peers:
        pl.semaphore_signal(barrier, inc=1, device_id={axis: to}, device_id_type=MESH)
    pl.semaphore_wait(barrier, len(peers))


class Links:
    def __init__(self, size, rows, copies):
        me = lax.axis_index("tensor")
        hi, lo = me // 2, me % 2
        self.me, self.size, self.high, self.half = me, size, size // 2, rows // 2
        self.near = hi * 2 + (1 - lo)
        self.ahead = [lax.rem(hi + s, self.high) * 2 + lo for s in range(self.high)]
        self.behind = [
            lax.rem(hi + self.high - s, self.high) * 2 + lo for s in range(self.high)
        ]
        self.second = self.half * size
        self.copies = copies
        steps = range(self.high)
        grid = [[lax.rem(hi + s, self.high) * 2 + (lo + l) % 2 for l in range(2)] for s in steps]
        self.first_ranks = [grid[s][l] for s in steps for l in range(2)]
        self.second_ranks = [grid[s][l] for l in range(2) for s in steps]
        self.peers = [("tensor", to) for to in [self.near] + self.ahead[1:]]

    def copy(self, src, dst, to):
        return self.copies.start(src, dst, "tensor", to)


class Column:
    def __init__(self, size, copies):
        self.me, self.chips, self.copies = lax.axis_index("dp"), size // 2, copies
        self.chip, self.core = self.me // 2, self.me % 2
        self.twin = self.chip * 2 + 1 - self.core
        self.right = self.block(1)
        self.left = self.block(-1)
        self.ring = [("dp", self.left)]
        self.pair = [("dp", self.twin)]

    def chip_at(self, step):
        return lax.rem(self.chip + self.chips + step, self.chips)

    def block(self, step):
        return self.chip_at(step) * 2 + self.core

    def copy(self, src, dst, to):
        return self.copies.start(src, dst, "dp", to)


class WeightRing:
    def __init__(self, column, loads, own, slot):
        self.column, self.loads, self.own, self.slot = column, loads, own, slot

    def start(self):
        k = self.column
        here = self.slot(k.me)
        self.hops = [k.copy(self.own, here, k.right)]
        self.twins = [k.copy(self.own, here, k.twin)]
        self.local = self.loads.copy(self.own, here)

    def advance(self):
        k = self.column
        step = len(self.twins)
        self.hops[step - 1].wait_recv()
        here = self.slot(k.block(-step))
        if step < k.chips - 1:
            self.hops.append(k.copy(here, here, k.right))
        self.twins.append(k.copy(here, here, k.twin))

    def finish(self):
        while len(self.twins) < self.column.chips:
            self.advance()
        for made in self.twins:
            made.wait()
        for made in self.hops:
            made.wait_send()
        self.local.wait()


def ring_copies(size):
    return size // 2 * 2 - 1


class SumRing:
    def __init__(self, column, loads, mine, twin, target, own, other, landing, staged, tile, tile_sems):
        self.column, self.loads = column, loads
        self.mine, self.twin, self.target = mine, twin, target
        self.own, self.other, self.landing, self.staged = own, other, landing, staged
        self.tile, self.tile_sems = tile, tile_sems
        self.sent = 0
        self.rows = sum_rows(own.shape[1])

    def load(self):
        block = self.column.chip_at(-1 - self.sent)
        self.loading = [
            self.loads.copy(self.mine.at[block], self.own),
            self.loads.copy(self.twin.at[block], self.other),
        ]

    def send(self, landed, more=True):
        k, rows = self.column, self.rows

        def body(i, _):
            here = pl.ds(pl.multiple_of(i * rows, rows), rows)
            value = self.own[here, :].astype(F32) + self.other[here, :].astype(F32)
            if landed is not None:
                value = value + self.landing[landed, here, :].astype(F32)
            self.staged[here, :] = value.astype(BF16)
            return 0

        lax.fori_loop(0, self.own.shape[0] // rows, body, 0)
        self.hop = k.copy(self.staged, self.landing.at[self.sent], k.right)
        self.sent += 1
        if more:
            self.load()

    def start(self, more=True):
        wait_all(self.loading)
        self.send(None, more)

    def prepare(self, landed):
        self.sent = 1
        self.load()
        self.loading.append(self.loads.copy(landed.at[0], self.landing.at[0]))

    def resume(self):
        wait_all(self.loading)
        self.send(0)

    def advance(self):
        self.hop.wait()
        wait_all(self.loading)
        self.send(self.sent - 1)

    def finish(self):
        k, rows = self.column, self.rows
        while self.sent < k.chips - 1:
            self.advance()
        self.hop.wait()
        wait_all(self.loading)
        landed = k.chips - 2
        slots = self.tile.shape[0]

        def body(i, _):
            here = pl.ds(pl.multiple_of(i * rows, rows), rows)
            slot = lax.rem(i, slots)
            copy = pltpu.make_async_copy(
                self.tile.at[slot], self.target.at[here], self.tile_sems.at[slot]
            )

            @pl.when(i >= slots)
            def _():
                copy.wait()

            value = self.own[here, :].astype(F32) + self.other[here, :].astype(F32)
            self.tile[slot] = value + self.landing[landed, here, :].astype(F32)
            copy.start()
            return 0

        count = self.own.shape[0] // rows
        lax.fori_loop(0, count, body, 0)
        for i in range(max(count - slots, 0), count):
            here = pl.ds(i * rows, rows)
            slot = i % slots
            pltpu.make_async_copy(
                self.tile.at[slot], self.target.at[here], self.tile_sems.at[slot]
            ).wait()


SUM_TILES = 4


def sum_rows(width):
    return 128 if width <= 256 else 16


def sum_scratch(chips, rows, width):
    return [
        ((rows, width), BF16),
        ((rows, width), BF16),
        ((chips - 1, rows, width), BF16),
        ((rows, width), BF16),
        ((SUM_TILES, sum_rows(width), width), F32),
    ]


def transfers(size):
    return 2 * (size // 2)


class Gather:
    def __init__(self, links, buf, base):
        self.links, self.buf, self.base = links, buf, base

    def rows(self, start, count):
        return self.buf.at[pl.ds(self.base + start, count)]

    def start(self):
        k, half, second = self.links, self.links.half, self.links.second
        self.first_near = k.copy(self.rows(0, half), self.rows(half, half), k.near)
        self.second_far = [
            k.copy(self.rows(second, half), self.rows(second + s * half, half), k.behind[s])
            for s in range(1, k.high)
        ]

    def middle(self):
        k, half, second = self.links, self.links.half, self.links.second
        self.first_near.wait_recv()
        self.first_far = [
            k.copy(self.rows(0, 2 * half), self.rows(2 * half * s, 2 * half), k.behind[s])
            for s in range(1, k.high)
        ]
        for made in self.second_far:
            made.wait_recv()
        block = k.high * half
        self.second_near = k.copy(self.rows(second, block), self.rows(second + block, block), k.near)

    def finish(self):
        for made in self.first_far + [self.second_near]:
            made.wait_recv()
        for made in [self.first_near, self.second_near] + self.first_far + self.second_far:
            made.wait_send()


class Scatter:
    def __init__(self, links, part, base, landing, staged, last, total):
        self.links, self.part, self.base = links, part, base
        self.landing, self.staged, self.last, self.total = landing, staged, last, total

    def start(self):
        k, half = self.links, self.links.half
        block = k.high * half
        self.first_far = [
            k.copy(
                self.part.at[pl.ds(self.base + 2 * half * s, 2 * half)],
                self.landing.at[pl.ds(2 * half * (s - 1), 2 * half)],
                k.ahead[s],
            )
            for s in range(1, k.high)
        ]
        self.second_near = k.copy(
            self.part.at[pl.ds(self.base + k.second + block, block)],
            self.landing.at[pl.ds(2 * half * (k.high - 1), block)],
            k.near,
        )

    def middle(self):
        k, half, base = self.links, self.links.half, self.base
        steps = half // STEP
        for made in self.first_far:
            made.wait_recv()

        def first(i, _):
            for where in range(2):
                row = where * half + i * STEP
                value = self.part[at(base + row), :].astype(F32)
                for s in range(1, k.high):
                    value = value + self.landing[at(2 * half * (s - 1) + row), :].astype(F32)
                if where == 0:
                    self.total[at(i * STEP), :] = value
                else:
                    self.staged[at(i * STEP), :] = value.astype(BF16)
            return 0

        lax.fori_loop(0, steps, first, 0)
        self.first_near = k.copy(
            self.staged.at[pl.ds(0, half)], self.last.at[pl.ds(0, half)], k.near
        )
        self.second_near.wait_recv()
        landed = 2 * half * (k.high - 1)

        def second(i, _):
            for s in range(k.high):
                row = s * half + i * STEP
                value = self.part[at(base + k.second + row), :].astype(F32)
                value = value + self.landing[at(landed + row), :].astype(F32)
                if s == 0:
                    self.total[at(half + i * STEP), :] = value
                else:
                    self.staged[at(row), :] = value.astype(BF16)
            return 0

        lax.fori_loop(0, steps, second, 0)
        self.second_far = [
            k.copy(
                self.staged.at[pl.ds(half * s, half)], self.last.at[pl.ds(half * s, half)], k.ahead[s]
            )
            for s in range(1, k.high)
        ]
        for made in self.first_far + [self.second_near]:
            made.wait_send()

    def finish(self):
        for made in [self.first_near] + self.second_far:
            made.wait_recv()
            made.wait_send()

    def chunk(self, where, i):
        k, half = self.links, self.links.half
        value = self.total[at(where * half + i * STEP), :]
        if where == 0:
            return value + self.last[at(i * STEP), :].astype(F32)
        for s in range(1, k.high):
            value = value + self.last[at(half * s + i * STEP), :].astype(F32)
        return value


def over_rows(half, body):
    for where in range(2):

        def inner(i, _, where=where):
            body(where, i, where * half + i * STEP)
            return 0

        lax.fori_loop(0, half // STEP, inner, 0)


class Loads:
    def __init__(self, sems):
        self.sems, self.used = sems, 0

    def copy(self, src, dst):
        made = pltpu.make_async_copy(src, dst, self.sems.at[self.used])
        self.used += 1
        made.start()
        return made


def wait_all(*groups):
    for group in groups:
        for made in group if isinstance(group, list) else [group]:
            made.wait()


def columns_in(loads, blocks, flat):
    count, _, width = blocks.shape
    return [loads.copy(blocks.at[j], flat.at[:, pl.ds(j * width, width)]) for j in range(count)]


def halves_out(column, count, make, tile, mine, twin, sems, twin_sem):
    wide = tile.shape[3]

    def outs(c, slot):
        here = pl.ds(pl.multiple_of(c * wide, wide), wide)
        local = pltpu.make_async_copy(tile.at[slot, 0], mine.at[:, here, :], sems.at[slot])
        away = pltpu.make_async_remote_copy(
            src_ref=tile.at[slot, 1],
            dst_ref=twin.at[:, here, :],
            send_sem=sems.at[2 + slot],
            recv_sem=twin_sem.at[0],
            device_id={"dp": column.twin},
            device_id_type=MESH,
        )
        return local, away

    def body(c, _):
        slot = lax.rem(c, 2)
        local, away = outs(c, slot)

        @pl.when(c >= 2)
        def _():
            local.wait()
            away.wait_send()

        def put(block, value):
            tile[slot, lax.rem(block + column.core, 2), block // 2] = value

        make(c, put)
        local.start()
        away.start()
        return 0

    lax.fori_loop(0, count, body, 0)
    for c in range(max(count - 2, 0), count):
        local, away = outs(c, c % 2)
        local.wait()
        away.wait_send()
    all_landed(column, twin, sems, twin_sem)


def blocks_out(column, make, tile, mine, twin, sems, twin_sems, ring):
    def local_copy(i):
        chip = column.chip_at(-1 - i)
        return pltpu.make_async_copy(tile.at[0], mine.at[chip], sems.at[0])

    def away_copy(i):
        return pltpu.make_async_remote_copy(
            src_ref=tile.at[1],
            dst_ref=twin.at[column.chip_at(-1 - i)],
            send_sem=sems.at[1],
            recv_sem=twin_sems.at[i],
            device_id={"dp": column.twin},
            device_id_type=MESH,
        )

    def body(i, _):
        chip, local, away = column.chip_at(-1 - i), local_copy(i), away_copy(i)

        @pl.when(i > 0)
        def _():
            away.wait_send()

        make(2 * chip + 1 - column.core, tile.at[1])
        away.start()

        @pl.when(i > 1)
        def _():
            local.wait()

        make(2 * chip + column.core, tile.at[0])
        local.start()
        return 0

    lax.fori_loop(0, 1, body, 0)
    local_copy(0).wait()
    away_copy(0).wait_recv()
    ring()
    lax.fori_loop(1, column.chips, body, 0)
    for i in range(1, column.chips):
        away_copy(i).wait_recv()
    local_copy(column.chips - 1).wait()
    away_copy(column.chips - 1).wait_send()


def all_landed(column, twin, sems, twin_sem):
    pltpu.make_async_remote_copy(
        src_ref=twin,
        dst_ref=twin,
        send_sem=sems.at[0],
        recv_sem=twin_sem.at[0],
        device_id={"dp": column.twin},
        device_id_type=MESH,
    ).wait_recv()


def normalized(value):
    centred = value - jnp.mean(value, axis=-1, keepdims=True)
    inverse = lax.rsqrt(jnp.mean(centred * centred, axis=-1, keepdims=True) + EPSILON)
    return centred * inverse, inverse


def norm_back(back, normed, inverse, gain):
    scaled = back * gain
    inner = jnp.mean(scaled, axis=-1, keepdims=True)
    along = jnp.mean(scaled * normed, axis=-1, keepdims=True)
    return inverse * (scaled - inner - normed * along)


def softmax_lanes(logits, lanes):
    logits = jnp.where(lanes, logits, MASKED)
    powers = jnp.exp(logits - jnp.max(logits, axis=-1, keepdims=True))
    return jnp.where(lanes, powers / jnp.sum(powers, axis=-1, keepdims=True), 0.0)


def turned(value, cosine, sine):
    return value * cosine + pltpu.roll(value, HD // 2, 1) * sine


def first_norm_kernel(
    dp_size,
    size,
    heads,
    units,
    tokens,
    params,
    rates,
    bucket,
    lengths,
    choices,
    mixer,
    merger,
    rows_out,
    mix_out,
    out_out,
    mask,
    cosine,
    sine,
    row_info,
    own,
    seq_info,
    usage,
    buf,
    slot_col,
    member_col,
    bucket_col,
    send,
    recv,
    load_sems,
):
    micro, rows, _ = tokens.shape
    count = lengths.shape[1]
    copies, loads = Copies(send, recv), Loads(load_sems)
    links, column = Links(size, rows, copies), Column(dp_size, copies)
    total = rows * size
    greet(*links.peers, *column.ring, *column.pair)
    rings = [
        WeightRing(column, loads, merger, lambda i: out_out.at[i]),
        WeightRing(column, loads, mixer, lambda i: mix_out.at[i]),
    ]
    for ring in rings:
        ring.start()
    gathers = []
    for m in range(micro):

        def body(where, i, row, m=m):
            value = tokens[m, at(row), :].astype(F32)
            low = normalized(value)[0] * params[ATTEND : ATTEND + 1, :]
            low = (low + params[ATTEND + 1 : ATTEND + 2, :]).astype(BF16)
            buf[at(m * total + where * links.second + i * STEP), :] = low

        over_rows(links.half, body)
        gathers.append(Gather(links, buf, m * total))
        gathers[m].start()

    half = links.half
    starts = [r * rows for r in links.first_ranks] + [r * rows + half for r in links.second_ranks]

    def slots(shape, dimension):
        index = lax.broadcasted_iota(jnp.int32, shape, dimension)
        offset = jnp.full(shape, starts[0], jnp.int32)
        for k in range(1, len(starts)):
            offset = jnp.where(index >= k * half, starts[k] - k * half, offset)
        return index + offset

    def ends(m):
        found, end = [], 0
        for s in range(count):
            end = end + lengths[m, s]
            found.append(end)
        return found

    def members(m, slot):
        member = jnp.zeros(slot.shape, jnp.int32)
        begin = jnp.zeros(slot.shape, jnp.int32)
        for end in ends(m):
            member = member + jnp.where(slot >= end, 1, 0)
            begin = jnp.where(slot >= end, end, begin)
        return member, slot - begin

    def by_member(member, values, other):
        value = jnp.full(member.shape, other)
        for s in range(count):
            value = jnp.where(member == s, values[s], value)
        return value

    chunk = min(128, total)
    lane = lax.broadcasted_iota(jnp.int32, (chunk, LANES), 1)
    slot_row = slots((8, total), 1)
    slot_col[...] = slots((total, LANES), 0)
    member_rows = [members(m, slot_row)[0] for m in range(micro)]
    for m in range(micro):

        def table(c, _, m=m):
            here = pl.ds(pl.multiple_of(c * chunk, chunk), chunk)
            slot = slot_col[here, :]
            member, place = members(m, slot)
            member_col[m, here, :] = member
            seen = (member[:, :1] == member_rows[m][:1, :]) & (slot[:, :1] >= slot_row[:1, :])
            mask[m, here, :] = jnp.where(seen, 0.0, MASKED)
            angle = place.astype(F32) * rates[...]
            turn = jnp.sin(angle)
            cosine[m, here, :] = jnp.cos(angle)
            sine[m, here, :] = jnp.where(lane < HD // 2, -turn, turn)
            natural = lax.broadcasted_iota(jnp.int32, (chunk, total), 1)
            picked = jnp.where(slot[:, :1] == natural, bucket[m : m + 1, :].astype(F32), 0.0)
            bucket_here = jnp.sum(picked, axis=-1, keepdims=True)
            bucket_col[m, here, :] = jnp.broadcast_to(bucket_here, (chunk, LANES))
            used = by_member(member, [H // NHC * (choices[m, s] + 1) for s in range(count)], 0)
            head_on = jnp.where(links.me * heads + lane < used, 1.0, 0.0)
            first_unit = jnp.full(lane.shape, links.me * units, jnp.int32).astype(F32)
            unit_on = jnp.where(first_unit < FF // NB * (bucket_here + 1.0), 1.0, 0.0)
            row_info[m, here, :] = jnp.where(
                lane < heads, head_on, jnp.where(lane == heads, unit_on, 0.0)
            )
            return 0

        lax.fori_loop(0, total // chunk, table, 0)
        if m == 0:
            rings[0].advance()
    for g in gathers:
        g.middle()
    rings[1].advance()
    if column.chips > 2:
        rings[0].advance()
    outs = []
    usage[...] = jnp.zeros_like(usage)
    few = lax.broadcasted_iota(jnp.int32, (8, LANES), 1)
    which = lax.broadcasted_iota(jnp.int32, (8, LANES), 0)
    lane_own = lax.broadcasted_iota(jnp.int32, (half, LANES), 1)
    for m, g in enumerate(gathers):
        g.finish()
        here = pl.ds(m * total, total)
        outs.append(loads.copy(buf.at[here], rows_out.at[here]))
        sequence = lax.broadcasted_iota(jnp.int32, (8, total), 0)
        hot = jnp.where(member_rows[m] == sequence, 1.0, 0.0).astype(BF16)
        divisor = jnp.maximum(by_member(which, [lengths[m, s] for s in range(count)], 0), 1)
        divisor = divisor.astype(F32)
        chosen = by_member(which, [choices[m, s] for s in range(count)], 0)
        means = dot(hot, buf[here, :]) / divisor[:, :1]
        logits = jnp.full((8, LANES), MASKED)
        for c in range(NHC):
            router = params[HEAD_ROUTER + c : HEAD_ROUTER + c + 1, :]
            logit = jnp.sum(means * router, axis=-1, keepdims=True)
            logits = jnp.where(few == c, logit, logits)
        share = softmax_lanes(logits, few < NHC)
        picked = jnp.sum(jnp.where(few == chosen, share, 0.0), axis=-1, keepdims=True)
        table = jnp.where(few == PICKED, picked, share)
        table = jnp.where(few == DIVISOR, divisor, table)
        seq_info[m] = jnp.where(few == CHOSEN, chosen.astype(F32), table)
        for where in range(2):
            source = pl.ds(where * links.second, half)
            member = member_col[m, source, :]
            gate = by_member(member, [NHC * picked[s : s + 1, :] for s in range(count)], 0.0)
            choice = by_member(member, [choices[m, s] for s in range(count)], -NHC)
            live = jnp.where(member < count, 1.0, 0.0)
            kind = bucket_col[m, source, :].astype(jnp.int32)
            hot = (lane_own == kind) | (lane_own == CHOICE + choice)
            hot = hot | ((lane_own == SEQ + member) & (member < count))
            value = jnp.where(hot & (choice >= -NHC), 1.0, 0.0)
            value = jnp.where(lane_own == GATE, gate, value)
            value = jnp.where(lane_own == LIVE, live, value)
            own[m, pl.ds(where * half, half), :] = value
            usage[0:1, :] += jnp.sum(value * live, axis=0, keepdims=True)
    for step in range(column.chips - 3):
        for ring in reversed(rings):
            ring.advance()
    for ring in rings:
        ring.finish()
    wait_all(outs)


def attend_kernel(
    dp_size,
    size,
    heads,
    rows_hbm,
    mix_hbm,
    out_hbm,
    mask_hbm,
    cosine,
    sine,
    row_info,
    own,
    tokens,
    cotangent,
    params,
    expand,
    shrink,
    qkv_out,
    heads_out,
    attention_out,
    second_out,
    share_out,
    branch_out,
    up_out,
    down_out,
    rows_buf,
    mix,
    out,
    mask,
    qkv,
    head_rows,
    part,
    landing,
    staged,
    last,
    second_buf,
    send,
    recv,
    load_sems,
):
    micro, rows, width = tokens.shape
    total = rows * size
    copies, loads = Copies(send, recv), Loads(load_sems)
    links, column = Links(size, rows, copies), Column(dp_size, copies)
    half = links.half
    mix_copy = loads.copy(mix_hbm, mix)
    row_copies = [
        loads.copy(rows_hbm.at[pl.ds(m * total, total)], rows_buf.at[pl.ds(m * total, total)])
        for m in range(micro)
    ]
    mask_copy = loads.copy(mask_hbm, mask)
    out_copies = columns_in(loads, out_hbm, out)
    greet(*links.peers, *column.ring, *column.pair)
    early = shrink.shape[0] // 4
    rings = [
        WeightRing(column, loads, shrink.at[pl.ds(0, early)], lambda i: down_out.at[i]),
        WeightRing(column, loads, expand, lambda i: up_out.at[i]),
    ]
    for ring in rings:
        ring.start()
    mix_copy.wait()
    scale = HD ** (-0.5)
    span = 3 * HD
    chunk = min(128, total)
    tile = min(512, width)
    saves = []

    def project(m):
        base = m * total
        cos, sin = cosine[m], sine[m]

        def head(h, _):
            mixed = dot(
                rows_buf[pl.ds(base, total), :], mix[:, pl.ds(pl.multiple_of(h * span, HD), span)]
            )
            here = pl.ds(pl.multiple_of(h * HD, HD), HD)
            qkv[m, 0, :, here] = turned(mixed[:, :HD], cos, sin).astype(BF16)
            qkv[m, 1, :, here] = turned(mixed[:, HD : 2 * HD], cos, sin).astype(BF16)
            qkv[m, 2, :, here] = mixed[:, 2 * HD :].astype(BF16)
            return 0

        lax.fori_loop(0, heads, head, 0)

    def attend(m):
        base = m * total

        def some(c, _):
            rows_here = pl.ds(pl.multiple_of(c * chunk, chunk), chunk)
            bias_here = mask[m, rows_here, :]
            info = row_info[m, rows_here, :]
            for h in range(heads):
                here = pl.ds(h * HD, HD)
                scores = dot_nt(qkv[m, 0, rows_here, here], qkv[m, 1, :, here]) * scale + bias_here
                peak = jnp.max(scores, axis=-1, keepdims=True)
                powers = jnp.exp(scores - peak)
                share = powers / jnp.sum(powers, axis=-1, keepdims=True)
                value = dot(share.astype(BF16), qkv[m, 2, :, here]).astype(BF16)
                value = value.astype(F32) * info[:, h : h + 1]
                head_rows[pl.ds(pl.multiple_of(base + c * chunk, chunk), chunk), here] = value.astype(
                    BF16
                )
            return 0

        lax.fori_loop(0, total // chunk, some, 0)

    def merge(m):
        base = m * total

        def body(j, _):
            here = pl.ds(pl.multiple_of(j * tile, tile), tile)
            part[pl.ds(base, total), here] = dot(
                head_rows[pl.ds(base, total), :], out[:, here]
            ).astype(BF16)
            return 0

        lax.fori_loop(0, width // tile, body, 0)

    scatters = [
        Scatter(
            links,
            part,
            m * total,
            landing.at[m],
            staged.at[m],
            last.at[m],
            attention_out.at[m],
        )
        for m in range(micro)
    ]
    gathers = [Gather(links, second_buf, m * total) for m in range(micro)]

    def second_norm(m):
        scatter = scatters[m]

        def body(where, i, row):
            attended = scatter.chunk(where, i)
            info = own[m, at(row), :]
            hidden = tokens[m, at(row), :].astype(F32) + info[:, GATE : GATE + 1] * attended
            attention_out[m, at(row), :] = attended
            low = normalized(hidden)[0] * params[FEED : FEED + 1, :]
            low = (low + params[FEED + 1 : FEED + 2, :]).astype(BF16)
            second_buf[at(m * total + where * links.second + i * STEP), :] = low
            low = low.astype(F32)
            lane = lax.broadcasted_iota(jnp.int32, (STEP, LANES), 1)
            logits = jnp.full((STEP, LANES), MASKED)
            for b in range(NB):
                router = params[WIDTH_ROUTER + b : WIDTH_ROUTER + b + 1, :]
                logits = jnp.where(lane == b, jnp.sum(low * router, axis=-1, keepdims=True), logits)
            share = softmax_lanes(logits, lane < NB)
            share_out[m, at(row), :] = share
            gate = NB * jnp.sum(share * info, axis=-1, keepdims=True)
            outer = cotangent[m, at(row), :].astype(F32) * info[:, LIVE : LIVE + 1]
            branch_out[m, at(row), :] = (gate * outer).astype(BF16)

        over_rows(half, body)

    for m in range(micro):
        row_copies[m].wait()
        project(m)
        if m == 0:
            mask_copy.wait()
        attend(m)
        if m == 0:
            wait_all(out_copies)
            rings[0].advance()
        else:
            scatters[m - 1].middle()
        merge(m)
        scatters[m].start()
    rings[1].advance()
    for m in range(micro):
        scatters[m].finish()
        second_norm(m)
        gathers[m].start()
        if m + 1 < micro:
            scatters[m + 1].middle()
            gathers[m].middle()
            if column.chips > 2:
                for ring in rings:
                    ring.advance()
    saves.append(loads.copy(qkv, qkv_out))
    saves.append(loads.copy(head_rows, heads_out))
    gathers[micro - 1].middle()
    for m in range(micro):
        gathers[m].finish()
        here = pl.ds(m * total, total)
        saves.append(loads.copy(second_buf.at[here], second_out.at[here]))
    for ring in rings:
        ring.finish()
    wait_all(saves)


def widen_kernel(
    dp_size,
    size,
    unit_lane,
    second_hbm,
    up_hbm,
    branch,
    row_info,
    shrink,
    rect_out,
    active_out,
    branch_out,
    down_out,
    mine_out,
    twin_out,
    second_rows,
    up,
    branch_buf,
    rect,
    active,
    tile,
    send,
    recv,
    load_sems,
    tile_sems,
    twin_sem,
):
    micro, rows, width = branch.shape
    total = rows * size
    units = up.shape[1]
    copies, loads = Copies(send, recv), Loads(load_sems)
    links, column = Links(size, rows, copies), Column(dp_size, copies)
    up_copy = loads.copy(up_hbm, up)
    second_copies = [
        loads.copy(second_hbm.at[pl.ds(m * total, total)], second_rows.at[pl.ds(m * total, total)])
        for m in range(micro)
    ]
    half = links.half
    own_copies = []
    for m in range(micro):
        for where in range(2):
            own_copies.append(
                loads.copy(
                    branch.at[m, pl.ds(where * half, half)],
                    branch_buf.at[pl.ds(m * total + where * links.second, half)],
                )
            )
    greet(*links.peers, *column.ring, *column.pair)
    late = down_out.shape[1]
    rest = shrink.at[pl.ds(shrink.shape[0] - late, late)]
    ring = WeightRing(column, loads, rest, lambda i: down_out.at[i])
    ring.start()
    wait_all(own_copies)
    gathers = [Gather(links, branch_buf, m * total) for m in range(micro)]
    for g in gathers:
        g.start()
    up_copy.wait()
    step = min(512, units)
    saves = []
    for m in range(micro):
        second_copies[m].wait()

        def body(j, _, m=m):
            here = pl.ds(pl.multiple_of(j * step, step), step)
            before = dot(second_rows[pl.ds(m * total, total), :], up[:, here])
            kept = jnp.maximum(before, 0.0) * row_info[m, :, unit_lane : unit_lane + 1]
            rect[pl.ds(m * total, total), here] = kept.astype(BF16)
            active[pl.ds(m * total, total), here] = (kept * kept).astype(BF16)
            return 0

        lax.fori_loop(0, units // step, body, 0)
        gathers[m].middle()
        here = pl.ds(m * total, total)
        saves.append(loads.copy(rect.at[here], rect_out.at[here]))
        saves.append(loads.copy(active.at[here], active_out.at[here]))
    ring.advance()
    for m, g in enumerate(gathers):
        g.finish()
        here = pl.ds(m * total, total)
        saves.append(loads.copy(branch_buf.at[here], branch_out.at[here]))
        if m == 0 and column.chips > 2:
            ring.advance()
    block, wide = mine_out.shape[2], tile.shape[3]

    def make(c, put):
        value = dot_tn(active[:, pl.ds(pl.multiple_of(c * wide, wide), wide)], branch_buf[...])
        for j in range(dp_size):
            put(j, value[:, j * block : (j + 1) * block].astype(BF16))

    halves_out(column, units // wide, make, tile, mine_out, twin_out, tile_sems, twin_sem)
    ring.finish()
    wait_all(saves)


def narrow_kernel(
    dp_size,
    size,
    down_early,
    down_late,
    up_hbm,
    active_hbm,
    rect_hbm,
    branch_hbm,
    second_hbm,
    tokens,
    cotangent,
    attention,
    share,
    own,
    params,
    mine_hbm,
    twin_hbm,
    block_out,
    mine_out,
    twin_out,
    hidden_out,
    back_out,
    stats_out,
    gate_out,
    sum_out,
    landed_out,
    down,
    up,
    active,
    rect,
    shared_rows,
    part,
    landing,
    staged,
    last,
    total_rows,
    gate_back,
    tile,
    sum_own,
    sum_other,
    sum_landing,
    sum_staged,
    sum_tile,
    send,
    recv,
    load_sems,
    tile_sems,
    twin_sem,
    sum_sems,
):
    micro, rows, width = tokens.shape
    total = rows * size
    units = up.shape[1]
    copies, loads = Copies(send, recv), Loads(load_sems)
    links, column = Links(size, rows, copies), Column(dp_size, copies)
    half = links.half
    here = [pl.ds(m * total, total) for m in range(micro)]
    ring = SumRing(
        column,
        loads,
        mine_hbm,
        twin_hbm,
        sum_out,
        sum_own,
        sum_other,
        sum_landing,
        sum_staged,
        sum_tile,
        sum_sems,
    )
    ring.load()
    early = down_early.shape[1]
    down_copies = columns_in(loads, down_early, down.at[pl.ds(0, early)])
    down_copies += columns_in(loads, down_late, down.at[pl.ds(early, units - early)])
    active_copies = [loads.copy(active_hbm.at[h], active.at[h]) for h in here]
    branch_copies = [loads.copy(branch_hbm.at[h], shared_rows.at[h]) for h in here]
    rect_copy = loads.copy(rect_hbm.at[here[0]], rect)
    up_copy = loads.copy(up_hbm, up)
    stats_out[...] = jnp.zeros_like(stats_out)
    gate_out[...] = jnp.zeros_like(gate_out)
    greet(*links.peers, *column.ring, *column.pair)
    ring.start()
    step = min(512, units)
    tile_cols = min(512, width)
    outs = [
        Scatter(
            links, part, m * total, landing.at[m], staged.at[m], last.at[m], total_rows.at[m]
        )
        for m in range(micro)
    ]
    backs = [
        Scatter(
            links,
            part,
            m * total,
            landing.at[micro + m],
            staged.at[micro + m],
            last.at[micro + m],
            hidden_out.at[m],
        )
        for m in range(micro)
    ]
    wait_all(down_copies)
    for m in range(micro):
        active_copies[m].wait()

        def body(j, _, m=m):
            cols = pl.ds(pl.multiple_of(j * tile_cols, tile_cols), tile_cols)
            part[here[m], cols] = dot(active[here[m], :], down[:, cols]).astype(BF16)
            return 0

        lax.fori_loop(0, width // tile_cols, body, 0)
        outs[m].start()
    for m in range(micro):
        branch_copies[m].wait()
        rect_copy.wait()

        def body(j, _, m=m):
            cols = pl.ds(pl.multiple_of(j * step, step), step)
            back = dot_nt(shared_rows[here[m], :], down[cols, :])
            active[here[m], cols] = (2.0 * rect[:, cols].astype(F32) * back).astype(BF16)
            return 0

        lax.fori_loop(0, units // step, body, 0)
        if m + 1 < micro:
            rect_copy = loads.copy(rect_hbm.at[here[m + 1]], rect)
        if m == 0:
            up_copy.wait()
    second_copies = [loads.copy(second_hbm.at[h], shared_rows.at[h]) for h in here]
    if column.chips > 2:
        ring.advance()
    for m in range(micro):
        outs[m].middle()

        def body(j, _, m=m):
            cols = pl.ds(pl.multiple_of(j * tile_cols, tile_cols), tile_cols)
            part[here[m], cols] = dot_nt(active[here[m], :], up[cols, :]).astype(BF16)
            return 0

        lax.fori_loop(0, width // tile_cols, body, 0)
        backs[m].start()

    def finish_out(m):
        outs[m].finish()

        def body(where, i, row):
            branch = outs[m].chunk(where, i)
            info = own[m, at(row), :]
            live = info[:, LIVE : LIVE + 1]
            outer = cotangent[m, at(row), :].astype(F32) * live
            hidden = tokens[m, at(row), :].astype(F32)
            hidden = hidden + info[:, GATE : GATE + 1] * attention[m, at(row), :]
            gate = NB * jnp.sum(share[m, at(row), :] * info, axis=-1, keepdims=True)
            block_out[m, at(row), :] = (live * (hidden + gate * branch)).astype(BF16)
            value = jnp.sum(outer * branch, axis=-1, keepdims=True)
            gate_back[m, at(row), :] = jnp.broadcast_to(value, (STEP, LANES))

        over_rows(half, body)

    def finish_back(m):
        backs[m].finish()

        def body(where, i, row):
            back = backs[m].chunk(where, i)
            info = own[m, at(row), :]
            portions = share[m, at(row), :]
            live = info[:, LIVE : LIVE + 1]
            outer = cotangent[m, at(row), :].astype(F32) * live
            hidden = tokens[m, at(row), :].astype(F32)
            attended = attention[m, at(row), :]
            hidden = hidden + info[:, GATE : GATE + 1] * attended
            normed, inverse = normalized(hidden)
            gain = params[FEED : FEED + 1, :]
            low = (normed * gain + params[FEED + 1 : FEED + 2, :]).astype(BF16).astype(F32)
            picked = jnp.sum(portions * info, axis=-1, keepdims=True)
            logit_back = NB * picked * (info - portions) * gate_back[m, at(row), :]
            for b in range(NB):
                column = logit_back[:, b : b + 1]
                back = back + column * params[WIDTH_ROUTER + b : WIDTH_ROUTER + b + 1, :]
                stats_out[2 + b : 3 + b, :] += jnp.sum(column * low, axis=0, keepdims=True)
            stats_out[0:1, :] += jnp.sum(back * normed, axis=0, keepdims=True)
            stats_out[1:2, :] += jnp.sum(back, axis=0, keepdims=True)
            hidden_back = outer + norm_back(back, normed, inverse, gain)
            hidden_out[m, at(row), :] = hidden_back
            back_out[m, at(row), :] = (info[:, GATE : GATE + 1] * hidden_back).astype(BF16)
            gate_part = jnp.sum(hidden_back * attended, axis=-1, keepdims=True)
            gate_out[m : m + 1, :] += jnp.sum(info * gate_part, axis=0, keepdims=True)

        over_rows(half, body)

    wait_all(second_copies)
    block = mine_out.shape[1]

    def make(c, ref):
        ref[...] = dot_tn(
            shared_rows[:, pl.ds(pl.multiple_of(c * block, block), block)], active[...]
        ).astype(BF16)

    early, other, staged_up = [up.at[pl.ds(i * block, block)] for i in range(3)]
    up_ring = SumRing(
        column, loads, mine_out, twin_out, None, early, other, landed_out, staged_up, None, None
    )

    def start_up():
        up_ring.load()
        up_ring.start(more=False)

    blocks_out(column, make, tile, mine_out, twin_out, tile_sems, twin_sem, start_up)
    if column.chips > 3:
        ring.advance()
    for m in range(micro):
        finish_out(m)
    for m in range(micro):
        backs[m].middle()
    for m in range(micro):
        finish_back(m)
    ring.finish()
    up_ring.hop.wait()


STATS_ONE = 6
STATS_USE = 12
STATS_ROWS = 16
SEQ_COUNT = 4


def attend_back_kernel(
    dp_size,
    size,
    heads,
    back,
    gate,
    out_hbm,
    qkv_hbm,
    heads_hbm,
    rows_hbm,
    mask_hbm,
    mix_hbm,
    cosine,
    sine,
    row_info,
    mine_hbm,
    twin_hbm,
    landed_hbm,
    tokens,
    hidden_back,
    own,
    seq_info,
    params,
    stats_two,
    usage,
    back_out,
    up_sum,
    mix_sum,
    out_sum,
    stats_out,
    mix_mine,
    mix_twin,
    out_mine,
    out_twin,
    buf,
    out,
    qkv,
    head_rows,
    rows_buf,
    mask,
    heads_back,
    mixed_back,
    score_back,
    shares,
    out_tile,
    mix_tile,
    gates,
    mix,
    landing,
    staged,
    last,
    *rest,
):
    up_bufs, mix_bufs, out_bufs = rest[:5], rest[5:10], rest[10:15]
    stats, share, pieces, sums, whole = rest[15:20]
    send, recv, load_sems = rest[20:23]
    out_sems, out_twin_sem, mix_sems, mix_twin_sem, up_sum_sems, mix_sum_sems, out_sum_sems = rest[23:]
    micro, rows, width = back.shape
    total = rows * size
    copies, loads = Copies(send, recv), Loads(load_sems)
    links, column = Links(size, rows, copies), Column(dp_size, copies)
    half = links.half
    ring = SumRing(column, loads, mine_hbm, twin_hbm, up_sum, *up_bufs, up_sum_sems)
    mix_ring = SumRing(column, loads, mix_mine, mix_twin, mix_sum, *mix_bufs, mix_sum_sems)
    out_ring = SumRing(column, loads, out_mine, out_twin, out_sum, *out_bufs, out_sum_sems)
    ring.prepare(landed_hbm)
    own_copies = []
    for m in range(micro):
        for where in range(2):
            own_copies.append(
                loads.copy(
                    back.at[m, pl.ds(where * half, half)],
                    buf.at[pl.ds(m * total + where * links.second, half)],
                )
            )
    out_copies = columns_in(loads, out_hbm, out)
    qkv_copy = loads.copy(qkv_hbm, qkv)
    mask_copy = loads.copy(mask_hbm, mask)
    heads_copy = loads.copy(heads_hbm, head_rows)
    rows_copy = loads.copy(rows_hbm, rows_buf)
    mix_copy = loads.copy(mix_hbm, mix)
    gates[links.me] = gate[...]
    near = [lax.rem(links.me + s, size) for s in range(1, size)]
    far = [lax.rem(column.me + s, dp_size) for s in range(1, dp_size)]
    greet(*[("tensor", to) for to in near], *[("dp", to) for to in far])
    wait_all(own_copies)
    gathers = [Gather(links, buf, m * total) for m in range(micro)]
    gathers[0].start()
    ring.resume()
    gate_copies = [links.copy(gate, gates.at[links.me], peer) for peer in near]
    stats[...] = jnp.zeros_like(stats)
    stats[0:8, :] = stats_two[...]
    stats[STATS_USE : STATS_USE + 1, 0:LANES] = usage[0:1, :]
    wait_all(out_copies)
    qkv_copy.wait()
    mask_copy.wait()
    scale = HD ** (-0.5)
    chunk = min(128, total)
    gathers[0].middle()
    for g in gathers[1:]:
        g.start()
    block, wide = out_mine.shape[2], out_tile.shape[3]
    here_rows = [pl.ds(m * total, total) for m in range(micro)]
    scatters = [
        Scatter(links, buf, m * total, landing.at[m], staged.at[m], last.at[m], back_out.at[m])
        for m in range(micro)
    ]

    def heads_part(m):
        base = m * total
        every = pl.ds(base, total)
        value = dot_nt(buf[every, :], out[...])
        for h in range(heads):
            here = pl.ds(h * HD, HD)
            heads_back[:, here] = (
                value[:, h * HD : (h + 1) * HD] * row_info[m, :, h : h + 1]
            ).astype(BF16)
        for h in range(heads):
            here = pl.ds(h * HD, HD)

            def some(c, _, m=m, here=here):
                rows_here = pl.ds(pl.multiple_of(c * chunk, chunk), chunk)
                scores = dot_nt(qkv[m, 0, rows_here, here], qkv[m, 1, :, here]) * scale
                scores = scores + mask[m, rows_here, :]
                powers = jnp.exp(scores - jnp.max(scores, axis=-1, keepdims=True))
                share = powers / jnp.sum(powers, axis=-1, keepdims=True)
                share_back = dot_nt(heads_back[rows_here, here], qkv[m, 2, :, here])
                inner = jnp.sum(share * share_back, axis=-1, keepdims=True)
                score_back[rows_here, :] = (share * (share_back - inner)).astype(BF16)
                shares[rows_here, :] = share.astype(BF16)
                return 0

            lax.fori_loop(0, total // chunk, some, 0)
            cos, sin = cosine[m], -sine[m]
            query_back = dot(score_back[...], qkv[m, 1, :, here]) * scale
            keys_back = dot_tn(score_back[...], qkv[m, 0, :, here]) * scale
            values_back = dot_tn(shares[...], heads_back[:, here])
            col = 3 * h * HD
            mixed_back[every, pl.ds(col, HD)] = turned(query_back, cos, sin).astype(BF16)
            mixed_back[every, pl.ds(col + HD, HD)] = turned(keys_back, cos, sin).astype(BF16)
            mixed_back[every, pl.ds(col + 2 * HD, HD)] = values_back.astype(BF16)
            if m == 0 and h == 0:
                for g in gathers[1:]:
                    g.middle()
                if column.chips > 3:
                    ring.advance()

    def make_out(c, put):
        value = dot_tn(head_rows[:, pl.ds(pl.multiple_of(c * wide, wide), wide)], buf[...])
        for j in range(dp_size):
            put(j, value[:, j * block : (j + 1) * block].astype(BF16))

    def make_mix(c, ref):
        ref[...] = dot_tn(
            rows_buf[:, pl.ds(pl.multiple_of(c * block, block), block)], mixed_back[...]
        ).astype(BF16)

    tile = min(512, width)

    def first_part(m):
        def body(j, _):
            cols = pl.ds(pl.multiple_of(j * tile, tile), tile)
            buf[here_rows[m], cols] = dot_nt(mixed_back[here_rows[m], :], mix[cols, :]).astype(BF16)
            return 0

        lax.fori_loop(0, width // tile, body, 0)
        scatters[m].start()

    gathers[0].finish()
    heads_part(0)
    for g in gathers[1:]:
        g.finish()
    heads_copy.wait()
    halves_out(
        column,
        heads * HD // wide,
        make_out,
        out_tile,
        out_mine,
        out_twin,
        out_sems,
        out_twin_sem,
    )
    out_ring.load()
    out_ring.start()
    mix_copy.wait()
    first_part(0)
    for m in range(1, micro):
        heads_part(m)
    scatters[0].middle()
    if column.chips > 2:
        out_ring.advance()
    rows_copy.wait()

    def start_mix():
        mix_ring.load()
        mix_ring.start(more=False)

    blocks_out(column, make_mix, mix_tile, mix_mine, mix_twin, mix_sems, mix_twin_sem, start_mix)
    mix_ring.load()
    if column.chips > 3:
        out_ring.advance()
    for m in range(1, micro):
        first_part(m)
    for made in gate_copies:
        made.wait()
    gate_sum = gates[0]
    for r in range(1, size):
        gate_sum = gate_sum + gates[r]

    def last_rows(m):
        s = scatters[m]
        s.finish()
        count = SEQ_COUNT
        lane = lax.broadcasted_iota(jnp.int32, (8, LANES), 1)
        which = lax.broadcasted_iota(jnp.int32, (8, LANES), 0)
        info = seq_info[m]
        gate_back = jnp.where(lane == SEQ + which, gate_sum[m : m + 1, :], 0.0)
        gate_back = jnp.sum(gate_back, axis=-1, keepdims=True)
        chosen = jnp.where(lane == info[:, CHOSEN : CHOSEN + 1].astype(jnp.int32), 1.0, 0.0)
        logit_back = NHC * info[:, PICKED : PICKED + 1] * (chosen - info) * gate_back
        logit_back = logit_back / info[:, DIVISOR : DIVISOR + 1]

        def body(where, i, row):
            back = s.chunk(where, i)
            normed, inverse = normalized(tokens[m, at(row), :].astype(F32))
            gain = params[ATTEND : ATTEND + 1, :]
            low = (normed * gain + params[ATTEND + 1 : ATTEND + 2, :]).astype(BF16).astype(F32)
            rows_info = own[m, at(row), :]
            spread = jnp.zeros((STEP, LANES), F32)
            for q in range(count):
                spread = spread + rows_info[:, SEQ + q : SEQ + q + 1] * logit_back[q : q + 1, :]
            for c in range(NHC):
                part = spread[:, c : c + 1]
                back = back + part * params[HEAD_ROUTER + c : HEAD_ROUTER + c + 1, :]
                at_row = STATS_ONE + 2 + c
                stats[at_row : at_row + 1, :] += jnp.sum(part * low, axis=0, keepdims=True)
            at_row = STATS_ONE
            stats[at_row : at_row + 1, :] += jnp.sum(back * normed, axis=0, keepdims=True)
            stats[at_row + 1 : at_row + 2, :] += jnp.sum(back, axis=0, keepdims=True)
            value = norm_back(back, normed, inverse, gain)
            back_out[m, at(row), :] = hidden_back[m, at(row), :] + value

        over_rows(links.half, body)

    last_rows(0)
    if column.chips > 2:
        mix_ring.advance()
    for s in scatters[1:]:
        s.middle()
    ring.finish()
    for m in range(1, micro):
        last_rows(m)

    piece = width // size
    mine = pl.ds(pl.multiple_of(links.me * piece, piece), piece)
    sent = [
        links.copy(
            stats.at[:, pl.ds(pl.multiple_of(to * piece, piece), piece)], pieces.at[links.me], to
        )
        for to in near
    ]
    pieces[links.me] = stats[:, mine]
    wait_all(sent)
    value = pieces[0]
    for r in range(1, size):
        value = value + pieces[r]
    share[0] = value
    sums[column.me] = value
    sent = [column.copy(share.at[0], sums.at[column.me], to) for to in far]
    if column.chips > 3:
        mix_ring.advance()
    out_ring.finish()
    wait_all(sent)
    value = sums[0]
    for r in range(1, dp_size):
        value = value + sums[r]
    share[1] = value
    whole[links.me] = value
    wait_all([links.copy(share.at[1], whole.at[links.me], to) for to in near])
    for r in range(size):
        stats_out[:, r * piece : (r + 1) * piece] = whole[r]
    mix_ring.finish()


ANY = pl.BlockSpec(memory_space=pl.ANY)
VMEM = pl.BlockSpec(memory_space=pltpu.VMEM)
SMEM = pl.BlockSpec(memory_space=pltpu.SMEM)


def call(kernel, ident, ins, outs, scratch, copies, loads, extra=(), flops=0, limit=56):
    dma = pltpu.SemaphoreType.DMA
    sems = [dma((copies,)), dma((copies,)), dma((loads,))] + [dma((n,)) for n in extra]
    moved = sum(a.size * a.dtype.itemsize for a, _ in ins)
    return pl.pallas_call(
        kernel,
        out_shape=[jax.ShapeDtypeStruct(shape, kind) for shape, kind, _ in outs],
        in_specs=[SMEM if near == "s" else VMEM if near else ANY for _, near in ins],
        out_specs=[VMEM if near else ANY for _, _, near in outs],
        scratch_shapes=[pltpu.VMEM(shape, kind) for shape, kind in scratch] + sems,
        compiler_params=pltpu.CompilerParams(
            collective_id=ident, has_side_effects=True, vmem_limit_bytes=limit * MIB
        ),
        cost_estimate=pl.CostEstimate(flops=flops, bytes_accessed=moved, transcendentals=0),
    )(*[a for a, _ in ins])


def local(
    dp_size,
    size,
    tokens,
    cotangent,
    mixer,
    merger,
    expand,
    shrink,
    attend_gain,
    attend_bias,
    feed_gain,
    feed_bias,
    width_router,
    head_router,
    lengths,
    head_choice,
    width_bucket,
):
    micro, rows, width = tokens.shape
    total = width_bucket.shape[1]
    every = micro * total
    half = rows // 2
    high = size // 2
    heads = merger.shape[0] // HD
    units = expand.shape[1]
    block = width // dp_size
    chips = dp_size // 2
    few = transfers(size)
    ringed = ring_copies(dp_size)

    vectors = jnp.concatenate([attend_gain, attend_bias, feed_gain, feed_bias]).reshape(4, width)
    params = jnp.concatenate(
        [vectors, jnp.concatenate([width_router, head_router], axis=1).T], axis=0
    ).astype(F32)
    rates = jnp.power(10000.0, -2.0 * jnp.arange(HD // 2, dtype=F32) / HD)
    rates = jnp.concatenate([rates, rates])[None]

    tables = (micro, total, LANES)
    first_rows, mix_weight, out_weight, mask, cosine, sine, row_info, own, seq_info, usage = call(
        functools.partial(first_norm_kernel, dp_size, size, heads, units),
        1,
        [
            (tokens, True),
            (params, True),
            (rates, True),
            (width_bucket, True),
            (lengths, "s"),
            (head_choice, "s"),
            (mixer, False),
            (merger, False),
        ],
        [
            ((every, width), BF16, False),
            ((dp_size,) + mixer.shape, BF16, False),
            ((dp_size,) + merger.shape, BF16, False),
            ((micro, total, total), F32, True),
            (tables, F32, True),
            (tables, F32, True),
            (tables, F32, True),
            ((micro, rows, LANES), F32, True),
            ((micro, 8, LANES), F32, True),
            ((8, LANES), F32, True),
        ],
        [
            ((every, width), BF16),
            ((total, LANES), jnp.int32),
            (tables, jnp.int32),
            (tables, F32),
        ],
        micro * few + 2 * ringed,
        micro + 2,
    )
    mix_weight = mix_weight.reshape(width, -1)

    lands = half * (2 * (high - 1) + high)
    stages = half * high
    wide_heads = heads * HD
    span = 3 * wide_heads
    buffers = [((micro, lands, width), BF16), ((micro, stages, width), BF16), ((micro, stages, width), BF16)]
    qkv, head_rows, attention, second_rows, width_share, branch_own, up_weight, down_early = call(
        functools.partial(attend_kernel, dp_size, size, heads),
        2,
        [
            (first_rows, False),
            (mix_weight, False),
            (out_weight, False),
            (mask, False),
            (cosine, True),
            (sine, True),
            (row_info, True),
            (own, True),
            (tokens, True),
            (cotangent, True),
            (params, True),
            (expand, False),
            (shrink, False),
        ],
        [
            ((micro, 3, total, wide_heads), BF16, False),
            ((every, wide_heads), BF16, False),
            ((micro, rows, width), F32, True),
            ((every, width), BF16, False),
            ((micro, rows, LANES), F32, True),
            ((micro, rows, width), BF16, True),
            ((dp_size,) + expand.shape, BF16, False),
            ((dp_size, units // 4, block), BF16, False),
        ],
        [
            ((every, width), BF16),
            ((width, span), BF16),
            ((wide_heads, width), BF16),
            ((micro, total, total), F32),
            ((micro, 3, total, wide_heads), BF16),
            ((every, wide_heads), BF16),
            ((every, width), BF16),
        ]
        + buffers
        + [((every, width), BF16)],
        2 * micro * few + 2 * ringed,
        2 + micro + dp_size + 2 + micro + 2,
        flops=2 * every * width * (span + wide_heads) + 8 * heads * micro * total * total * HD,
    )

    up_weight = up_weight.reshape(width, -1)
    unit_tile = 256
    rect, active, branch_rows, down_late, down_mine, down_twin = call(
        functools.partial(widen_kernel, dp_size, size, heads),
        3,
        [
            (second_rows, False),
            (up_weight, False),
            (branch_own, False),
            (row_info, True),
            (shrink, False),
        ],
        [
            ((every, units), BF16, False),
            ((every, units), BF16, False),
            ((every, width), BF16, False),
            ((dp_size, units - units // 4, block), BF16, False),
            ((chips, units, block), BF16, False),
            ((chips, units, block), BF16, False),
        ],
        [
            ((every, width), BF16),
            ((width, units), BF16),
            ((every, width), BF16),
            ((every, units), BF16),
            ((every, units), BF16),
            ((2, 2, chips, unit_tile, block), BF16),
        ],
        micro * few + ringed,
        2 + 6 * micro,
        (4, 1),
        flops=4 * every * width * units,
    )

    narrowed = call(
        functools.partial(narrow_kernel, dp_size, size),
        4,
        [
            (down_early, False),
            (down_late, False),
            (up_weight, False),
            (active, False),
            (rect, False),
            (branch_rows, False),
            (second_rows, False),
            (tokens, True),
            (cotangent, True),
            (attention, True),
            (width_share, True),
            (own, True),
            (params, True),
            (down_mine, False),
            (down_twin, False),
        ],
        [
            ((micro, rows, width), BF16, True),
            ((chips, block, units), BF16, False),
            ((chips, block, units), BF16, False),
            ((micro, rows, width), F32, True),
            ((micro, rows, width), BF16, True),
            ((8, width), F32, True),
            ((8, LANES), F32, True),
            ((units, block), F32, False),
            ((1, block, units), BF16, False),
        ],
        [
            ((units, width), BF16),
            ((width, units), BF16),
            ((every, units), BF16),
            ((total, units), BF16),
            ((every, width), BF16),
            ((every, width), BF16),
            ((2 * micro, lands, width), BF16),
            ((2 * micro, stages, width), BF16),
            ((2 * micro, stages, width), BF16),
            ((micro, rows, width), F32),
            ((micro, rows, LANES), F32),
            ((2, block, units), BF16),
        ]
        + sum_scratch(chips, units, block),
        2 * micro * few + chips,
        2 * dp_size + 4 * micro + 1 + 2 * chips + 2,
        (2, chips, SUM_TILES),
        flops=8 * every * width * units,
        limit=63,
    )
    block_output, up_mine, up_twin, hidden_back, back_own, stats_two, gate_part = narrowed[:7]
    down_sum, up_landed = narrowed[7:]

    out_tile = min(256, wide_heads)
    lasts = call(
        functools.partial(attend_back_kernel, dp_size, size, heads),
        5,
        [
            (back_own, False),
            (gate_part, True),
            (out_weight, False),
            (qkv, False),
            (head_rows, False),
            (first_rows, False),
            (mask, False),
            (mix_weight, False),
            (cosine, True),
            (sine, True),
            (row_info, True),
            (up_mine, False),
            (up_twin, False),
            (up_landed, False),
            (tokens, True),
            (hidden_back, True),
            (own, True),
            (seq_info, True),
            (params, True),
            (stats_two, True),
            (usage, True),
        ],
        [
            ((micro, rows, width), F32, True),
            ((block, units), F32, False),
            ((block, span), F32, False),
            ((wide_heads, block), F32, False),
            ((STATS_ROWS, width), F32, True),
            ((chips, block, span), BF16, False),
            ((chips, block, span), BF16, False),
            ((chips, wide_heads, block), BF16, False),
            ((chips, wide_heads, block), BF16, False),
        ],
        [
            ((every, width), BF16),
            ((wide_heads, width), BF16),
            ((micro, 3, total, wide_heads), BF16),
            ((every, wide_heads), BF16),
            ((every, width), BF16),
            ((micro, total, total), F32),
            ((total, wide_heads), BF16),
            ((every, span), BF16),
            ((total, total), BF16),
            ((total, total), BF16),
            ((2, 2, chips, out_tile, block), BF16),
            ((2, block, span), BF16),
            ((size, 8, LANES), F32),
            ((width, span), BF16),
        ]
        + buffers
        + sum_scratch(chips, block, units)
        + sum_scratch(chips, block, span)
        + sum_scratch(chips, wide_heads, block)
        + [
            ((STATS_ROWS, width), F32),
            ((2, STATS_ROWS, width // size), F32),
            ((size, STATS_ROWS, width // size), F32),
            ((dp_size, STATS_ROWS, width // size), F32),
            ((size, STATS_ROWS, width // size), F32),
        ],
        2 * micro * few + 3 * (size - 1) + dp_size - 1 + 3 * (chips - 1),
        2 * micro + dp_size + 6 + 6 * chips,
        (4, 1, 2, chips, SUM_TILES, SUM_TILES, SUM_TILES),
        flops=4 * every * width * (wide_heads + span) + 20 * heads * micro * total * total * HD,
        limit=63,
    )
    tokens_gradient, up_sum, mix_sum, out_sum, stats = lasts[:5]
    return (
        block_output,
        tokens_gradient,
        mix_sum,
        out_sum,
        up_sum,
        down_sum,
        stats[STATS_ONE],
        stats[STATS_ONE + 1],
        stats[0],
        stats[1],
        stats[2 : 2 + NB].T,
        stats[STATS_ONE + 2 : STATS_ONE + 2 + NHC].T,
        stats[STATS_USE, :NB],
        stats[STATS_USE, CHOICE : CHOICE + NHC],
    )


def solution(mesh):
    def run(*args):
        return local(mesh.shape["dp"], mesh.shape["tensor"], *args)

    rows = P(None, ("dp", "tensor"), None)
    tall, wide = P("dp", "tensor"), P("tensor", "dp")
    weights = (tall, wide, tall, wide)
    return jax.shard_map(
        run,
        mesh=mesh,
        in_specs=(rows, rows) + weights + (P(),) * 6 + (P(None, "dp"),) * 3,
        out_specs=(rows, rows) + weights + (P(),) * 8,
        check_vma=False,
    )
```

```python
import functools

import jax
import jax.numpy as jnp
from jax import lax
from jax.experimental import pallas as pl
from jax.experimental.pallas import tpu as pltpu
from jax.sharding import PartitionSpec as P

H = 16
HD = 128
FF = 8192
NB = 4
NHC = 4

EPSILON = 1e-05
HIGHEST = lax.Precision.HIGHEST
MASKED = -1e30
BF16 = jnp.bfloat16
F32 = jnp.float32
MESH = pl.DeviceIdType.MESH
MIB = 1024 * 1024
LANES = 128
STEP = 16

GATE = 4
LIVE = 5
SEQ = 8
CHOICE = 16

PICKED = 4
DIVISOR = 5
CHOSEN = 6

ATTEND = 0
FEED = 2
WIDTH_ROUTER = 4
HEAD_ROUTER = 8


def dot(left, right):
    return jnp.dot(left, right, preferred_element_type=F32)


def dot_nt(left, right):
    return lax.dot_general(left, right, (((1,), (1,)), ((), ())), preferred_element_type=F32)


def dot_tn(left, right):
    return lax.dot_general(left, right, (((0,), (0,)), ((), ())), preferred_element_type=F32)


def at(start, size=STEP):
    return pl.ds(pl.multiple_of(start, STEP), size)


class Copies:
    def __init__(self, send_sems, recv_sems):
        self.send_sems, self.recv_sems, self.used = send_sems, recv_sems, 0

    def start(self, src, dst, axis, to):
        made = pltpu.make_async_remote_copy(
            src_ref=src,
            dst_ref=dst,
            send_sem=self.send_sems.at[self.used],
            recv_sem=self.recv_sems.at[self.used],
            device_id={axis: to},
            device_id_type=MESH,
        )
        self.used += 1
        made.start()
        return made


def greet(*peers):
    barrier = pltpu.get_barrier_semaphore()
    for axis, to in peers:
        pl.semaphore_signal(barrier, inc=1, device_id={axis: to}, device_id_type=MESH)
    pl.semaphore_wait(barrier, len(peers))


class Links:
    def __init__(self, size, rows, copies):
        me = lax.axis_index("tensor")
        hi, lo = me // 2, me % 2
        self.me, self.size, self.high, self.half = me, size, size // 2, rows // 2
        self.near = hi * 2 + (1 - lo)
        self.ahead = [lax.rem(hi + s, self.high) * 2 + lo for s in range(self.high)]
        self.behind = [
            lax.rem(hi + self.high - s, self.high) * 2 + lo for s in range(self.high)
        ]
        self.second = self.half * size
        self.copies = copies
        steps = range(self.high)
        grid = [[lax.rem(hi + s, self.high) * 2 + (lo + l) % 2 for l in range(2)] for s in steps]
        self.first_ranks = [grid[s][l] for s in steps for l in range(2)]
        self.second_ranks = [grid[s][l] for l in range(2) for s in steps]
        self.peers = [("tensor", to) for to in [self.near] + self.ahead[1:]]

    def copy(self, src, dst, to):
        return self.copies.start(src, dst, "tensor", to)


class Column:
    def __init__(self, size, copies):
        self.me, self.chips, self.copies = lax.axis_index("dp"), size // 2, copies
        self.chip, self.core = self.me // 2, self.me % 2
        self.twin = self.chip * 2 + 1 - self.core
        self.right = self.block(1)
        self.left = self.block(-1)
        self.ring = [("dp", self.left)]
        self.pair = [("dp", self.twin)]

    def chip_at(self, step):
        return lax.rem(self.chip + self.chips + step, self.chips)

    def block(self, step):
        return self.chip_at(step) * 2 + self.core

    def copy(self, src, dst, to):
        return self.copies.start(src, dst, "dp", to)


class WeightRing:
    def __init__(self, column, loads, own, slot):
        self.column, self.loads, self.own, self.slot = column, loads, own, slot

    def start(self):
        k = self.column
        here = self.slot(k.me)
        self.hops = [k.copy(self.own, here, k.right)]
        self.twins = [k.copy(self.own, here, k.twin)]
        self.local = self.loads.copy(self.own, here)

    def advance(self):
        k = self.column
        step = len(self.twins)
        self.hops[step - 1].wait_recv()
        here = self.slot(k.block(-step))
        if step < k.chips - 1:
            self.hops.append(k.copy(here, here, k.right))
        self.twins.append(k.copy(here, here, k.twin))

    def advance_all(self):
        while len(self.twins) < self.column.chips:
            self.advance()

    def finish(self):
        self.advance_all()
        for made in self.twins:
            made.wait()
        for made in self.hops:
            made.wait_send()
        self.local.wait()


def ring_copies(size):
    return size // 2 * 2 - 1


class SumRing:
    def __init__(self, column, loads, mine, twin, target, own, other, landing, staged, tile, tile_sems):
        self.column, self.loads = column, loads
        self.mine, self.twin, self.target = mine, twin, target
        self.own, self.other, self.landing, self.staged = own, other, landing, staged
        self.tile, self.tile_sems = tile, tile_sems
        self.sent = 0
        self.rows = sum_rows(own.shape[1])

    def load(self):
        block = self.column.chip_at(-1 - self.sent)
        self.loading = [
            self.loads.copy(self.mine.at[block], self.own),
            self.loads.copy(self.twin.at[block], self.other),
        ]

    def send(self, landed, more=True):
        k, rows = self.column, self.rows

        def body(i, _):
            here = pl.ds(pl.multiple_of(i * rows, rows), rows)
            value = self.own[here, :].astype(F32) + self.other[here, :].astype(F32)
            if landed is not None:
                value = value + self.landing[landed, here, :].astype(F32)
            self.staged[here, :] = value.astype(BF16)
            return 0

        lax.fori_loop(0, self.own.shape[0] // rows, body, 0)
        self.hop = k.copy(self.staged, self.landing.at[self.sent], k.right)
        self.sent += 1
        if more:
            self.load()

    def start(self, more=True):
        wait_all(self.loading)
        self.send(None, more)

    def prepare(self, landed):
        self.sent = 1
        self.load()
        self.loading.append(self.loads.copy(landed.at[0], self.landing.at[0]))

    def resume(self):
        wait_all(self.loading)
        self.send(0)

    def advance(self):
        self.hop.wait()
        wait_all(self.loading)
        self.send(self.sent - 1)

    def finish(self):
        k, rows = self.column, self.rows
        while self.sent < k.chips - 1:
            self.advance()
        self.hop.wait()
        wait_all(self.loading)
        landed = k.chips - 2
        slots = self.tile.shape[0]

        def body(i, _):
            here = pl.ds(pl.multiple_of(i * rows, rows), rows)
            slot = lax.rem(i, slots)
            copy = pltpu.make_async_copy(
                self.tile.at[slot], self.target.at[here], self.tile_sems.at[slot]
            )

            @pl.when(i >= slots)
            def _():
                copy.wait()

            value = self.own[here, :].astype(F32) + self.other[here, :].astype(F32)
            self.tile[slot] = value + self.landing[landed, here, :].astype(F32)
            copy.start()
            return 0

        count = self.own.shape[0] // rows
        lax.fori_loop(0, count, body, 0)
        for i in range(max(count - slots, 0), count):
            here = pl.ds(i * rows, rows)
            slot = i % slots
            pltpu.make_async_copy(
                self.tile.at[slot], self.target.at[here], self.tile_sems.at[slot]
            ).wait()


SUM_TILES = 4


def sum_rows(width):
    return 128 if width <= 256 else 16


def sum_scratch(chips, rows, width):
    return [
        ((rows, width), BF16),
        ((rows, width), BF16),
        ((chips - 1, rows, width), BF16),
        ((rows, width), BF16),
        ((SUM_TILES, sum_rows(width), width), F32),
    ]


def transfers(size):
    return 2 * (size // 2)


class Gather:
    def __init__(self, links, buf, base):
        self.links, self.buf, self.base = links, buf, base

    def rows(self, start, count):
        return self.buf.at[pl.ds(self.base + start, count)]

    def start(self):
        k, half, second = self.links, self.links.half, self.links.second
        self.first_near = k.copy(self.rows(0, half), self.rows(half, half), k.near)
        self.second_far = [
            k.copy(self.rows(second, half), self.rows(second + s * half, half), k.behind[s])
            for s in range(1, k.high)
        ]

    def middle(self):
        k, half, second = self.links, self.links.half, self.links.second
        self.first_near.wait_recv()
        self.first_far = [
            k.copy(self.rows(0, 2 * half), self.rows(2 * half * s, 2 * half), k.behind[s])
            for s in range(1, k.high)
        ]
        for made in self.second_far:
            made.wait_recv()
        block = k.high * half
        self.second_near = k.copy(self.rows(second, block), self.rows(second + block, block), k.near)

    def finish(self):
        for made in self.first_far + [self.second_near]:
            made.wait_recv()
        for made in [self.first_near, self.second_near] + self.first_far + self.second_far:
            made.wait_send()


class Scatter:
    def __init__(self, links, part, base, landing, staged, last, total):
        self.links, self.part, self.base = links, part, base
        self.landing, self.staged, self.last, self.total = landing, staged, last, total

    def start(self):
        k, half = self.links, self.links.half
        block = k.high * half
        self.first_far = [
            k.copy(
                self.part.at[pl.ds(self.base + 2 * half * s, 2 * half)],
                self.landing.at[pl.ds(2 * half * (s - 1), 2 * half)],
                k.ahead[s],
            )
            for s in range(1, k.high)
        ]
        self.second_near = k.copy(
            self.part.at[pl.ds(self.base + k.second + block, block)],
            self.landing.at[pl.ds(2 * half * (k.high - 1), block)],
            k.near,
        )

    def middle(self):
        k, half, base = self.links, self.links.half, self.base
        steps = half // STEP
        for made in self.first_far:
            made.wait_recv()

        def first(i, _):
            for where in range(2):
                row = where * half + i * STEP
                value = self.part[at(base + row), :].astype(F32)
                for s in range(1, k.high):
                    value = value + self.landing[at(2 * half * (s - 1) + row), :].astype(F32)
                if where == 0:
                    self.total[at(i * STEP), :] = value
                else:
                    self.staged[at(i * STEP), :] = value.astype(BF16)
            return 0

        lax.fori_loop(0, steps, first, 0)
        self.first_near = k.copy(
            self.staged.at[pl.ds(0, half)], self.last.at[pl.ds(0, half)], k.near
        )
        self.second_near.wait_recv()
        landed = 2 * half * (k.high - 1)

        def second(i, _):
            for s in range(k.high):
                row = s * half + i * STEP
                value = self.part[at(base + k.second + row), :].astype(F32)
                value = value + self.landing[at(landed + row), :].astype(F32)
                if s == 0:
                    self.total[at(half + i * STEP), :] = value
                else:
                    self.staged[at(row), :] = value.astype(BF16)
            return 0

        lax.fori_loop(0, steps, second, 0)
        self.second_far = [
            k.copy(
                self.staged.at[pl.ds(half * s, half)], self.last.at[pl.ds(half * s, half)], k.ahead[s]
            )
            for s in range(1, k.high)
        ]
        for made in self.first_far + [self.second_near]:
            made.wait_send()

    def finish(self):
        for made in [self.first_near] + self.second_far:
            made.wait_recv()
            made.wait_send()

    def chunk(self, where, i):
        k, half = self.links, self.links.half
        value = self.total[at(where * half + i * STEP), :]
        if where == 0:
            return value + self.last[at(i * STEP), :].astype(F32)
        for s in range(1, k.high):
            value = value + self.last[at(half * s + i * STEP), :].astype(F32)
        return value


def over_rows(half, body):
    for where in range(2):

        def inner(i, _, where=where):
            body(where, i, where * half + i * STEP)
            return 0

        lax.fori_loop(0, half // STEP, inner, 0)


class Loads:
    def __init__(self, sems):
        self.sems, self.used = sems, 0

    def copy(self, src, dst):
        made = pltpu.make_async_copy(src, dst, self.sems.at[self.used])
        self.used += 1
        made.start()
        return made


def wait_all(*groups):
    for group in groups:
        for made in group if isinstance(group, list) else [group]:
            made.wait()


def columns_in(loads, blocks, flat):
    count, _, width = blocks.shape
    return [loads.copy(blocks.at[j], flat.at[:, pl.ds(j * width, width)]) for j in range(count)]


def halves_out(column, count, make, tile, mine, twin, sems, twin_sem, between=None):
    wide = tile.shape[3]

    def outs(c, slot):
        here = pl.ds(pl.multiple_of(c * wide, wide), wide)
        local = pltpu.make_async_copy(tile.at[slot, 0], mine.at[:, here, :], sems.at[slot])
        away = pltpu.make_async_remote_copy(
            src_ref=tile.at[slot, 1],
            dst_ref=twin.at[:, here, :],
            send_sem=sems.at[2 + slot],
            recv_sem=twin_sem.at[0],
            device_id={"dp": column.twin},
            device_id_type=MESH,
        )
        return local, away

    def body(c, _):
        slot = lax.rem(c, 2)
        local, away = outs(c, slot)

        @pl.when(c >= 2)
        def _():
            local.wait()
            away.wait_send()

        def put(block, value):
            tile[slot, lax.rem(block + column.core, 2), block // 2] = value

        make(c, put)
        local.start()
        away.start()
        return 0

    lax.fori_loop(0, count // 2, body, 0)
    if between is not None:
        between()
    lax.fori_loop(count // 2, count, body, 0)
    for c in range(max(count - 2, 0), count):
        local, away = outs(c, c % 2)
        local.wait()
        away.wait_send()
    all_landed(column, twin, sems, twin_sem)


def blocks_out(column, make, tile, mine, twin, sems, twin_sems, ring):
    def local_copy(i):
        chip = column.chip_at(-1 - i)
        return pltpu.make_async_copy(tile.at[0], mine.at[chip], sems.at[0])

    def away_copy(i):
        return pltpu.make_async_remote_copy(
            src_ref=tile.at[1],
            dst_ref=twin.at[column.chip_at(-1 - i)],
            send_sem=sems.at[1],
            recv_sem=twin_sems.at[i],
            device_id={"dp": column.twin},
            device_id_type=MESH,
        )

    def body(i, _):
        chip, local, away = column.chip_at(-1 - i), local_copy(i), away_copy(i)

        @pl.when(i > 0)
        def _():
            away.wait_send()

        make(2 * chip + 1 - column.core, tile.at[1])
        away.start()

        @pl.when(i > 1)
        def _():
            local.wait()

        make(2 * chip + column.core, tile.at[0])
        local.start()
        return 0

    lax.fori_loop(0, 1, body, 0)
    local_copy(0).wait()
    away_copy(0).wait_recv()
    ring()
    lax.fori_loop(1, column.chips, body, 0)
    for i in range(1, column.chips):
        away_copy(i).wait_recv()
    local_copy(column.chips - 1).wait()
    away_copy(column.chips - 1).wait_send()


def all_landed(column, twin, sems, twin_sem):
    pltpu.make_async_remote_copy(
        src_ref=twin,
        dst_ref=twin,
        send_sem=sems.at[0],
        recv_sem=twin_sem.at[0],
        device_id={"dp": column.twin},
        device_id_type=MESH,
    ).wait_recv()


def normalized(value):
    centred = value - jnp.mean(value, axis=-1, keepdims=True)
    inverse = lax.rsqrt(jnp.mean(centred * centred, axis=-1, keepdims=True) + EPSILON)
    return centred * inverse, inverse


def norm_back(back, normed, inverse, gain):
    scaled = back * gain
    inner = jnp.mean(scaled, axis=-1, keepdims=True)
    along = jnp.mean(scaled * normed, axis=-1, keepdims=True)
    return inverse * (scaled - inner - normed * along)


def softmax_lanes(logits, lanes):
    logits = jnp.where(lanes, logits, MASKED)
    powers = jnp.exp(logits - jnp.max(logits, axis=-1, keepdims=True))
    return jnp.where(lanes, powers / jnp.sum(powers, axis=-1, keepdims=True), 0.0)


def turned(value, cosine, sine):
    return value * cosine + pltpu.roll(value, HD // 2, 1) * sine


def attend_kernel(
    dp_size,
    size,
    heads,
    units,
    tokens,
    cotangent,
    params,
    rates,
    bucket,
    lengths,
    choices,
    mixer,
    merger,
    expand,
    shrink,
    rows_out,
    mix_out,
    out_out,
    mask,
    cosine,
    sine,
    row_info,
    own,
    seq_info,
    usage,
    qkv_out,
    heads_out,
    attention_out,
    second_out,
    share_out,
    up_out,
    down_out,
    rect_out,
    active_out,
    branch_out,
    mine_out,
    twin_out,
    rows_buf,
    slot_col,
    member_col,
    bucket_col,
    mix,
    out,
    qkv,
    head_rows,
    part,
    landing,
    staged,
    last,
    second_buf,
    up,
    branch_buf,
    tile_out,
    send,
    recv,
    load_sems,
    tile_sems,
    twin_sem,
):
    micro, rows, width = tokens.shape
    count = lengths.shape[1]
    rect, active = rows_buf, part
    total = rows * size
    copies, loads = Copies(send, recv), Loads(load_sems)
    links, column = Links(size, rows, copies), Column(dp_size, copies)
    half = links.half
    block = mixer.shape[0]
    greet(*links.peers, *column.ring, *column.pair)
    mix_ring = WeightRing(
        column, loads, mixer, lambda i: mix.at[pl.ds(pl.multiple_of(i * block, block), block)]
    )
    out_ring = WeightRing(
        column,
        loads,
        merger,
        lambda i: out.at[:, pl.ds(pl.multiple_of(i * block, block), block)],
    )
    mix_ring.start()
    first_gathers = []
    for m in range(micro):

        def body(where, i, row, m=m):
            value = tokens[m, at(row), :].astype(F32)
            low = normalized(value)[0] * params[ATTEND : ATTEND + 1, :]
            low = (low + params[ATTEND + 1 : ATTEND + 2, :]).astype(BF16)
            rows_buf[at(m * total + where * links.second + i * STEP), :] = low

        over_rows(links.half, body)
        first_gathers.append(Gather(links, rows_buf, m * total))
        first_gathers[m].start()

    starts = [r * rows for r in links.first_ranks] + [r * rows + half for r in links.second_ranks]

    def slots(shape, dimension):
        index = lax.broadcasted_iota(jnp.int32, shape, dimension)
        offset = jnp.full(shape, starts[0], jnp.int32)
        for k in range(1, len(starts)):
            offset = jnp.where(index >= k * half, starts[k] - k * half, offset)
        return index + offset

    def ends(m):
        found, end = [], 0
        for s in range(count):
            end = end + lengths[m, s]
            found.append(end)
        return found

    def members(m, slot):
        member = jnp.zeros(slot.shape, jnp.int32)
        begin = jnp.zeros(slot.shape, jnp.int32)
        for end in ends(m):
            member = member + jnp.where(slot >= end, 1, 0)
            begin = jnp.where(slot >= end, end, begin)
        return member, slot - begin

    def by_member(member, values, other):
        value = jnp.full(member.shape, other)
        for s in range(count):
            value = jnp.where(member == s, values[s], value)
        return value

    chunk = min(128, total)
    lane = lax.broadcasted_iota(jnp.int32, (chunk, LANES), 1)
    slot_row = slots((8, total), 1)
    slot_col[...] = slots((total, LANES), 0)
    member_rows = [members(m, slot_row)[0] for m in range(micro)]
    for m in range(micro):

        def table(c, _, m=m):
            here = pl.ds(pl.multiple_of(c * chunk, chunk), chunk)
            slot = slot_col[here, :]
            member, place = members(m, slot)
            member_col[m, here, :] = member
            seen = (member[:, :1] == member_rows[m][:1, :]) & (slot[:, :1] >= slot_row[:1, :])
            mask[m, here, :] = jnp.where(seen, 0.0, MASKED)
            angle = place.astype(F32) * rates[...]
            turn = jnp.sin(angle)
            cosine[m, here, :] = jnp.cos(angle)
            sine[m, here, :] = jnp.where(lane < HD // 2, -turn, turn)
            natural = lax.broadcasted_iota(jnp.int32, (chunk, total), 1)
            picked = jnp.where(slot[:, :1] == natural, bucket[m : m + 1, :].astype(F32), 0.0)
            bucket_here = jnp.sum(picked, axis=-1, keepdims=True)
            bucket_col[m, here, :] = jnp.broadcast_to(bucket_here, (chunk, LANES))
            used = by_member(member, [H // NHC * (choices[m, s] + 1) for s in range(count)], 0)
            head_on = jnp.where(links.me * heads + lane < used, 1.0, 0.0)
            first_unit = jnp.full(lane.shape, links.me * units, jnp.int32).astype(F32)
            unit_on = jnp.where(first_unit < FF // NB * (bucket_here + 1.0), 1.0, 0.0)
            row_info[m, here, :] = jnp.where(
                lane < heads, head_on, jnp.where(lane == heads, unit_on, 0.0)
            )
            return 0

        lax.fori_loop(0, total // chunk, table, 0)
    for g in first_gathers:
        g.middle()
    mix_ring.advance()
    outs, rows_saves = [], []
    usage[...] = jnp.zeros_like(usage)
    few = lax.broadcasted_iota(jnp.int32, (8, LANES), 1)
    which = lax.broadcasted_iota(jnp.int32, (8, LANES), 0)
    lane_own = lax.broadcasted_iota(jnp.int32, (half, LANES), 1)
    for m, g in enumerate(first_gathers):
        g.finish()
        here = pl.ds(m * total, total)
        rows_saves.append(loads.copy(rows_buf.at[here], rows_out.at[here]))
        sequence = lax.broadcasted_iota(jnp.int32, (8, total), 0)
        hot = jnp.where(member_rows[m] == sequence, 1.0, 0.0).astype(BF16)
        divisor = jnp.maximum(by_member(which, [lengths[m, s] for s in range(count)], 0), 1)
        divisor = divisor.astype(F32)
        chosen = by_member(which, [choices[m, s] for s in range(count)], 0)
        means = dot(hot, rows_buf[here, :]) / divisor[:, :1]
        logits = jnp.full((8, LANES), MASKED)
        for c in range(NHC):
            router = params[HEAD_ROUTER + c : HEAD_ROUTER + c + 1, :]
            logit = jnp.sum(means * router, axis=-1, keepdims=True)
            logits = jnp.where(few == c, logit, logits)
        share = softmax_lanes(logits, few < NHC)
        picked = jnp.sum(jnp.where(few == chosen, share, 0.0), axis=-1, keepdims=True)
        table = jnp.where(few == PICKED, picked, share)
        table = jnp.where(few == DIVISOR, divisor, table)
        seq_info[m] = jnp.where(few == CHOSEN, chosen.astype(F32), table)
        for where in range(2):
            source = pl.ds(where * links.second, half)
            member = member_col[m, source, :]
            gate = by_member(member, [NHC * picked[s : s + 1, :] for s in range(count)], 0.0)
            choice = by_member(member, [choices[m, s] for s in range(count)], -NHC)
            live = jnp.where(member < count, 1.0, 0.0)
            kind = bucket_col[m, source, :].astype(jnp.int32)
            hot = (lane_own == kind) | (lane_own == CHOICE + choice)
            hot = hot | ((lane_own == SEQ + member) & (member < count))
            value = jnp.where(hot & (choice >= -NHC), 1.0, 0.0)
            value = jnp.where(lane_own == GATE, gate, value)
            value = jnp.where(lane_own == LIVE, live, value)
            own[m, pl.ds(where * half, half), :] = value
            usage[0:1, :] += jnp.sum(value * live, axis=0, keepdims=True)
    if column.chips > 2:
        mix_ring.advance()
    out_ring.start()
    mix_ring.advance_all()
    out_ring.advance()
    mix_ring.finish()
    outs.append(loads.copy(mix, mix_out))
    up_ring = WeightRing(
        column, loads, expand, lambda i: up.at[pl.ds(pl.multiple_of(i * block, block), block)]
    )
    down_ring = WeightRing(column, loads, shrink, lambda i: down_out.at[i])
    scale = HD ** (-0.5)
    span = 3 * HD
    tile = min(512, width)
    saves = outs

    def project(m):
        base = m * total
        cos, sin = cosine[m], sine[m]

        def head(h, _):
            mixed = dot(
                rows_buf[pl.ds(base, total), :], mix[:, pl.ds(pl.multiple_of(h * span, HD), span)]
            )
            here = pl.ds(pl.multiple_of(h * HD, HD), HD)
            qkv[m, 0, :, here] = turned(mixed[:, :HD], cos, sin).astype(BF16)
            qkv[m, 1, :, here] = turned(mixed[:, HD : 2 * HD], cos, sin).astype(BF16)
            qkv[m, 2, :, here] = mixed[:, 2 * HD :].astype(BF16)
            return 0

        lax.fori_loop(0, heads, head, 0)

    def attend(m):
        base = m * total

        def some(c, _):
            rows_here = pl.ds(pl.multiple_of(c * chunk, chunk), chunk)
            bias_here = mask[m, rows_here, :]
            info = row_info[m, rows_here, :]
            for h in range(heads):
                here = pl.ds(h * HD, HD)
                scores = dot_nt(qkv[m, 0, rows_here, here], qkv[m, 1, :, here]) * scale + bias_here
                peak = jnp.max(scores, axis=-1, keepdims=True)
                powers = jnp.exp(scores - peak)
                share = powers / jnp.sum(powers, axis=-1, keepdims=True)
                value = dot(share.astype(BF16), qkv[m, 2, :, here]).astype(BF16)
                value = value.astype(F32) * info[:, h : h + 1]
                head_rows[pl.ds(pl.multiple_of(base + c * chunk, chunk), chunk), here] = value.astype(
                    BF16
                )
            return 0

        lax.fori_loop(0, total // chunk, some, 0)

    def merge(m):
        base = m * total

        def body(j, _):
            here = pl.ds(pl.multiple_of(j * tile, tile), tile)
            part[pl.ds(base, total), here] = dot(
                head_rows[pl.ds(base, total), :], out[:, here]
            ).astype(BF16)
            return 0

        lax.fori_loop(0, width // tile, body, 0)

    scatters = [
        Scatter(
            links,
            part,
            m * total,
            landing.at[m],
            staged.at[m],
            last.at[m],
            attention_out.at[m],
        )
        for m in range(micro)
    ]
    gathers = [Gather(links, second_buf, m * total) for m in range(micro)]

    def second_norm(m):
        scatter = scatters[m]

        def body(where, i, row):
            attended = scatter.chunk(where, i)
            info = own[m, at(row), :]
            hidden = tokens[m, at(row), :].astype(F32) + info[:, GATE : GATE + 1] * attended
            attention_out[m, at(row), :] = attended
            low = normalized(hidden)[0] * params[FEED : FEED + 1, :]
            low = (low + params[FEED + 1 : FEED + 2, :]).astype(BF16)
            second_buf[at(m * total + where * links.second + i * STEP), :] = low
            low = low.astype(F32)
            lane = lax.broadcasted_iota(jnp.int32, (STEP, LANES), 1)
            logits = jnp.full((STEP, LANES), MASKED)
            for b in range(NB):
                router = params[WIDTH_ROUTER + b : WIDTH_ROUTER + b + 1, :]
                logits = jnp.where(lane == b, jnp.sum(low * router, axis=-1, keepdims=True), logits)
            share = softmax_lanes(logits, lane < NB)
            share_out[m, at(row), :] = share
            gate = NB * jnp.sum(share * info, axis=-1, keepdims=True)
            outer = cotangent[m, at(row), :].astype(F32) * info[:, LIVE : LIVE + 1]
            branch_buf[at(m * total + where * links.second + i * STEP), :] = (gate * outer).astype(
                BF16
            )

        over_rows(half, body)

    for m in range(micro):
        project(m)
        if m == 0:
            if column.chips > 2:
                out_ring.advance()
            up_ring.start()
        attend(m)
        if m == 0:
            out_ring.finish()
            outs.append(loads.copy(out, out_out))
        else:
            scatters[m - 1].middle()
        merge(m)
        scatters[m].start()
    branch_gathers = [Gather(links, branch_buf, m * total) for m in range(micro)]
    up_ring.advance()
    for m in range(micro):
        scatters[m].finish()
        second_norm(m)
        gathers[m].start()
        if m + 1 < micro:
            scatters[m + 1].middle()
            gathers[m].middle()
            if column.chips > 2:
                up_ring.advance()
    down_ring.start()
    saves.append(loads.copy(qkv, qkv_out))
    saves.append(loads.copy(head_rows, heads_out))
    gathers[micro - 1].middle()
    for g in branch_gathers:
        g.start()
    for m in range(micro):
        gathers[m].finish()
        here = pl.ds(m * total, total)
        saves.append(loads.copy(second_buf.at[here], second_out.at[here]))
    up_ring.finish()
    saves.append(loads.copy(up, up_out))
    wait_all(rows_saves)
    step = min(512, units)
    for m in range(micro):

        def widen(j, _, m=m):
            here = pl.ds(pl.multiple_of(j * step, step), step)
            before = dot(second_buf[pl.ds(m * total, total), :], up[:, here])
            kept = jnp.maximum(before, 0.0) * row_info[m, :, heads : heads + 1]
            rect[pl.ds(m * total, total), here] = kept.astype(BF16)
            active[pl.ds(m * total, total), here] = (kept * kept).astype(BF16)
            return 0

        lax.fori_loop(0, units // step, widen, 0)
        here = pl.ds(m * total, total)
        saves.append(loads.copy(rect.at[here, pl.ds(0, units)], rect_out.at[here]))
        saves.append(loads.copy(active.at[here, pl.ds(0, units)], active_out.at[here]))
        if m == 0:
            for g in branch_gathers:
                g.middle()
            down_ring.advance()
    for m, g in enumerate(branch_gathers):
        g.finish()
        here = pl.ds(m * total, total)
        saves.append(loads.copy(branch_buf.at[here], branch_out.at[here]))
    wide = tile_out.shape[3]

    def make(c, put):
        value = dot_tn(active[:, pl.ds(pl.multiple_of(c * wide, wide), wide)], branch_buf[...])
        for j in range(dp_size):
            put(j, value[:, j * block : (j + 1) * block].astype(BF16))

    halves_out(
        column,
        units // wide,
        make,
        tile_out,
        mine_out,
        twin_out,
        tile_sems,
        twin_sem,
        down_ring.advance if column.chips > 2 else None,
    )
    down_ring.finish()
    wait_all(saves)


def narrow_kernel(
    dp_size,
    size,
    down_hbm,
    up_hbm,
    active_hbm,
    rect_hbm,
    branch_hbm,
    second_hbm,
    tokens,
    cotangent,
    attention,
    share,
    own,
    params,
    mine_hbm,
    twin_hbm,
    block_out,
    mine_out,
    twin_out,
    hidden_out,
    back_out,
    stats_out,
    gate_out,
    sum_out,
    landed_out,
    down,
    up,
    active,
    rect,
    shared_rows,
    part,
    landing,
    staged,
    last,
    total_rows,
    gate_back,
    tile,
    sum_own,
    sum_other,
    sum_landing,
    sum_staged,
    sum_tile,
    send,
    recv,
    load_sems,
    tile_sems,
    twin_sem,
    sum_sems,
):
    micro, rows, width = tokens.shape
    total = rows * size
    units = up.shape[1]
    copies, loads = Copies(send, recv), Loads(load_sems)
    links, column = Links(size, rows, copies), Column(dp_size, copies)
    half = links.half
    here = [pl.ds(m * total, total) for m in range(micro)]
    ring = SumRing(
        column,
        loads,
        mine_hbm,
        twin_hbm,
        sum_out,
        sum_own,
        sum_other,
        sum_landing,
        sum_staged,
        sum_tile,
        sum_sems,
    )
    ring.load()
    down_copies = columns_in(loads, down_hbm, down)
    active_copies = [loads.copy(active_hbm.at[h], active.at[h]) for h in here]
    branch_copies = [loads.copy(branch_hbm.at[h], shared_rows.at[h]) for h in here]
    rect_copy = loads.copy(rect_hbm.at[here[0]], rect)
    up_copy = loads.copy(up_hbm, up)
    stats_out[...] = jnp.zeros_like(stats_out)
    gate_out[...] = jnp.zeros_like(gate_out)
    greet(*links.peers, *column.ring, *column.pair)
    ring.start()
    step = min(512, units)
    tile_cols = min(512, width)
    outs = [
        Scatter(
            links, part, m * total, landing.at[m], staged.at[m], last.at[m], total_rows.at[m]
        )
        for m in range(micro)
    ]
    backs = [
        Scatter(
            links,
            part,
            m * total,
            landing.at[micro + m],
            staged.at[micro + m],
            last.at[micro + m],
            hidden_out.at[m],
        )
        for m in range(micro)
    ]
    wait_all(down_copies)
    for m in range(micro):
        active_copies[m].wait()

        def body(j, _, m=m):
            cols = pl.ds(pl.multiple_of(j * tile_cols, tile_cols), tile_cols)
            part[here[m], cols] = dot(active[here[m], :], down[:, cols]).astype(BF16)
            return 0

        lax.fori_loop(0, width // tile_cols, body, 0)
        outs[m].start()
    for m in range(micro):
        branch_copies[m].wait()
        rect_copy.wait()

        def body(j, _, m=m):
            cols = pl.ds(pl.multiple_of(j * step, step), step)
            back = dot_nt(shared_rows[here[m], :], down[cols, :])
            active[here[m], cols] = (2.0 * rect[:, cols].astype(F32) * back).astype(BF16)
            return 0

        lax.fori_loop(0, units // step, body, 0)
        if m + 1 < micro:
            rect_copy = loads.copy(rect_hbm.at[here[m + 1]], rect)
        if m == 0:
            up_copy.wait()
    second_copies = [loads.copy(second_hbm.at[h], shared_rows.at[h]) for h in here]
    if column.chips > 2:
        ring.advance()
    for m in range(micro):
        outs[m].middle()

        def body(j, _, m=m):
            cols = pl.ds(pl.multiple_of(j * tile_cols, tile_cols), tile_cols)
            part[here[m], cols] = dot_nt(active[here[m], :], up[cols, :]).astype(BF16)
            return 0

        lax.fori_loop(0, width // tile_cols, body, 0)
        backs[m].start()

    def finish_out(m):
        outs[m].finish()

        def body(where, i, row):
            branch = outs[m].chunk(where, i)
            info = own[m, at(row), :]
            live = info[:, LIVE : LIVE + 1]
            outer = cotangent[m, at(row), :].astype(F32) * live
            hidden = tokens[m, at(row), :].astype(F32)
            hidden = hidden + info[:, GATE : GATE + 1] * attention[m, at(row), :]
            gate = NB * jnp.sum(share[m, at(row), :] * info, axis=-1, keepdims=True)
            block_out[m, at(row), :] = (live * (hidden + gate * branch)).astype(BF16)
            value = jnp.sum(outer * branch, axis=-1, keepdims=True)
            gate_back[m, at(row), :] = jnp.broadcast_to(value, (STEP, LANES))

        over_rows(half, body)

    def finish_back(m):
        backs[m].finish()

        def body(where, i, row):
            back = backs[m].chunk(where, i)
            info = own[m, at(row), :]
            portions = share[m, at(row), :]
            live = info[:, LIVE : LIVE + 1]
            outer = cotangent[m, at(row), :].astype(F32) * live
            hidden = tokens[m, at(row), :].astype(F32)
            attended = attention[m, at(row), :]
            hidden = hidden + info[:, GATE : GATE + 1] * attended
            normed, inverse = normalized(hidden)
            gain = params[FEED : FEED + 1, :]
            low = (normed * gain + params[FEED + 1 : FEED + 2, :]).astype(BF16).astype(F32)
            picked = jnp.sum(portions * info, axis=-1, keepdims=True)
            logit_back = NB * picked * (info - portions) * gate_back[m, at(row), :]
            for b in range(NB):
                column = logit_back[:, b : b + 1]
                back = back + column * params[WIDTH_ROUTER + b : WIDTH_ROUTER + b + 1, :]
                stats_out[2 + b : 3 + b, :] += jnp.sum(column * low, axis=0, keepdims=True)
            stats_out[0:1, :] += jnp.sum(back * normed, axis=0, keepdims=True)
            stats_out[1:2, :] += jnp.sum(back, axis=0, keepdims=True)
            hidden_back = outer + norm_back(back, normed, inverse, gain)
            hidden_out[m, at(row), :] = hidden_back
            back_out[m, at(row), :] = (info[:, GATE : GATE + 1] * hidden_back).astype(BF16)
            gate_part = jnp.sum(hidden_back * attended, axis=-1, keepdims=True)
            gate_out[m : m + 1, :] += jnp.sum(info * gate_part, axis=0, keepdims=True)

        over_rows(half, body)

    wait_all(second_copies)
    block = mine_out.shape[1]

    def make(c, ref):
        ref[...] = dot_tn(
            shared_rows[:, pl.ds(pl.multiple_of(c * block, block), block)], active[...]
        ).astype(BF16)

    early, other, staged_up = [up.at[pl.ds(i * block, block)] for i in range(3)]
    up_ring = SumRing(
        column, loads, mine_out, twin_out, None, early, other, landed_out, staged_up, None, None
    )

    def start_up():
        up_ring.load()
        up_ring.start(more=False)

    blocks_out(column, make, tile, mine_out, twin_out, tile_sems, twin_sem, start_up)
    if column.chips > 3:
        ring.advance()
    for m in range(micro):
        finish_out(m)
    for m in range(micro):
        backs[m].middle()
    for m in range(micro):
        finish_back(m)
    ring.finish()
    up_ring.hop.wait()


STATS_ONE = 6
STATS_USE = 12
STATS_ROWS = 16
SEQ_COUNT = 4


def attend_back_kernel(
    dp_size,
    size,
    heads,
    back,
    gate,
    out_hbm,
    qkv_hbm,
    heads_hbm,
    rows_hbm,
    mask_hbm,
    mix_hbm,
    cosine,
    sine,
    row_info,
    mine_hbm,
    twin_hbm,
    landed_hbm,
    tokens,
    hidden_back,
    own,
    seq_info,
    params,
    stats_two,
    usage,
    back_out,
    up_sum,
    mix_sum,
    out_sum,
    stats_out,
    mix_mine,
    mix_twin,
    out_mine,
    out_twin,
    buf,
    out,
    qkv,
    head_rows,
    rows_buf,
    mask,
    heads_back,
    mixed_back,
    score_back,
    shares,
    out_tile,
    mix_tile,
    gates,
    mix,
    landing,
    staged,
    last,
    *rest,
):
    up_bufs, mix_bufs, out_bufs = rest[:5], rest[5:10], rest[10:15]
    stats, share, pieces, sums, whole = rest[15:20]
    send, recv, load_sems = rest[20:23]
    out_sems, out_twin_sem, mix_sems, mix_twin_sem, up_sum_sems, mix_sum_sems, out_sum_sems = rest[23:]
    micro, rows, width = back.shape
    total = rows * size
    copies, loads = Copies(send, recv), Loads(load_sems)
    links, column = Links(size, rows, copies), Column(dp_size, copies)
    half = links.half
    ring = SumRing(column, loads, mine_hbm, twin_hbm, up_sum, *up_bufs, up_sum_sems)
    mix_ring = SumRing(column, loads, mix_mine, mix_twin, mix_sum, *mix_bufs, mix_sum_sems)
    out_ring = SumRing(column, loads, out_mine, out_twin, out_sum, *out_bufs, out_sum_sems)
    ring.prepare(landed_hbm)
    own_copies = []
    for m in range(micro):
        for where in range(2):
            own_copies.append(
                loads.copy(
                    back.at[m, pl.ds(where * half, half)],
                    buf.at[pl.ds(m * total + where * links.second, half)],
                )
            )
    out_copies = [loads.copy(out_hbm, out)]
    qkv_copy = loads.copy(qkv_hbm, qkv)
    mask_copy = loads.copy(mask_hbm, mask)
    heads_copy = loads.copy(heads_hbm, head_rows)
    rows_copy = loads.copy(rows_hbm, rows_buf)
    mix_copy = loads.copy(mix_hbm, mix)
    gates[links.me] = gate[...]
    near = [lax.rem(links.me + s, size) for s in range(1, size)]
    far = [lax.rem(column.me + s, dp_size) for s in range(1, dp_size)]
    greet(*[("tensor", to) for to in near], *[("dp", to) for to in far])
    wait_all(own_copies)
    gathers = [Gather(links, buf, m * total) for m in range(micro)]
    gathers[0].start()
    ring.resume()
    gate_copies = [links.copy(gate, gates.at[links.me], peer) for peer in near]
    stats[...] = jnp.zeros_like(stats)
    stats[0:8, :] = stats_two[...]
    stats[STATS_USE : STATS_USE + 1, 0:LANES] = usage[0:1, :]
    wait_all(out_copies)
    qkv_copy.wait()
    mask_copy.wait()
    scale = HD ** (-0.5)
    chunk = min(128, total)
    gathers[0].middle()
    for g in gathers[1:]:
        g.start()
    block, wide = out_mine.shape[2], out_tile.shape[3]
    here_rows = [pl.ds(m * total, total) for m in range(micro)]
    scatters = [
        Scatter(links, buf, m * total, landing.at[m], staged.at[m], last.at[m], back_out.at[m])
        for m in range(micro)
    ]

    def heads_part(m):
        base = m * total
        every = pl.ds(base, total)
        value = dot_nt(buf[every, :], out[...])
        for h in range(heads):
            here = pl.ds(h * HD, HD)
            heads_back[:, here] = (
                value[:, h * HD : (h + 1) * HD] * row_info[m, :, h : h + 1]
            ).astype(BF16)
        for h in range(heads):
            here = pl.ds(h * HD, HD)

            def some(c, _, m=m, here=here):
                rows_here = pl.ds(pl.multiple_of(c * chunk, chunk), chunk)
                scores = dot_nt(qkv[m, 0, rows_here, here], qkv[m, 1, :, here]) * scale
                scores = scores + mask[m, rows_here, :]
                powers = jnp.exp(scores - jnp.max(scores, axis=-1, keepdims=True))
                share = powers / jnp.sum(powers, axis=-1, keepdims=True)
                share_back = dot_nt(heads_back[rows_here, here], qkv[m, 2, :, here])
                inner = jnp.sum(share * share_back, axis=-1, keepdims=True)
                score_back[rows_here, :] = (share * (share_back - inner)).astype(BF16)
                shares[rows_here, :] = share.astype(BF16)
                return 0

            lax.fori_loop(0, total // chunk, some, 0)
            cos, sin = cosine[m], -sine[m]
            query_back = dot(score_back[...], qkv[m, 1, :, here]) * scale
            keys_back = dot_tn(score_back[...], qkv[m, 0, :, here]) * scale
            values_back = dot_tn(shares[...], heads_back[:, here])
            col = 3 * h * HD
            mixed_back[every, pl.ds(col, HD)] = turned(query_back, cos, sin).astype(BF16)
            mixed_back[every, pl.ds(col + HD, HD)] = turned(keys_back, cos, sin).astype(BF16)
            mixed_back[every, pl.ds(col + 2 * HD, HD)] = values_back.astype(BF16)
            if m == 0 and h == 0:
                for g in gathers[1:]:
                    g.middle()
                if column.chips > 3:
                    ring.advance()

    def make_out(c, put):
        value = dot_tn(head_rows[:, pl.ds(pl.multiple_of(c * wide, wide), wide)], buf[...])
        for j in range(dp_size):
            put(j, value[:, j * block : (j + 1) * block].astype(BF16))

    def make_mix(c, ref):
        ref[...] = dot_tn(
            rows_buf[:, pl.ds(pl.multiple_of(c * block, block), block)], mixed_back[...]
        ).astype(BF16)

    tile = min(512, width)

    def first_part(m):
        def body(j, _):
            cols = pl.ds(pl.multiple_of(j * tile, tile), tile)
            buf[here_rows[m], cols] = dot_nt(mixed_back[here_rows[m], :], mix[cols, :]).astype(BF16)
            return 0

        lax.fori_loop(0, width // tile, body, 0)
        scatters[m].start()

    gathers[0].finish()
    heads_part(0)
    for g in gathers[1:]:
        g.finish()
    heads_copy.wait()
    halves_out(
        column,
        heads * HD // wide,
        make_out,
        out_tile,
        out_mine,
        out_twin,
        out_sems,
        out_twin_sem,
    )
    out_ring.load()
    out_ring.start()
    mix_copy.wait()
    first_part(0)
    for m in range(1, micro):
        heads_part(m)
    scatters[0].middle()
    if column.chips > 2:
        out_ring.advance()
    rows_copy.wait()

    def start_mix():
        mix_ring.load()
        mix_ring.start(more=False)

    blocks_out(column, make_mix, mix_tile, mix_mine, mix_twin, mix_sems, mix_twin_sem, start_mix)
    mix_ring.load()
    if column.chips > 3:
        out_ring.advance()
    for m in range(1, micro):
        first_part(m)
    for made in gate_copies:
        made.wait()
    gate_sum = gates[0]
    for r in range(1, size):
        gate_sum = gate_sum + gates[r]

    def last_rows(m):
        s = scatters[m]
        s.finish()
        count = SEQ_COUNT
        lane = lax.broadcasted_iota(jnp.int32, (8, LANES), 1)
        which = lax.broadcasted_iota(jnp.int32, (8, LANES), 0)
        info = seq_info[m]
        gate_back = jnp.where(lane == SEQ + which, gate_sum[m : m + 1, :], 0.0)
        gate_back = jnp.sum(gate_back, axis=-1, keepdims=True)
        chosen = jnp.where(lane == info[:, CHOSEN : CHOSEN + 1].astype(jnp.int32), 1.0, 0.0)
        logit_back = NHC * info[:, PICKED : PICKED + 1] * (chosen - info) * gate_back
        logit_back = logit_back / info[:, DIVISOR : DIVISOR + 1]

        def body(where, i, row):
            back = s.chunk(where, i)
            normed, inverse = normalized(tokens[m, at(row), :].astype(F32))
            gain = params[ATTEND : ATTEND + 1, :]
            low = (normed * gain + params[ATTEND + 1 : ATTEND + 2, :]).astype(BF16).astype(F32)
            rows_info = own[m, at(row), :]
            spread = jnp.zeros((STEP, LANES), F32)
            for q in range(count):
                spread = spread + rows_info[:, SEQ + q : SEQ + q + 1] * logit_back[q : q + 1, :]
            for c in range(NHC):
                part = spread[:, c : c + 1]
                back = back + part * params[HEAD_ROUTER + c : HEAD_ROUTER + c + 1, :]
                at_row = STATS_ONE + 2 + c
                stats[at_row : at_row + 1, :] += jnp.sum(part * low, axis=0, keepdims=True)
            at_row = STATS_ONE
            stats[at_row : at_row + 1, :] += jnp.sum(back * normed, axis=0, keepdims=True)
            stats[at_row + 1 : at_row + 2, :] += jnp.sum(back, axis=0, keepdims=True)
            value = norm_back(back, normed, inverse, gain)
            back_out[m, at(row), :] = hidden_back[m, at(row), :] + value

        over_rows(links.half, body)

    last_rows(0)
    if column.chips > 2:
        mix_ring.advance()
    for s in scatters[1:]:
        s.middle()
    ring.finish()
    for m in range(1, micro):
        last_rows(m)

    piece = width // size
    mine = pl.ds(pl.multiple_of(links.me * piece, piece), piece)
    sent = [
        links.copy(
            stats.at[:, pl.ds(pl.multiple_of(to * piece, piece), piece)], pieces.at[links.me], to
        )
        for to in near
    ]
    pieces[links.me] = stats[:, mine]
    wait_all(sent)
    value = pieces[0]
    for r in range(1, size):
        value = value + pieces[r]
    share[0] = value
    sums[column.me] = value
    sent = [column.copy(share.at[0], sums.at[column.me], to) for to in far]
    if column.chips > 3:
        mix_ring.advance()
    out_ring.finish()
    wait_all(sent)
    value = sums[0]
    for r in range(1, dp_size):
        value = value + sums[r]
    share[1] = value
    whole[links.me] = value
    wait_all([links.copy(share.at[1], whole.at[links.me], to) for to in near])
    for r in range(size):
        stats_out[:, r * piece : (r + 1) * piece] = whole[r]
    mix_ring.finish()


ANY = pl.BlockSpec(memory_space=pl.ANY)
VMEM = pl.BlockSpec(memory_space=pltpu.VMEM)
SMEM = pl.BlockSpec(memory_space=pltpu.SMEM)


def call(kernel, ident, ins, outs, scratch, copies, loads, extra=(), flops=0, limit=56):
    dma = pltpu.SemaphoreType.DMA
    sems = [dma((copies,)), dma((copies,)), dma((loads,))] + [dma((n,)) for n in extra]
    moved = sum(a.size * a.dtype.itemsize for a, _ in ins)
    return pl.pallas_call(
        kernel,
        out_shape=[jax.ShapeDtypeStruct(shape, kind) for shape, kind, _ in outs],
        in_specs=[SMEM if near == "s" else VMEM if near else ANY for _, near in ins],
        out_specs=[VMEM if near else ANY for _, _, near in outs],
        scratch_shapes=[pltpu.VMEM(shape, kind) for shape, kind in scratch] + sems,
        compiler_params=pltpu.CompilerParams(
            collective_id=ident, has_side_effects=True, vmem_limit_bytes=limit * MIB
        ),
        cost_estimate=pl.CostEstimate(flops=flops, bytes_accessed=moved, transcendentals=0),
    )(*[a for a, _ in ins])


def local(
    dp_size,
    size,
    tokens,
    cotangent,
    mixer,
    merger,
    expand,
    shrink,
    attend_gain,
    attend_bias,
    feed_gain,
    feed_bias,
    width_router,
    head_router,
    lengths,
    head_choice,
    width_bucket,
):
    micro, rows, width = tokens.shape
    total = width_bucket.shape[1]
    every = micro * total
    half = rows // 2
    high = size // 2
    heads = merger.shape[0] // HD
    units = expand.shape[1]
    block = width // dp_size
    chips = dp_size // 2
    few = transfers(size)
    ringed = ring_copies(dp_size)

    vectors = jnp.concatenate([attend_gain, attend_bias, feed_gain, feed_bias]).reshape(4, width)
    params = jnp.concatenate(
        [vectors, jnp.concatenate([width_router, head_router], axis=1).T], axis=0
    ).astype(F32)
    rates = jnp.power(10000.0, -2.0 * jnp.arange(HD // 2, dtype=F32) / HD)
    rates = jnp.concatenate([rates, rates])[None]

    tables = (micro, total, LANES)
    lands = half * (2 * (high - 1) + high)
    stages = half * high
    wide_heads = heads * HD
    span = 3 * wide_heads
    buffers = [((micro, lands, width), BF16), ((micro, stages, width), BF16), ((micro, stages, width), BF16)]
    attended = call(
        functools.partial(attend_kernel, dp_size, size, heads, units),
        2,
        [
            (tokens, True),
            (cotangent, True),
            (params, True),
            (rates, True),
            (width_bucket, True),
            (lengths, "s"),
            (head_choice, "s"),
            (mixer, False),
            (merger, False),
            (expand, False),
            (shrink, False),
        ],
        [
            ((every, width), BF16, False),
            ((width, span), BF16, False),
            ((wide_heads, width), BF16, False),
            ((micro, total, total), F32, True),
            (tables, F32, True),
            (tables, F32, True),
            (tables, F32, True),
            ((micro, rows, LANES), F32, True),
            ((micro, 8, LANES), F32, True),
            ((8, LANES), F32, True),
            ((micro, 3, total, wide_heads), BF16, False),
            ((every, wide_heads), BF16, False),
            ((micro, rows, width), F32, True),
            ((every, width), BF16, False),
            ((micro, rows, LANES), F32, True),
            ((width, units), BF16, False),
            ((dp_size, units, block), BF16, False),
            ((every, units), BF16, False),
            ((every, units), BF16, False),
            ((every, width), BF16, False),
            ((chips, units, block), BF16, False),
            ((chips, units, block), BF16, False),
        ],
        [
            ((every, width), BF16),
            ((total, LANES), jnp.int32),
            (tables, jnp.int32),
            (tables, F32),
            ((width, span), BF16),
            ((wide_heads, width), BF16),
            ((micro, 3, total, wide_heads), BF16),
            ((every, wide_heads), BF16),
            ((every, width), BF16),
        ]
        + buffers
        + [
            ((every, width), BF16),
            ((width, units), BF16),
            ((every, width), BF16),
            ((2, 2, chips, min(256, units), block), BF16),
        ],
        4 * micro * few + 4 * ringed,
        4 + micro + 2 + 2 + micro + 1 + 3 * micro,
        (4, 1),
        flops=2 * every * width * (span + wide_heads + 2 * units),
        limit=63,
    )
    first_rows, mix_weight, out_weight, mask, cosine, sine, row_info = attended[:7]
    own, seq_info, usage, qkv, head_rows, attention, second_rows = attended[7:14]
    width_share, up_weight, down_weight, rect, active, branch_rows = attended[14:20]
    down_mine, down_twin = attended[20:]

    narrowed = call(
        functools.partial(narrow_kernel, dp_size, size),
        4,
        [
            (down_weight, False),
            (up_weight, False),
            (active, False),
            (rect, False),
            (branch_rows, False),
            (second_rows, False),
            (tokens, True),
            (cotangent, True),
            (attention, True),
            (width_share, True),
            (own, True),
            (params, True),
            (down_mine, False),
            (down_twin, False),
        ],
        [
            ((micro, rows, width), BF16, True),
            ((chips, block, units), BF16, False),
            ((chips, block, units), BF16, False),
            ((micro, rows, width), F32, True),
            ((micro, rows, width), BF16, True),
            ((8, width), F32, True),
            ((8, LANES), F32, True),
            ((units, block), F32, False),
            ((1, block, units), BF16, False),
        ],
        [
            ((units, width), BF16),
            ((width, units), BF16),
            ((every, units), BF16),
            ((total, units), BF16),
            ((every, width), BF16),
            ((every, width), BF16),
            ((2 * micro, lands, width), BF16),
            ((2 * micro, stages, width), BF16),
            ((2 * micro, stages, width), BF16),
            ((micro, rows, width), F32),
            ((micro, rows, LANES), F32),
            ((2, block, units), BF16),
        ]
        + sum_scratch(chips, units, block),
        2 * micro * few + chips,
        dp_size + 4 * micro + 1 + 2 * chips + 2,
        (2, chips, SUM_TILES),
        flops=8 * every * width * units,
        limit=63,
    )
    block_output, up_mine, up_twin, hidden_back, back_own, stats_two, gate_part = narrowed[:7]
    down_sum, up_landed = narrowed[7:]

    out_tile = min(256, wide_heads)
    lasts = call(
        functools.partial(attend_back_kernel, dp_size, size, heads),
        5,
        [
            (back_own, False),
            (gate_part, True),
            (out_weight, False),
            (qkv, False),
            (head_rows, False),
            (first_rows, False),
            (mask, False),
            (mix_weight, False),
            (cosine, True),
            (sine, True),
            (row_info, True),
            (up_mine, False),
            (up_twin, False),
            (up_landed, False),
            (tokens, True),
            (hidden_back, True),
            (own, True),
            (seq_info, True),
            (params, True),
            (stats_two, True),
            (usage, True),
        ],
        [
            ((micro, rows, width), F32, True),
            ((block, units), F32, False),
            ((block, span), F32, False),
            ((wide_heads, block), F32, False),
            ((STATS_ROWS, width), F32, True),
            ((chips, block, span), BF16, False),
            ((chips, block, span), BF16, False),
            ((chips, wide_heads, block), BF16, False),
            ((chips, wide_heads, block), BF16, False),
        ],
        [
            ((every, width), BF16),
            ((wide_heads, width), BF16),
            ((micro, 3, total, wide_heads), BF16),
            ((every, wide_heads), BF16),
            ((every, width), BF16),
            ((micro, total, total), F32),
            ((total, wide_heads), BF16),
            ((every, span), BF16),
            ((total, total), BF16),
            ((total, total), BF16),
            ((2, 2, chips, out_tile, block), BF16),
            ((2, block, span), BF16),
            ((size, 8, LANES), F32),
            ((width, span), BF16),
        ]
        + buffers
        + sum_scratch(chips, block, units)
        + sum_scratch(chips, block, span)
        + sum_scratch(chips, wide_heads, block)
        + [
            ((STATS_ROWS, width), F32),
            ((2, STATS_ROWS, width // size), F32),
            ((size, STATS_ROWS, width // size), F32),
            ((dp_size, STATS_ROWS, width // size), F32),
            ((size, STATS_ROWS, width // size), F32),
        ],
        2 * micro * few + 3 * (size - 1) + dp_size - 1 + 3 * (chips - 1),
        2 * micro + dp_size + 6 + 6 * chips,
        (4, 1, 2, chips, SUM_TILES, SUM_TILES, SUM_TILES),
        flops=4 * every * width * (wide_heads + span) + 20 * heads * micro * total * total * HD,
        limit=63,
    )
    tokens_gradient, up_sum, mix_sum, out_sum, stats = lasts[:5]
    return (
        block_output,
        tokens_gradient,
        mix_sum,
        out_sum,
        up_sum,
        down_sum,
        stats[STATS_ONE],
        stats[STATS_ONE + 1],
        stats[0],
        stats[1],
        stats[2 : 2 + NB].T,
        stats[STATS_ONE + 2 : STATS_ONE + 2 + NHC].T,
        stats[STATS_USE, :NB],
        stats[STATS_USE, CHOICE : CHOICE + NHC],
    )


def solution(mesh):
    def run(*args):
        return local(mesh.shape["dp"], mesh.shape["tensor"], *args)

    rows = P(None, ("dp", "tensor"), None)
    tall, wide = P("dp", "tensor"), P("tensor", "dp")
    weights = (tall, wide, tall, wide)
    return jax.shard_map(
        run,
        mesh=mesh,
        in_specs=(rows, rows) + weights + (P(),) * 6 + (P(None, "dp"),) * 3,
        out_specs=(rows, rows) + weights + (P(),) * 8,
        check_vma=False,
    )
```

```python
import functools

import jax
import jax.numpy as jnp
from jax import lax
from jax.experimental import pallas as pl
from jax.experimental.pallas import tpu as pltpu
from jax.sharding import PartitionSpec as P

H = 16
HD = 128
FF = 8192
NB = 4
NHC = 4

EPSILON = 1e-05
HIGHEST = lax.Precision.HIGHEST
MASKED = -1e30
BF16 = jnp.bfloat16
F32 = jnp.float32
MESH = pl.DeviceIdType.MESH
MIB = 1024 * 1024
LANES = 128
STEP = 16

GATE = 4
LIVE = 5
SEQ = 8
CHOICE = 16

PICKED = 4
DIVISOR = 5
CHOSEN = 6

ATTEND = 0
FEED = 2
WIDTH_ROUTER = 4
HEAD_ROUTER = 8


def dot(left, right):
    return jnp.dot(left, right, preferred_element_type=F32)


def dot_nt(left, right):
    return lax.dot_general(left, right, (((1,), (1,)), ((), ())), preferred_element_type=F32)


def dot_tn(left, right):
    return lax.dot_general(left, right, (((0,), (0,)), ((), ())), preferred_element_type=F32)


def at(start, size=STEP):
    return pl.ds(pl.multiple_of(start, STEP), size)


class Copies:
    def __init__(self, send_sems, recv_sems):
        self.send_sems, self.recv_sems, self.used = send_sems, recv_sems, 0

    def start(self, src, dst, axis, to):
        made = pltpu.make_async_remote_copy(
            src_ref=src,
            dst_ref=dst,
            send_sem=self.send_sems.at[self.used],
            recv_sem=self.recv_sems.at[self.used],
            device_id={axis: to},
            device_id_type=MESH,
        )
        self.used += 1
        made.start()
        return made


def greet(*peers):
    barrier = pltpu.get_barrier_semaphore()
    for axis, to in peers:
        pl.semaphore_signal(barrier, inc=1, device_id={axis: to}, device_id_type=MESH)
    pl.semaphore_wait(barrier, len(peers))


class Links:
    def __init__(self, size, rows, copies):
        me = lax.axis_index("tensor")
        hi, lo = me // 2, me % 2
        self.me, self.size, self.high, self.half = me, size, size // 2, rows // 2
        self.near = hi * 2 + (1 - lo)
        self.ahead = [lax.rem(hi + s, self.high) * 2 + lo for s in range(self.high)]
        self.behind = [
            lax.rem(hi + self.high - s, self.high) * 2 + lo for s in range(self.high)
        ]
        self.second = self.half * size
        self.copies = copies
        steps = range(self.high)
        grid = [[lax.rem(hi + s, self.high) * 2 + (lo + l) % 2 for l in range(2)] for s in steps]
        self.first_ranks = [grid[s][l] for s in steps for l in range(2)]
        self.second_ranks = [grid[s][l] for l in range(2) for s in steps]
        self.peers = [("tensor", to) for to in [self.near] + self.ahead[1:]]

    def copy(self, src, dst, to):
        return self.copies.start(src, dst, "tensor", to)


class Column:
    def __init__(self, size, copies):
        self.me, self.chips, self.copies = lax.axis_index("dp"), size // 2, copies
        self.chip, self.core = self.me // 2, self.me % 2
        self.twin = self.chip * 2 + 1 - self.core
        self.right = self.block(1)
        self.left = self.block(-1)
        self.ring = [("dp", self.left)]
        self.pair = [("dp", self.twin)]

    def chip_at(self, step):
        return lax.rem(self.chip + self.chips + step, self.chips)

    def block(self, step):
        return self.chip_at(step) * 2 + self.core

    def copy(self, src, dst, to):
        return self.copies.start(src, dst, "dp", to)


class WeightRing:
    def __init__(self, column, loads, own, slot):
        self.column, self.loads, self.own, self.slot = column, loads, own, slot

    def start(self):
        k = self.column
        here = self.slot(k.me)
        self.hops = [k.copy(self.own, here, k.right)]
        self.twins = [k.copy(self.own, here, k.twin)]
        self.local = self.loads.copy(self.own, here)

    def advance(self):
        k = self.column
        step = len(self.twins)
        self.hops[step - 1].wait_recv()
        here = self.slot(k.block(-step))
        if step < k.chips - 1:
            self.hops.append(k.copy(here, here, k.right))
        self.twins.append(k.copy(here, here, k.twin))

    def advance_all(self):
        while len(self.twins) < self.column.chips:
            self.advance()

    def finish(self):
        self.advance_all()
        for made in self.twins:
            made.wait()
        for made in self.hops:
            made.wait_send()
        self.local.wait()


def ring_copies(size):
    return size // 2 * 2 - 1


class SumRing:
    def __init__(self, column, loads, mine, twin, target, own, other, landing, staged, tile, tile_sems):
        self.column, self.loads = column, loads
        self.mine, self.twin, self.target = mine, twin, target
        self.own, self.other, self.landing, self.staged = own, other, landing, staged
        self.tile, self.tile_sems = tile, tile_sems
        self.sent = 0
        self.rows = sum_rows(own.shape[1])

    def load(self):
        block = self.column.chip_at(-1 - self.sent)
        self.loading = [
            self.loads.copy(self.mine.at[block], self.own),
            self.loads.copy(self.twin.at[block], self.other),
        ]

    def send(self, landed, more=True):
        k, rows = self.column, self.rows

        def body(i, _):
            here = pl.ds(pl.multiple_of(i * rows, rows), rows)
            value = self.own[here, :].astype(F32) + self.other[here, :].astype(F32)
            if landed is not None:
                value = value + self.landing[landed, here, :].astype(F32)
            self.staged[here, :] = value.astype(BF16)
            return 0

        lax.fori_loop(0, self.own.shape[0] // rows, body, 0)
        self.hop = k.copy(self.staged, self.landing.at[self.sent], k.right)
        self.sent += 1
        if more:
            self.load()

    def start(self, more=True):
        wait_all(self.loading)
        self.send(None, more)

    def prepare(self, landed):
        self.sent = 1
        self.load()
        self.loading.append(self.loads.copy(landed.at[0], self.landing.at[0]))

    def resume(self):
        wait_all(self.loading)
        self.send(0)

    def advance(self):
        self.hop.wait()
        wait_all(self.loading)
        self.send(self.sent - 1)

    def finish(self):
        k, rows = self.column, self.rows
        while self.sent < k.chips - 1:
            self.advance()
        self.hop.wait()
        wait_all(self.loading)
        landed = k.chips - 2
        slots = self.tile.shape[0]

        def body(i, _):
            here = pl.ds(pl.multiple_of(i * rows, rows), rows)
            slot = lax.rem(i, slots)
            copy = pltpu.make_async_copy(
                self.tile.at[slot], self.target.at[here], self.tile_sems.at[slot]
            )

            @pl.when(i >= slots)
            def _():
                copy.wait()

            value = self.own[here, :].astype(F32) + self.other[here, :].astype(F32)
            self.tile[slot] = value + self.landing[landed, here, :].astype(F32)
            copy.start()
            return 0

        count = self.own.shape[0] // rows
        lax.fori_loop(0, count, body, 0)
        for i in range(max(count - slots, 0), count):
            here = pl.ds(i * rows, rows)
            slot = i % slots
            pltpu.make_async_copy(
                self.tile.at[slot], self.target.at[here], self.tile_sems.at[slot]
            ).wait()


SUM_TILES = 4


def sum_rows(width):
    return 128 if width <= 256 else 16


def sum_scratch(chips, rows, width):
    return [
        ((rows, width), BF16),
        ((rows, width), BF16),
        ((chips - 1, rows, width), BF16),
        ((rows, width), BF16),
        ((SUM_TILES, sum_rows(width), width), F32),
    ]


def transfers(size):
    return 2 * (size // 2)


class Gather:
    def __init__(self, links, buf, base):
        self.links, self.buf, self.base = links, buf, base

    def rows(self, start, count):
        return self.buf.at[pl.ds(self.base + start, count)]

    def start(self):
        k, half, second = self.links, self.links.half, self.links.second
        self.first_near = k.copy(self.rows(0, half), self.rows(half, half), k.near)
        self.second_far = [
            k.copy(self.rows(second, half), self.rows(second + s * half, half), k.behind[s])
            for s in range(1, k.high)
        ]

    def middle(self):
        k, half, second = self.links, self.links.half, self.links.second
        self.first_near.wait_recv()
        self.first_far = [
            k.copy(self.rows(0, 2 * half), self.rows(2 * half * s, 2 * half), k.behind[s])
            for s in range(1, k.high)
        ]
        for made in self.second_far:
            made.wait_recv()
        block = k.high * half
        self.second_near = k.copy(self.rows(second, block), self.rows(second + block, block), k.near)

    def finish(self):
        for made in self.first_far + [self.second_near]:
            made.wait_recv()
        for made in [self.first_near, self.second_near] + self.first_far + self.second_far:
            made.wait_send()


class Scatter:
    def __init__(self, links, part, base, landing, staged, last, total):
        self.links, self.part, self.base = links, part, base
        self.landing, self.staged, self.last, self.total = landing, staged, last, total

    def start(self):
        k, half = self.links, self.links.half
        block = k.high * half
        self.first_far = [
            k.copy(
                self.part.at[pl.ds(self.base + 2 * half * s, 2 * half)],
                self.landing.at[pl.ds(2 * half * (s - 1), 2 * half)],
                k.ahead[s],
            )
            for s in range(1, k.high)
        ]
        self.second_near = k.copy(
            self.part.at[pl.ds(self.base + k.second + block, block)],
            self.landing.at[pl.ds(2 * half * (k.high - 1), block)],
            k.near,
        )

    def middle(self):
        k, half, base = self.links, self.links.half, self.base
        steps = half // STEP
        for made in self.first_far:
            made.wait_recv()

        def first(i, _):
            for where in range(2):
                row = where * half + i * STEP
                value = self.part[at(base + row), :].astype(F32)
                for s in range(1, k.high):
                    value = value + self.landing[at(2 * half * (s - 1) + row), :].astype(F32)
                if where == 0:
                    self.total[at(i * STEP), :] = value
                else:
                    self.staged[at(i * STEP), :] = value.astype(BF16)
            return 0

        lax.fori_loop(0, steps, first, 0)
        self.first_near = k.copy(
            self.staged.at[pl.ds(0, half)], self.last.at[pl.ds(0, half)], k.near
        )
        self.second_near.wait_recv()
        landed = 2 * half * (k.high - 1)

        def second(i, _):
            for s in range(k.high):
                row = s * half + i * STEP
                value = self.part[at(base + k.second + row), :].astype(F32)
                value = value + self.landing[at(landed + row), :].astype(F32)
                if s == 0:
                    self.total[at(half + i * STEP), :] = value
                else:
                    self.staged[at(row), :] = value.astype(BF16)
            return 0

        lax.fori_loop(0, steps, second, 0)
        self.second_far = [
            k.copy(
                self.staged.at[pl.ds(half * s, half)], self.last.at[pl.ds(half * s, half)], k.ahead[s]
            )
            for s in range(1, k.high)
        ]
        for made in self.first_far + [self.second_near]:
            made.wait_send()

    def finish(self):
        for made in [self.first_near] + self.second_far:
            made.wait_recv()
            made.wait_send()

    def chunk(self, where, i):
        k, half = self.links, self.links.half
        value = self.total[at(where * half + i * STEP), :]
        if where == 0:
            return value + self.last[at(i * STEP), :].astype(F32)
        for s in range(1, k.high):
            value = value + self.last[at(half * s + i * STEP), :].astype(F32)
        return value


def over_rows(half, body):
    for where in range(2):

        def inner(i, _, where=where):
            body(where, i, where * half + i * STEP)
            return 0

        lax.fori_loop(0, half // STEP, inner, 0)


class Loads:
    def __init__(self, sems):
        self.sems, self.used = sems, 0

    def copy(self, src, dst):
        made = pltpu.make_async_copy(src, dst, self.sems.at[self.used])
        self.used += 1
        made.start()
        return made


def wait_all(*groups):
    for group in groups:
        for made in group if isinstance(group, list) else [group]:
            made.wait()


def columns_in(loads, blocks, flat):
    count, _, width = blocks.shape
    return [loads.copy(blocks.at[j], flat.at[:, pl.ds(j * width, width)]) for j in range(count)]


def halves_out(column, count, make, tile, mine, twin, sems, twin_sem, between=None):
    wide = tile.shape[3]

    def outs(c, slot):
        here = pl.ds(pl.multiple_of(c * wide, wide), wide)
        local = pltpu.make_async_copy(tile.at[slot, 0], mine.at[:, here, :], sems.at[slot])
        away = pltpu.make_async_remote_copy(
            src_ref=tile.at[slot, 1],
            dst_ref=twin.at[:, here, :],
            send_sem=sems.at[2 + slot],
            recv_sem=twin_sem.at[0],
            device_id={"dp": column.twin},
            device_id_type=MESH,
        )
        return local, away

    def body(c, _):
        slot = lax.rem(c, 2)
        local, away = outs(c, slot)

        @pl.when(c >= 2)
        def _():
            local.wait()
            away.wait_send()

        def put(block, value):
            tile[slot, lax.rem(block + column.core, 2), block // 2] = value

        make(c, put)
        local.start()
        away.start()
        return 0

    lax.fori_loop(0, count // 2, body, 0)
    if between is not None:
        between()
    lax.fori_loop(count // 2, count, body, 0)
    for c in range(max(count - 2, 0), count):
        local, away = outs(c, c % 2)
        local.wait()
        away.wait_send()
    all_landed(column, twin, sems, twin_sem)


def blocks_out(column, make, tile, mine, twin, sems, twin_sems, ring):
    def local_copy(i):
        chip = column.chip_at(-1 - i)
        return pltpu.make_async_copy(tile.at[0], mine.at[chip], sems.at[0])

    def away_copy(i):
        return pltpu.make_async_remote_copy(
            src_ref=tile.at[1],
            dst_ref=twin.at[column.chip_at(-1 - i)],
            send_sem=sems.at[1],
            recv_sem=twin_sems.at[i],
            device_id={"dp": column.twin},
            device_id_type=MESH,
        )

    def body(i, _):
        chip, local, away = column.chip_at(-1 - i), local_copy(i), away_copy(i)

        @pl.when(i > 0)
        def _():
            away.wait_send()

        make(2 * chip + 1 - column.core, tile.at[1])
        away.start()

        @pl.when(i > 1)
        def _():
            local.wait()

        make(2 * chip + column.core, tile.at[0])
        local.start()
        return 0

    lax.fori_loop(0, 1, body, 0)
    local_copy(0).wait()
    away_copy(0).wait_recv()
    ring()
    lax.fori_loop(1, column.chips, body, 0)
    for i in range(1, column.chips):
        away_copy(i).wait_recv()
    local_copy(column.chips - 1).wait()
    away_copy(column.chips - 1).wait_send()


def all_landed(column, twin, sems, twin_sem):
    pltpu.make_async_remote_copy(
        src_ref=twin,
        dst_ref=twin,
        send_sem=sems.at[0],
        recv_sem=twin_sem.at[0],
        device_id={"dp": column.twin},
        device_id_type=MESH,
    ).wait_recv()


def normalized(value):
    centred = value - jnp.mean(value, axis=-1, keepdims=True)
    inverse = lax.rsqrt(jnp.mean(centred * centred, axis=-1, keepdims=True) + EPSILON)
    return centred * inverse, inverse


def norm_back(back, normed, inverse, gain):
    scaled = back * gain
    inner = jnp.mean(scaled, axis=-1, keepdims=True)
    along = jnp.mean(scaled * normed, axis=-1, keepdims=True)
    return inverse * (scaled - inner - normed * along)


def softmax_lanes(logits, lanes):
    logits = jnp.where(lanes, logits, MASKED)
    powers = jnp.exp(logits - jnp.max(logits, axis=-1, keepdims=True))
    return jnp.where(lanes, powers / jnp.sum(powers, axis=-1, keepdims=True), 0.0)


def turned(value, cosine, sine):
    return value * cosine + pltpu.roll(value, HD // 2, 1) * sine


def attend_kernel(
    dp_size,
    size,
    heads,
    units,
    tokens,
    cotangent,
    params,
    rates,
    bucket,
    lengths,
    choices,
    mixer,
    merger,
    expand,
    shrink,
    rows_out,
    mix_out,
    out_out,
    mask,
    cosine,
    sine,
    row_info,
    own,
    seq_info,
    usage,
    qkv_out,
    heads_out,
    attention_out,
    second_out,
    share_out,
    up_out,
    down_out,
    rect_out,
    active_out,
    branch_out,
    mine_out,
    twin_out,
    rows_buf,
    slot_col,
    member_col,
    bucket_col,
    mix,
    out,
    qkv,
    head_rows,
    part,
    landing,
    staged,
    last,
    second_buf,
    up,
    branch_buf,
    tile_out,
    send,
    recv,
    load_sems,
    tile_sems,
    twin_sem,
):
    micro, rows, width = tokens.shape
    count = lengths.shape[1]
    rect, active = rows_buf, part
    total = rows * size
    copies, loads = Copies(send, recv), Loads(load_sems)
    links, column = Links(size, rows, copies), Column(dp_size, copies)
    half = links.half
    block = mixer.shape[0]
    greet(*links.peers, *column.ring, *column.pair)
    mix_ring = WeightRing(
        column, loads, mixer, lambda i: mix.at[pl.ds(pl.multiple_of(i * block, block), block)]
    )
    out_ring = WeightRing(
        column,
        loads,
        merger,
        lambda i: out.at[:, pl.ds(pl.multiple_of(i * block, block), block)],
    )
    mix_ring.start()
    first_gathers = []
    for m in range(micro):

        def body(where, i, row, m=m):
            value = tokens[m, at(row), :].astype(F32)
            low = normalized(value)[0] * params[ATTEND : ATTEND + 1, :]
            low = (low + params[ATTEND + 1 : ATTEND + 2, :]).astype(BF16)
            rows_buf[at(m * total + where * links.second + i * STEP), :] = low

        over_rows(links.half, body)
        first_gathers.append(Gather(links, rows_buf, m * total))
        first_gathers[m].start()

    starts = [r * rows for r in links.first_ranks] + [r * rows + half for r in links.second_ranks]

    def slots(shape, dimension):
        index = lax.broadcasted_iota(jnp.int32, shape, dimension)
        offset = jnp.full(shape, starts[0], jnp.int32)
        for k in range(1, len(starts)):
            offset = jnp.where(index >= k * half, starts[k] - k * half, offset)
        return index + offset

    def ends(m):
        found, end = [], 0
        for s in range(count):
            end = end + lengths[m, s]
            found.append(end)
        return found

    def members(m, slot):
        member = jnp.zeros(slot.shape, jnp.int32)
        begin = jnp.zeros(slot.shape, jnp.int32)
        for end in ends(m):
            member = member + jnp.where(slot >= end, 1, 0)
            begin = jnp.where(slot >= end, end, begin)
        return member, slot - begin

    def by_member(member, values, other):
        value = jnp.full(member.shape, other)
        for s in range(count):
            value = jnp.where(member == s, values[s], value)
        return value

    chunk = min(128, total)
    lane = lax.broadcasted_iota(jnp.int32, (chunk, LANES), 1)
    slot_row = slots((8, total), 1)
    slot_col[...] = slots((total, LANES), 0)
    member_rows = [members(m, slot_row)[0] for m in range(micro)]
    for m in range(micro):

        def table(c, _, m=m):
            here = pl.ds(pl.multiple_of(c * chunk, chunk), chunk)
            slot = slot_col[here, :]
            member, place = members(m, slot)
            member_col[m, here, :] = member
            seen = (member[:, :1] == member_rows[m][:1, :]) & (slot[:, :1] >= slot_row[:1, :])
            mask[m, here, :] = jnp.where(seen, 0.0, MASKED)
            angle = place.astype(F32) * rates[...]
            turn = jnp.sin(angle)
            cosine[m, here, :] = jnp.cos(angle)
            sine[m, here, :] = jnp.where(lane < HD // 2, -turn, turn)
            natural = lax.broadcasted_iota(jnp.int32, (chunk, total), 1)
            picked = jnp.where(slot[:, :1] == natural, bucket[m : m + 1, :].astype(F32), 0.0)
            bucket_here = jnp.sum(picked, axis=-1, keepdims=True)
            bucket_col[m, here, :] = jnp.broadcast_to(bucket_here, (chunk, LANES))
            used = by_member(member, [H // NHC * (choices[m, s] + 1) for s in range(count)], 0)
            head_on = jnp.where(links.me * heads + lane < used, 1.0, 0.0)
            first_unit = jnp.full(lane.shape, links.me * units, jnp.int32).astype(F32)
            unit_on = jnp.where(first_unit < FF // NB * (bucket_here + 1.0), 1.0, 0.0)
            row_info[m, here, :] = jnp.where(
                lane < heads, head_on, jnp.where(lane == heads, unit_on, 0.0)
            )
            return 0

        lax.fori_loop(0, total // chunk, table, 0)
    for g in first_gathers:
        g.middle()
    mix_ring.advance()
    outs, rows_saves = [], []
    usage[...] = jnp.zeros_like(usage)
    few = lax.broadcasted_iota(jnp.int32, (8, LANES), 1)
    which = lax.broadcasted_iota(jnp.int32, (8, LANES), 0)
    lane_own = lax.broadcasted_iota(jnp.int32, (half, LANES), 1)
    for m, g in enumerate(first_gathers):
        g.finish()
        here = pl.ds(m * total, total)
        rows_saves.append(loads.copy(rows_buf.at[here], rows_out.at[here]))
        sequence = lax.broadcasted_iota(jnp.int32, (8, total), 0)
        hot = jnp.where(member_rows[m] == sequence, 1.0, 0.0).astype(BF16)
        divisor = jnp.maximum(by_member(which, [lengths[m, s] for s in range(count)], 0), 1)
        divisor = divisor.astype(F32)
        chosen = by_member(which, [choices[m, s] for s in range(count)], 0)
        means = dot(hot, rows_buf[here, :]) / divisor[:, :1]
        logits = jnp.full((8, LANES), MASKED)
        for c in range(NHC):
            router = params[HEAD_ROUTER + c : HEAD_ROUTER + c + 1, :]
            logit = jnp.sum(means * router, axis=-1, keepdims=True)
            logits = jnp.where(few == c, logit, logits)
        share = softmax_lanes(logits, few < NHC)
        picked = jnp.sum(jnp.where(few == chosen, share, 0.0), axis=-1, keepdims=True)
        table = jnp.where(few == PICKED, picked, share)
        table = jnp.where(few == DIVISOR, divisor, table)
        seq_info[m] = jnp.where(few == CHOSEN, chosen.astype(F32), table)
        for where in range(2):
            source = pl.ds(where * links.second, half)
            member = member_col[m, source, :]
            gate = by_member(member, [NHC * picked[s : s + 1, :] for s in range(count)], 0.0)
            choice = by_member(member, [choices[m, s] for s in range(count)], -NHC)
            live = jnp.where(member < count, 1.0, 0.0)
            kind = bucket_col[m, source, :].astype(jnp.int32)
            hot = (lane_own == kind) | (lane_own == CHOICE + choice)
            hot = hot | ((lane_own == SEQ + member) & (member < count))
            value = jnp.where(hot & (choice >= -NHC), 1.0, 0.0)
            value = jnp.where(lane_own == GATE, gate, value)
            value = jnp.where(lane_own == LIVE, live, value)
            own[m, pl.ds(where * half, half), :] = value
            usage[0:1, :] += jnp.sum(value * live, axis=0, keepdims=True)
    if column.chips > 2:
        mix_ring.advance()
    out_ring.start()
    mix_ring.advance_all()
    out_ring.advance()
    mix_ring.finish()
    outs.append(loads.copy(mix, mix_out))
    up_ring = WeightRing(
        column, loads, expand, lambda i: up.at[pl.ds(pl.multiple_of(i * block, block), block)]
    )
    down_ring = WeightRing(column, loads, shrink, lambda i: down_out.at[i])
    scale = HD ** (-0.5)
    span = 3 * HD
    tile = min(512, width)
    saves = outs

    def project(m):
        base = m * total
        cos, sin = cosine[m], sine[m]

        def head(h, _):
            mixed = dot(
                rows_buf[pl.ds(base, total), :], mix[:, pl.ds(pl.multiple_of(h * span, HD), span)]
            )
            here = pl.ds(pl.multiple_of(h * HD, HD), HD)
            qkv[m, 0, :, here] = turned(mixed[:, :HD], cos, sin).astype(BF16)
            qkv[m, 1, :, here] = turned(mixed[:, HD : 2 * HD], cos, sin).astype(BF16)
            qkv[m, 2, :, here] = mixed[:, 2 * HD :].astype(BF16)
            return 0

        lax.fori_loop(0, heads, head, 0)

    def attend(m):
        base = m * total

        def some(c, _):
            rows_here = pl.ds(pl.multiple_of(c * chunk, chunk), chunk)
            bias_here = mask[m, rows_here, :]
            info = row_info[m, rows_here, :]
            for h in range(heads):
                here = pl.ds(h * HD, HD)
                scores = dot_nt(qkv[m, 0, rows_here, here], qkv[m, 1, :, here]) * scale + bias_here
                peak = jnp.max(scores, axis=-1, keepdims=True)
                powers = jnp.exp(scores - peak)
                share = powers / jnp.sum(powers, axis=-1, keepdims=True)
                value = dot(share.astype(BF16), qkv[m, 2, :, here]).astype(BF16)
                value = value.astype(F32) * info[:, h : h + 1]
                head_rows[pl.ds(pl.multiple_of(base + c * chunk, chunk), chunk), here] = value.astype(
                    BF16
                )
            return 0

        lax.fori_loop(0, total // chunk, some, 0)

    def merge(m):
        base = m * total

        def body(j, _):
            here = pl.ds(pl.multiple_of(j * tile, tile), tile)
            part[pl.ds(base, total), here] = dot(
                head_rows[pl.ds(base, total), :], out[:, here]
            ).astype(BF16)
            return 0

        lax.fori_loop(0, width // tile, body, 0)

    scatters = [
        Scatter(
            links,
            part,
            m * total,
            landing.at[m],
            staged.at[m],
            last.at[m],
            attention_out.at[m],
        )
        for m in range(micro)
    ]
    gathers = [Gather(links, second_buf, m * total) for m in range(micro)]

    def second_norm(m):
        scatter = scatters[m]

        def body(where, i, row):
            attended = scatter.chunk(where, i)
            info = own[m, at(row), :]
            hidden = tokens[m, at(row), :].astype(F32) + info[:, GATE : GATE + 1] * attended
            attention_out[m, at(row), :] = attended
            low = normalized(hidden)[0] * params[FEED : FEED + 1, :]
            low = (low + params[FEED + 1 : FEED + 2, :]).astype(BF16)
            second_buf[at(m * total + where * links.second + i * STEP), :] = low
            low = low.astype(F32)
            lane = lax.broadcasted_iota(jnp.int32, (STEP, LANES), 1)
            logits = jnp.full((STEP, LANES), MASKED)
            for b in range(NB):
                router = params[WIDTH_ROUTER + b : WIDTH_ROUTER + b + 1, :]
                logits = jnp.where(lane == b, jnp.sum(low * router, axis=-1, keepdims=True), logits)
            share = softmax_lanes(logits, lane < NB)
            share_out[m, at(row), :] = share
            gate = NB * jnp.sum(share * info, axis=-1, keepdims=True)
            outer = cotangent[m, at(row), :].astype(F32) * info[:, LIVE : LIVE + 1]
            branch_buf[at(m * total + where * links.second + i * STEP), :] = (gate * outer).astype(
                BF16
            )

        over_rows(half, body)

    for m in range(micro):
        project(m)
        if m == 0:
            if column.chips > 2:
                out_ring.advance()
            up_ring.start()
        attend(m)
        if m == 0:
            out_ring.finish()
            outs.append(loads.copy(out, out_out))
        else:
            scatters[m - 1].middle()
        merge(m)
        scatters[m].start()
    branch_gathers = [Gather(links, branch_buf, m * total) for m in range(micro)]
    up_ring.advance()
    for m in range(micro):
        scatters[m].finish()
        second_norm(m)
        gathers[m].start()
        if m + 1 < micro:
            scatters[m + 1].middle()
            gathers[m].middle()
            if column.chips > 2:
                up_ring.advance()
    down_ring.start()
    saves.append(loads.copy(qkv, qkv_out))
    saves.append(loads.copy(head_rows, heads_out))
    gathers[micro - 1].middle()
    for g in branch_gathers:
        g.start()
    for m in range(micro):
        gathers[m].finish()
        here = pl.ds(m * total, total)
        saves.append(loads.copy(second_buf.at[here], second_out.at[here]))
    up_ring.finish()
    saves.append(loads.copy(up, up_out))
    wait_all(rows_saves)
    step = min(512, units)
    for m in range(micro):

        def widen(j, _, m=m):
            here = pl.ds(pl.multiple_of(j * step, step), step)
            before = dot(second_buf[pl.ds(m * total, total), :], up[:, here])
            kept = jnp.maximum(before, 0.0) * row_info[m, :, heads : heads + 1]
            rect[pl.ds(m * total, total), here] = kept.astype(BF16)
            active[pl.ds(m * total, total), here] = (kept * kept).astype(BF16)
            return 0

        lax.fori_loop(0, units // step, widen, 0)
        here = pl.ds(m * total, total)
        saves.append(loads.copy(rect.at[here, pl.ds(0, units)], rect_out.at[here]))
        saves.append(loads.copy(active.at[here, pl.ds(0, units)], active_out.at[here]))
        if m == 0:
            for g in branch_gathers:
                g.middle()
            down_ring.advance()
    for m, g in enumerate(branch_gathers):
        g.finish()
        here = pl.ds(m * total, total)
        saves.append(loads.copy(branch_buf.at[here], branch_out.at[here]))
    wide = tile_out.shape[3]

    def make(c, put):
        value = dot_tn(active[:, pl.ds(pl.multiple_of(c * wide, wide), wide)], branch_buf[...])
        for j in range(dp_size):
            put(j, value[:, j * block : (j + 1) * block].astype(BF16))

    halves_out(
        column,
        units // wide,
        make,
        tile_out,
        mine_out,
        twin_out,
        tile_sems,
        twin_sem,
        down_ring.advance if column.chips > 2 else None,
    )
    down_ring.finish()
    wait_all(saves)


def narrow_kernel(
    dp_size,
    size,
    down_hbm,
    up_hbm,
    active_hbm,
    rect_hbm,
    branch_hbm,
    second_hbm,
    tokens,
    cotangent,
    attention,
    share,
    own,
    params,
    mine_hbm,
    twin_hbm,
    block_out,
    mine_out,
    twin_out,
    hidden_out,
    back_out,
    stats_out,
    gate_out,
    sum_out,
    landed_out,
    gathered_out,
    down,
    up,
    active,
    rect,
    shared_rows,
    part,
    landing,
    staged,
    last,
    total_rows,
    gate_back,
    tile,
    sum_own,
    sum_other,
    sum_landing,
    sum_staged,
    sum_tile,
    send,
    recv,
    load_sems,
    tile_sems,
    twin_sem,
    sum_sems,
):
    micro, rows, width = tokens.shape
    total = rows * size
    units = up.shape[1]
    copies, loads = Copies(send, recv), Loads(load_sems)
    links, column = Links(size, rows, copies), Column(dp_size, copies)
    half = links.half
    here = [pl.ds(m * total, total) for m in range(micro)]
    ring = SumRing(
        column,
        loads,
        mine_hbm,
        twin_hbm,
        sum_out,
        sum_own,
        sum_other,
        sum_landing,
        sum_staged,
        sum_tile,
        sum_sems,
    )
    ring.load()
    down_copies = columns_in(loads, down_hbm, down)
    active_copies = [loads.copy(active_hbm.at[h], active.at[h]) for h in here]
    branch_copies = [loads.copy(branch_hbm.at[h], shared_rows.at[h]) for h in here]
    rect_copy = loads.copy(rect_hbm.at[here[0]], rect)
    up_copy = loads.copy(up_hbm, up)
    stats_out[...] = jnp.zeros_like(stats_out)
    gate_out[...] = jnp.zeros_like(gate_out)
    greet(*links.peers, *column.ring, *column.pair)
    ring.start()
    step = min(512, units)
    tile_cols = min(512, width)
    outs = [
        Scatter(
            links, part, m * total, landing.at[m], staged.at[m], last.at[m], total_rows.at[m]
        )
        for m in range(micro)
    ]
    backs = [
        Scatter(
            links,
            part,
            m * total,
            landing.at[micro + m],
            staged.at[micro + m],
            last.at[micro + m],
            hidden_out.at[m],
        )
        for m in range(micro)
    ]
    wait_all(down_copies)
    for m in range(micro):
        active_copies[m].wait()

        def body(j, _, m=m):
            cols = pl.ds(pl.multiple_of(j * tile_cols, tile_cols), tile_cols)
            part[here[m], cols] = dot(active[here[m], :], down[:, cols]).astype(BF16)
            return 0

        lax.fori_loop(0, width // tile_cols, body, 0)
        outs[m].start()
    for m in range(micro):
        branch_copies[m].wait()
        rect_copy.wait()

        def body(j, _, m=m):
            cols = pl.ds(pl.multiple_of(j * step, step), step)
            back = dot_nt(shared_rows[here[m], :], down[cols, :])
            active[here[m], cols] = (2.0 * rect[:, cols].astype(F32) * back).astype(BF16)
            return 0

        lax.fori_loop(0, units // step, body, 0)
        if m + 1 < micro:
            rect_copy = loads.copy(rect_hbm.at[here[m + 1]], rect)
        if m == 0:
            up_copy.wait()
    second_copies = [loads.copy(second_hbm.at[h], shared_rows.at[h]) for h in here]
    if column.chips > 2:
        ring.advance()
    for m in range(micro):
        outs[m].middle()

        def body(j, _, m=m):
            cols = pl.ds(pl.multiple_of(j * tile_cols, tile_cols), tile_cols)
            part[here[m], cols] = dot_nt(active[here[m], :], up[cols, :]).astype(BF16)
            return 0

        lax.fori_loop(0, width // tile_cols, body, 0)
        backs[m].start()

    def finish_out(m):
        outs[m].finish()

        def body(where, i, row):
            branch = outs[m].chunk(where, i)
            info = own[m, at(row), :]
            live = info[:, LIVE : LIVE + 1]
            outer = cotangent[m, at(row), :].astype(F32) * live
            hidden = tokens[m, at(row), :].astype(F32)
            hidden = hidden + info[:, GATE : GATE + 1] * attention[m, at(row), :]
            gate = NB * jnp.sum(share[m, at(row), :] * info, axis=-1, keepdims=True)
            block_out[m, at(row), :] = (live * (hidden + gate * branch)).astype(BF16)
            value = jnp.sum(outer * branch, axis=-1, keepdims=True)
            gate_back[m, at(row), :] = jnp.broadcast_to(value, (STEP, LANES))

        over_rows(half, body)

    def finish_back(m):
        backs[m].finish()

        def body(where, i, row):
            back = backs[m].chunk(where, i)
            info = own[m, at(row), :]
            portions = share[m, at(row), :]
            live = info[:, LIVE : LIVE + 1]
            outer = cotangent[m, at(row), :].astype(F32) * live
            hidden = tokens[m, at(row), :].astype(F32)
            attended = attention[m, at(row), :]
            hidden = hidden + info[:, GATE : GATE + 1] * attended
            normed, inverse = normalized(hidden)
            gain = params[FEED : FEED + 1, :]
            low = (normed * gain + params[FEED + 1 : FEED + 2, :]).astype(BF16).astype(F32)
            picked = jnp.sum(portions * info, axis=-1, keepdims=True)
            logit_back = NB * picked * (info - portions) * gate_back[m, at(row), :]
            for b in range(NB):
                column = logit_back[:, b : b + 1]
                back = back + column * params[WIDTH_ROUTER + b : WIDTH_ROUTER + b + 1, :]
                stats_out[2 + b : 3 + b, :] += jnp.sum(column * low, axis=0, keepdims=True)
            stats_out[0:1, :] += jnp.sum(back * normed, axis=0, keepdims=True)
            stats_out[1:2, :] += jnp.sum(back, axis=0, keepdims=True)
            hidden_back = outer + norm_back(back, normed, inverse, gain)
            hidden_out[m, at(row), :] = hidden_back
            attention_back = (info[:, GATE : GATE + 1] * hidden_back).astype(BF16)
            if m == 0:
                shared_rows[at(where * links.second + i * STEP), :] = attention_back
            else:
                back_out[m - 1, at(row), :] = attention_back
            gate_part = jnp.sum(hidden_back * attended, axis=-1, keepdims=True)
            gate_out[m : m + 1, :] += jnp.sum(info * gate_part, axis=0, keepdims=True)

        over_rows(half, body)

    wait_all(second_copies)
    block = mine_out.shape[1]

    def make(c, ref):
        ref[...] = dot_tn(
            shared_rows[:, pl.ds(pl.multiple_of(c * block, block), block)], active[...]
        ).astype(BF16)

    early, other, staged_up = [up.at[pl.ds(i * block, block)] for i in range(3)]
    up_ring = SumRing(
        column, loads, mine_out, twin_out, None, early, other, landed_out, staged_up, None, None
    )

    def start_up():
        up_ring.load()
        up_ring.start(more=False)

    blocks_out(column, make, tile, mine_out, twin_out, tile_sems, twin_sem, start_up)
    if column.chips > 3:
        ring.advance()
    for m in range(micro):
        finish_out(m)
    for m in range(micro):
        backs[m].middle()
    gather = Gather(links, shared_rows, 0)
    for m in range(micro):
        finish_back(m)
        if m == 0:
            gather.start()
    gather.middle()
    ring.finish()
    gather.finish()
    save = loads.copy(shared_rows.at[pl.ds(0, total)], gathered_out)
    up_ring.hop.wait()
    save.wait()


STATS_ONE = 6
STATS_USE = 12
STATS_ROWS = 16
SEQ_COUNT = 4


def attend_back_kernel(
    dp_size,
    size,
    heads,
    back,
    gathered_hbm,
    gate,
    out_hbm,
    qkv_hbm,
    heads_hbm,
    rows_hbm,
    mask_hbm,
    mix_hbm,
    cosine,
    sine,
    row_info,
    mine_hbm,
    twin_hbm,
    landed_hbm,
    tokens,
    hidden_back,
    own,
    seq_info,
    params,
    stats_two,
    usage,
    back_out,
    up_sum,
    mix_sum,
    out_sum,
    stats_out,
    mix_mine,
    mix_twin,
    out_mine,
    out_twin,
    buf,
    out,
    qkv,
    head_rows,
    rows_buf,
    mask,
    heads_back,
    mixed_back,
    score_back,
    shares,
    out_tile,
    mix_tile,
    gates,
    mix,
    landing,
    staged,
    last,
    *rest,
):
    up_bufs, mix_bufs, out_bufs = rest[:5], rest[5:10], rest[10:15]
    stats, share, pieces, sums, whole = rest[15:20]
    send, recv, load_sems = rest[20:23]
    out_sems, out_twin_sem, mix_sems, mix_twin_sem, up_sum_sems, mix_sum_sems, out_sum_sems = rest[23:]
    micro, rows, width = tokens.shape
    total = rows * size
    copies, loads = Copies(send, recv), Loads(load_sems)
    links, column = Links(size, rows, copies), Column(dp_size, copies)
    half = links.half
    ring = SumRing(column, loads, mine_hbm, twin_hbm, up_sum, *up_bufs, up_sum_sems)
    mix_ring = SumRing(column, loads, mix_mine, mix_twin, mix_sum, *mix_bufs, mix_sum_sems)
    out_ring = SumRing(column, loads, out_mine, out_twin, out_sum, *out_bufs, out_sum_sems)
    ring.prepare(landed_hbm)
    first_copy = loads.copy(gathered_hbm, buf.at[pl.ds(0, total)])
    own_copies = []
    for m in range(1, micro):
        for where in range(2):
            own_copies.append(
                loads.copy(
                    back.at[m - 1, pl.ds(where * half, half)],
                    buf.at[pl.ds(m * total + where * links.second, half)],
                )
            )
    out_copies = [loads.copy(out_hbm, out)]
    qkv_copy = loads.copy(qkv_hbm, qkv)
    mask_copy = loads.copy(mask_hbm, mask)
    heads_copy = loads.copy(heads_hbm, head_rows)
    rows_copy = loads.copy(rows_hbm, rows_buf)
    mix_copy = loads.copy(mix_hbm, mix)
    gates[links.me] = gate[...]
    near = [lax.rem(links.me + s, size) for s in range(1, size)]
    far = [lax.rem(column.me + s, dp_size) for s in range(1, dp_size)]
    greet(*[("tensor", to) for to in near], *[("dp", to) for to in far])
    wait_all(own_copies)
    gathers = [Gather(links, buf, m * total) for m in range(1, micro)]
    for g in gathers:
        g.start()
    ring.resume()
    gate_copies = [links.copy(gate, gates.at[links.me], peer) for peer in near]
    stats[...] = jnp.zeros_like(stats)
    stats[0:8, :] = stats_two[...]
    stats[STATS_USE : STATS_USE + 1, 0:LANES] = usage[0:1, :]
    wait_all(out_copies)
    qkv_copy.wait()
    mask_copy.wait()
    scale = HD ** (-0.5)
    chunk = min(128, total)
    block, wide = out_mine.shape[2], out_tile.shape[3]
    here_rows = [pl.ds(m * total, total) for m in range(micro)]
    scatters = [
        Scatter(links, buf, m * total, landing.at[m], staged.at[m], last.at[m], back_out.at[m])
        for m in range(micro)
    ]

    def heads_part(m):
        base = m * total
        every = pl.ds(base, total)
        value = dot_nt(buf[every, :], out[...])
        for h in range(heads):
            here = pl.ds(h * HD, HD)
            heads_back[:, here] = (
                value[:, h * HD : (h + 1) * HD] * row_info[m, :, h : h + 1]
            ).astype(BF16)
        for h in range(heads):
            here = pl.ds(h * HD, HD)

            def some(c, _, m=m, here=here):
                rows_here = pl.ds(pl.multiple_of(c * chunk, chunk), chunk)
                scores = dot_nt(qkv[m, 0, rows_here, here], qkv[m, 1, :, here]) * scale
                scores = scores + mask[m, rows_here, :]
                powers = jnp.exp(scores - jnp.max(scores, axis=-1, keepdims=True))
                share = powers / jnp.sum(powers, axis=-1, keepdims=True)
                share_back = dot_nt(heads_back[rows_here, here], qkv[m, 2, :, here])
                inner = jnp.sum(share * share_back, axis=-1, keepdims=True)
                score_back[rows_here, :] = (share * (share_back - inner)).astype(BF16)
                shares[rows_here, :] = share.astype(BF16)
                return 0

            lax.fori_loop(0, total // chunk, some, 0)
            cos, sin = cosine[m], -sine[m]
            query_back = dot(score_back[...], qkv[m, 1, :, here]) * scale
            keys_back = dot_tn(score_back[...], qkv[m, 0, :, here]) * scale
            values_back = dot_tn(shares[...], heads_back[:, here])
            col = 3 * h * HD
            mixed_back[every, pl.ds(col, HD)] = turned(query_back, cos, sin).astype(BF16)
            mixed_back[every, pl.ds(col + HD, HD)] = turned(keys_back, cos, sin).astype(BF16)
            mixed_back[every, pl.ds(col + 2 * HD, HD)] = values_back.astype(BF16)
            if m == 0 and h == 0:
                for g in gathers:
                    g.middle()

    def make_out(c, put):
        value = dot_tn(head_rows[:, pl.ds(pl.multiple_of(c * wide, wide), wide)], buf[...])
        for j in range(dp_size):
            put(j, value[:, j * block : (j + 1) * block].astype(BF16))

    def make_mix(c, ref):
        ref[...] = dot_tn(
            rows_buf[:, pl.ds(pl.multiple_of(c * block, block), block)], mixed_back[...]
        ).astype(BF16)

    tile = min(512, width)

    def first_part(m):
        def body(j, _):
            cols = pl.ds(pl.multiple_of(j * tile, tile), tile)
            buf[here_rows[m], cols] = dot_nt(mixed_back[here_rows[m], :], mix[cols, :]).astype(BF16)
            return 0

        lax.fori_loop(0, width // tile, body, 0)
        scatters[m].start()

    first_copy.wait()
    heads_part(0)
    for g in gathers:
        g.finish()
    heads_copy.wait()
    halves_out(
        column,
        heads * HD // wide,
        make_out,
        out_tile,
        out_mine,
        out_twin,
        out_sems,
        out_twin_sem,
    )
    if column.chips > 3:
        ring.advance()
    out_ring.load()
    out_ring.start()
    mix_copy.wait()
    first_part(0)
    for m in range(1, micro):
        heads_part(m)
    scatters[0].middle()
    rows_copy.wait()

    def start_mix():
        mix_ring.load()
        mix_ring.start(more=False)

    blocks_out(column, make_mix, mix_tile, mix_mine, mix_twin, mix_sems, mix_twin_sem, start_mix)
    mix_ring.load()
    if column.chips > 2:
        out_ring.advance()
    for m in range(1, micro):
        first_part(m)
    for made in gate_copies:
        made.wait()
    gate_sum = gates[0]
    for r in range(1, size):
        gate_sum = gate_sum + gates[r]

    def last_rows(m):
        s = scatters[m]
        s.finish()
        count = SEQ_COUNT
        lane = lax.broadcasted_iota(jnp.int32, (8, LANES), 1)
        which = lax.broadcasted_iota(jnp.int32, (8, LANES), 0)
        info = seq_info[m]
        gate_back = jnp.where(lane == SEQ + which, gate_sum[m : m + 1, :], 0.0)
        gate_back = jnp.sum(gate_back, axis=-1, keepdims=True)
        chosen = jnp.where(lane == info[:, CHOSEN : CHOSEN + 1].astype(jnp.int32), 1.0, 0.0)
        logit_back = NHC * info[:, PICKED : PICKED + 1] * (chosen - info) * gate_back
        logit_back = logit_back / info[:, DIVISOR : DIVISOR + 1]

        def body(where, i, row):
            back = s.chunk(where, i)
            normed, inverse = normalized(tokens[m, at(row), :].astype(F32))
            gain = params[ATTEND : ATTEND + 1, :]
            low = (normed * gain + params[ATTEND + 1 : ATTEND + 2, :]).astype(BF16).astype(F32)
            rows_info = own[m, at(row), :]
            spread = jnp.zeros((STEP, LANES), F32)
            for q in range(count):
                spread = spread + rows_info[:, SEQ + q : SEQ + q + 1] * logit_back[q : q + 1, :]
            for c in range(NHC):
                part = spread[:, c : c + 1]
                back = back + part * params[HEAD_ROUTER + c : HEAD_ROUTER + c + 1, :]
                at_row = STATS_ONE + 2 + c
                stats[at_row : at_row + 1, :] += jnp.sum(part * low, axis=0, keepdims=True)
            at_row = STATS_ONE
            stats[at_row : at_row + 1, :] += jnp.sum(back * normed, axis=0, keepdims=True)
            stats[at_row + 1 : at_row + 2, :] += jnp.sum(back, axis=0, keepdims=True)
            value = norm_back(back, normed, inverse, gain)
            back_out[m, at(row), :] = hidden_back[m, at(row), :] + value

        over_rows(links.half, body)

    if column.chips > 3:
        out_ring.advance()
    if column.chips > 2:
        mix_ring.advance()
    last_rows(0)
    for s in scatters[1:]:
        s.middle()
    if column.chips > 3:
        mix_ring.advance()
    ring.finish()
    for m in range(1, micro):
        last_rows(m)

    piece = width // size
    mine = pl.ds(pl.multiple_of(links.me * piece, piece), piece)
    sent = [
        links.copy(
            stats.at[:, pl.ds(pl.multiple_of(to * piece, piece), piece)], pieces.at[links.me], to
        )
        for to in near
    ]
    pieces[links.me] = stats[:, mine]
    wait_all(sent)
    value = pieces[0]
    for r in range(1, size):
        value = value + pieces[r]
    share[0] = value
    sums[column.me] = value
    sent = [column.copy(share.at[0], sums.at[column.me], to) for to in far]
    out_ring.finish()
    mix_ring.finish()
    wait_all(sent)
    value = sums[0]
    for r in range(1, dp_size):
        value = value + sums[r]
    share[1] = value
    whole[links.me] = value
    wait_all([links.copy(share.at[1], whole.at[links.me], to) for to in near])
    for r in range(size):
        stats_out[:, r * piece : (r + 1) * piece] = whole[r]


ANY = pl.BlockSpec(memory_space=pl.ANY)
VMEM = pl.BlockSpec(memory_space=pltpu.VMEM)
SMEM = pl.BlockSpec(memory_space=pltpu.SMEM)


def call(kernel, ident, ins, outs, scratch, copies, loads, extra=(), flops=0, limit=56):
    dma = pltpu.SemaphoreType.DMA
    sems = [dma((copies,)), dma((copies,)), dma((loads,))] + [dma((n,)) for n in extra]
    moved = sum(a.size * a.dtype.itemsize for a, _ in ins)
    return pl.pallas_call(
        kernel,
        out_shape=[jax.ShapeDtypeStruct(shape, kind) for shape, kind, _ in outs],
        in_specs=[SMEM if near == "s" else VMEM if near else ANY for _, near in ins],
        out_specs=[VMEM if near else ANY for _, _, near in outs],
        scratch_shapes=[pltpu.VMEM(shape, kind) for shape, kind in scratch] + sems,
        compiler_params=pltpu.CompilerParams(
            collective_id=ident, has_side_effects=True, vmem_limit_bytes=limit * MIB
        ),
        cost_estimate=pl.CostEstimate(flops=flops, bytes_accessed=moved, transcendentals=0),
    )(*[a for a, _ in ins])


def local(
    dp_size,
    size,
    tokens,
    cotangent,
    mixer,
    merger,
    expand,
    shrink,
    attend_gain,
    attend_bias,
    feed_gain,
    feed_bias,
    width_router,
    head_router,
    lengths,
    head_choice,
    width_bucket,
):
    micro, rows, width = tokens.shape
    total = width_bucket.shape[1]
    every = micro * total
    half = rows // 2
    high = size // 2
    heads = merger.shape[0] // HD
    units = expand.shape[1]
    block = width // dp_size
    chips = dp_size // 2
    few = transfers(size)
    ringed = ring_copies(dp_size)

    vectors = jnp.concatenate([attend_gain, attend_bias, feed_gain, feed_bias]).reshape(4, width)
    params = jnp.concatenate(
        [vectors, jnp.concatenate([width_router, head_router], axis=1).T], axis=0
    ).astype(F32)
    rates = jnp.power(10000.0, -2.0 * jnp.arange(HD // 2, dtype=F32) / HD)
    rates = jnp.concatenate([rates, rates])[None]

    tables = (micro, total, LANES)
    lands = half * (2 * (high - 1) + high)
    stages = half * high
    wide_heads = heads * HD
    span = 3 * wide_heads
    buffers = [((micro, lands, width), BF16), ((micro, stages, width), BF16), ((micro, stages, width), BF16)]
    attended = call(
        functools.partial(attend_kernel, dp_size, size, heads, units),
        2,
        [
            (tokens, True),
            (cotangent, True),
            (params, True),
            (rates, True),
            (width_bucket, True),
            (lengths, "s"),
            (head_choice, "s"),
            (mixer, False),
            (merger, False),
            (expand, False),
            (shrink, False),
        ],
        [
            ((every, width), BF16, False),
            ((width, span), BF16, False),
            ((wide_heads, width), BF16, False),
            ((micro, total, total), F32, True),
            (tables, F32, True),
            (tables, F32, True),
            (tables, F32, True),
            ((micro, rows, LANES), F32, True),
            ((micro, 8, LANES), F32, True),
            ((8, LANES), F32, True),
            ((micro, 3, total, wide_heads), BF16, False),
            ((every, wide_heads), BF16, False),
            ((micro, rows, width), F32, True),
            ((every, width), BF16, False),
            ((micro, rows, LANES), F32, True),
            ((width, units), BF16, False),
            ((dp_size, units, block), BF16, False),
            ((every, units), BF16, False),
            ((every, units), BF16, False),
            ((every, width), BF16, False),
            ((chips, units, block), BF16, False),
            ((chips, units, block), BF16, False),
        ],
        [
            ((every, width), BF16),
            ((total, LANES), jnp.int32),
            (tables, jnp.int32),
            (tables, F32),
            ((width, span), BF16),
            ((wide_heads, width), BF16),
            ((micro, 3, total, wide_heads), BF16),
            ((every, wide_heads), BF16),
            ((every, width), BF16),
        ]
        + buffers
        + [
            ((every, width), BF16),
            ((width, units), BF16),
            ((every, width), BF16),
            ((2, 2, chips, min(256, units), block), BF16),
        ],
        4 * micro * few + 4 * ringed,
        4 + micro + 2 + 2 + micro + 1 + 3 * micro,
        (4, 1),
        flops=2 * every * width * (span + wide_heads + 2 * units),
        limit=63,
    )
    first_rows, mix_weight, out_weight, mask, cosine, sine, row_info = attended[:7]
    own, seq_info, usage, qkv, head_rows, attention, second_rows = attended[7:14]
    width_share, up_weight, down_weight, rect, active, branch_rows = attended[14:20]
    down_mine, down_twin = attended[20:]

    narrowed = call(
        functools.partial(narrow_kernel, dp_size, size),
        4,
        [
            (down_weight, False),
            (up_weight, False),
            (active, False),
            (rect, False),
            (branch_rows, False),
            (second_rows, False),
            (tokens, True),
            (cotangent, True),
            (attention, True),
            (width_share, True),
            (own, True),
            (params, True),
            (down_mine, False),
            (down_twin, False),
        ],
        [
            ((micro, rows, width), BF16, True),
            ((chips, block, units), BF16, False),
            ((chips, block, units), BF16, False),
            ((micro, rows, width), F32, True),
            ((micro - 1, rows, width), BF16, True),
            ((8, width), F32, True),
            ((8, LANES), F32, True),
            ((units, block), F32, False),
            ((1, block, units), BF16, False),
            ((total, width), BF16, False),
        ],
        [
            ((units, width), BF16),
            ((width, units), BF16),
            ((every, units), BF16),
            ((total, units), BF16),
            ((every, width), BF16),
            ((every, width), BF16),
            ((2 * micro, lands, width), BF16),
            ((2 * micro, stages, width), BF16),
            ((2 * micro, stages, width), BF16),
            ((micro, rows, width), F32),
            ((micro, rows, LANES), F32),
            ((2, block, units), BF16),
        ]
        + sum_scratch(chips, units, block),
        2 * micro * few + few + chips,
        dp_size + 4 * micro + 1 + 2 * chips + 3,
        (2, chips, SUM_TILES),
        flops=8 * every * width * units,
        limit=63,
    )
    block_output, up_mine, up_twin, hidden_back, back_own, stats_two, gate_part = narrowed[:7]
    down_sum, up_landed, back_rows = narrowed[7:]

    out_tile = min(256, wide_heads)
    lasts = call(
        functools.partial(attend_back_kernel, dp_size, size, heads),
        5,
        [
            (back_own, False),
            (back_rows, False),
            (gate_part, True),
            (out_weight, False),
            (qkv, False),
            (head_rows, False),
            (first_rows, False),
            (mask, False),
            (mix_weight, False),
            (cosine, True),
            (sine, True),
            (row_info, True),
            (up_mine, False),
            (up_twin, False),
            (up_landed, False),
            (tokens, True),
            (hidden_back, True),
            (own, True),
            (seq_info, True),
            (params, True),
            (stats_two, True),
            (usage, True),
        ],
        [
            ((micro, rows, width), F32, True),
            ((block, units), F32, False),
            ((block, span), F32, False),
            ((wide_heads, block), F32, False),
            ((STATS_ROWS, width), F32, True),
            ((chips, block, span), BF16, False),
            ((chips, block, span), BF16, False),
            ((chips, wide_heads, block), BF16, False),
            ((chips, wide_heads, block), BF16, False),
        ],
        [
            ((every, width), BF16),
            ((wide_heads, width), BF16),
            ((micro, 3, total, wide_heads), BF16),
            ((every, wide_heads), BF16),
            ((every, width), BF16),
            ((micro, total, total), F32),
            ((total, wide_heads), BF16),
            ((every, span), BF16),
            ((total, total), BF16),
            ((total, total), BF16),
            ((2, 2, chips, out_tile, block), BF16),
            ((2, block, span), BF16),
            ((size, 8, LANES), F32),
            ((width, span), BF16),
        ]
        + buffers
        + sum_scratch(chips, block, units)
        + sum_scratch(chips, block, span)
        + sum_scratch(chips, wide_heads, block)
        + [
            ((STATS_ROWS, width), F32),
            ((2, STATS_ROWS, width // size), F32),
            ((size, STATS_ROWS, width // size), F32),
            ((dp_size, STATS_ROWS, width // size), F32),
            ((size, STATS_ROWS, width // size), F32),
        ],
        2 * micro * few + 3 * (size - 1) + dp_size - 1 + 3 * (chips - 1),
        2 * micro + dp_size + 6 + 6 * chips,
        (4, 1, 2, chips, SUM_TILES, SUM_TILES, SUM_TILES),
        flops=4 * every * width * (wide_heads + span) + 20 * heads * micro * total * total * HD,
        limit=63,
    )
    tokens_gradient, up_sum, mix_sum, out_sum, stats = lasts[:5]
    return (
        block_output,
        tokens_gradient,
        mix_sum,
        out_sum,
        up_sum,
        down_sum,
        stats[STATS_ONE],
        stats[STATS_ONE + 1],
        stats[0],
        stats[1],
        stats[2 : 2 + NB].T,
        stats[STATS_ONE + 2 : STATS_ONE + 2 + NHC].T,
        stats[STATS_USE, :NB],
        stats[STATS_USE, CHOICE : CHOICE + NHC],
    )


def solution(mesh):
    def run(*args):
        return local(mesh.shape["dp"], mesh.shape["tensor"], *args)

    rows = P(None, ("dp", "tensor"), None)
    tall, wide = P("dp", "tensor"), P("tensor", "dp")
    weights = (tall, wide, tall, wide)
    return jax.shard_map(
        run,
        mesh=mesh,
        in_specs=(rows, rows) + weights + (P(),) * 6 + (P(None, "dp"),) * 3,
        out_specs=(rows, rows) + weights + (P(),) * 8,
        check_vma=False,
    )
```

```python
import functools

import jax
import jax.numpy as jnp
from jax import lax
from jax.experimental import pallas as pl
from jax.experimental.pallas import tpu as pltpu
from jax.sharding import PartitionSpec as P

H = 16
HD = 128
FF = 8192
NB = 4
NHC = 4

EPSILON = 1e-05
HIGHEST = lax.Precision.HIGHEST
MASKED = -1e30
BF16 = jnp.bfloat16
F32 = jnp.float32
MESH = pl.DeviceIdType.MESH
MIB = 1024 * 1024
LANES = 128
STEP = 16

GATE = 4
LIVE = 5
SEQ = 8
CHOICE = 16

PICKED = 4
DIVISOR = 5
CHOSEN = 6

ATTEND = 0
FEED = 2
WIDTH_ROUTER = 4
HEAD_ROUTER = 8


def dot(left, right):
    return jnp.dot(left, right, preferred_element_type=F32)


def dot_nt(left, right):
    return lax.dot_general(left, right, (((1,), (1,)), ((), ())), preferred_element_type=F32)


def dot_tn(left, right):
    return lax.dot_general(left, right, (((0,), (0,)), ((), ())), preferred_element_type=F32)


def at(start, size=STEP):
    return pl.ds(pl.multiple_of(start, STEP), size)


class Copies:
    def __init__(self, send_sems, recv_sems):
        self.send_sems, self.recv_sems, self.used = send_sems, recv_sems, 0

    def start(self, src, dst, axis, to):
        made = pltpu.make_async_remote_copy(
            src_ref=src,
            dst_ref=dst,
            send_sem=self.send_sems.at[self.used],
            recv_sem=self.recv_sems.at[self.used],
            device_id={axis: to},
            device_id_type=MESH,
        )
        self.used += 1
        made.start()
        return made


def greet(*peers):
    barrier = pltpu.get_barrier_semaphore()
    for axis, to in peers:
        pl.semaphore_signal(barrier, inc=1, device_id={axis: to}, device_id_type=MESH)
    pl.semaphore_wait(barrier, len(peers))


class Links:
    def __init__(self, size, rows, copies):
        me = lax.axis_index("tensor")
        hi, lo = me // 2, me % 2
        self.me, self.size, self.high, self.half = me, size, size // 2, rows // 2
        self.near = hi * 2 + (1 - lo)
        self.ahead = [lax.rem(hi + s, self.high) * 2 + lo for s in range(self.high)]
        self.behind = [
            lax.rem(hi + self.high - s, self.high) * 2 + lo for s in range(self.high)
        ]
        self.second = self.half * size
        self.copies = copies
        steps = range(self.high)
        grid = [[lax.rem(hi + s, self.high) * 2 + (lo + l) % 2 for l in range(2)] for s in steps]
        self.first_ranks = [grid[s][l] for s in steps for l in range(2)]
        self.second_ranks = [grid[s][l] for l in range(2) for s in steps]
        self.peers = [("tensor", to) for to in [self.near] + self.ahead[1:]]

    def copy(self, src, dst, to):
        return self.copies.start(src, dst, "tensor", to)


class Column:
    def __init__(self, size, copies):
        self.me, self.chips, self.copies = lax.axis_index("dp"), size // 2, copies
        self.chip, self.core = self.me // 2, self.me % 2
        self.twin = self.chip * 2 + 1 - self.core
        self.right = self.block(1)
        self.left = self.block(-1)
        self.ring = [("dp", self.left)]
        self.pair = [("dp", self.twin)]

    def chip_at(self, step):
        return lax.rem(self.chip + self.chips + step, self.chips)

    def block(self, step):
        return self.chip_at(step) * 2 + self.core

    def copy(self, src, dst, to):
        return self.copies.start(src, dst, "dp", to)


class WeightRing:
    def __init__(self, column, loads, own, slot):
        self.column, self.loads, self.own, self.slot = column, loads, own, slot

    def start(self):
        k = self.column
        here = self.slot(k.me)
        self.hops = [k.copy(self.own, here, k.right)]
        self.twins = [k.copy(self.own, here, k.twin)]
        self.local = self.loads.copy(self.own, here)

    def advance(self):
        k = self.column
        step = len(self.twins)
        self.hops[step - 1].wait_recv()
        here = self.slot(k.block(-step))
        if step < k.chips - 1:
            self.hops.append(k.copy(here, here, k.right))
        self.twins.append(k.copy(here, here, k.twin))

    def advance_all(self):
        while len(self.twins) < self.column.chips:
            self.advance()

    def finish(self):
        self.advance_all()
        for made in self.twins:
            made.wait()
        for made in self.hops:
            made.wait_send()
        self.local.wait()


def ring_copies(size):
    return size // 2 * 2 - 1


class SumRing:
    def __init__(self, column, loads, mine, twin, target, own, other, landing, staged, tile, tile_sems):
        self.column, self.loads = column, loads
        self.mine, self.twin, self.target = mine, twin, target
        self.own, self.other, self.landing, self.staged = own, other, landing, staged
        self.tile, self.tile_sems = tile, tile_sems
        self.sent = 0
        self.rows = sum_rows(own.shape[1])

    def load(self):
        block = self.column.chip_at(-1 - self.sent)
        self.loading = [
            self.loads.copy(self.mine.at[block], self.own),
            self.loads.copy(self.twin.at[block], self.other),
        ]

    def send(self, landed, more=True):
        k, rows = self.column, self.rows

        def body(i, _):
            here = pl.ds(pl.multiple_of(i * rows, rows), rows)
            value = self.own[here, :].astype(F32) + self.other[here, :].astype(F32)
            if landed is not None:
                value = value + self.landing[landed, here, :].astype(F32)
            self.staged[here, :] = value.astype(BF16)
            return 0

        lax.fori_loop(0, self.own.shape[0] // rows, body, 0)
        self.hop = k.copy(self.staged, self.landing.at[self.sent], k.right)
        self.sent += 1
        if more:
            self.load()

    def start(self, more=True):
        wait_all(self.loading)
        self.send(None, more)

    def prepare(self, landed):
        self.sent = 1
        self.load()
        self.loading.append(self.loads.copy(landed.at[0], self.landing.at[0]))

    def resume(self):
        wait_all(self.loading)
        self.send(0)

    def advance(self):
        self.hop.wait()
        wait_all(self.loading)
        self.send(self.sent - 1)

    def finish(self):
        k, rows = self.column, self.rows
        while self.sent < k.chips - 1:
            self.advance()
        self.hop.wait()
        wait_all(self.loading)
        landed = k.chips - 2
        slots = self.tile.shape[0]

        def body(i, _):
            here = pl.ds(pl.multiple_of(i * rows, rows), rows)
            slot = lax.rem(i, slots)
            copy = pltpu.make_async_copy(
                self.tile.at[slot], self.target.at[here], self.tile_sems.at[slot]
            )

            @pl.when(i >= slots)
            def _():
                copy.wait()

            value = self.own[here, :].astype(F32) + self.other[here, :].astype(F32)
            self.tile[slot] = value + self.landing[landed, here, :].astype(F32)
            copy.start()
            return 0

        count = self.own.shape[0] // rows
        lax.fori_loop(0, count, body, 0)
        for i in range(max(count - slots, 0), count):
            here = pl.ds(i * rows, rows)
            slot = i % slots
            pltpu.make_async_copy(
                self.tile.at[slot], self.target.at[here], self.tile_sems.at[slot]
            ).wait()


SUM_TILES = 4


def sum_rows(width):
    return 128 if width <= 256 else 16


def sum_scratch(chips, rows, width):
    return [
        ((rows, width), BF16),
        ((rows, width), BF16),
        ((chips - 1, rows, width), BF16),
        ((rows, width), BF16),
        ((SUM_TILES, sum_rows(width), width), F32),
    ]


def transfers(size):
    return 2 * (size // 2)


class Gather:
    def __init__(self, links, buf, base):
        self.links, self.buf, self.base = links, buf, base

    def rows(self, start, count):
        return self.buf.at[pl.ds(self.base + start, count)]

    def start(self):
        k, half, second = self.links, self.links.half, self.links.second
        self.first_near = k.copy(self.rows(0, half), self.rows(half, half), k.near)
        self.second_far = [
            k.copy(self.rows(second, half), self.rows(second + s * half, half), k.behind[s])
            for s in range(1, k.high)
        ]

    def middle(self):
        k, half, second = self.links, self.links.half, self.links.second
        self.first_near.wait_recv()
        self.first_far = [
            k.copy(self.rows(0, 2 * half), self.rows(2 * half * s, 2 * half), k.behind[s])
            for s in range(1, k.high)
        ]
        for made in self.second_far:
            made.wait_recv()
        block = k.high * half
        self.second_near = k.copy(self.rows(second, block), self.rows(second + block, block), k.near)

    def finish(self):
        for made in self.first_far + [self.second_near]:
            made.wait_recv()
        for made in [self.first_near, self.second_near] + self.first_far + self.second_far:
            made.wait_send()


class Scatter:
    def __init__(self, links, part, base, landing, staged, last, total):
        self.links, self.part, self.base = links, part, base
        self.landing, self.staged, self.last, self.total = landing, staged, last, total

    def start(self):
        k, half = self.links, self.links.half
        block = k.high * half
        self.first_far = [
            k.copy(
                self.part.at[pl.ds(self.base + 2 * half * s, 2 * half)],
                self.landing.at[pl.ds(2 * half * (s - 1), 2 * half)],
                k.ahead[s],
            )
            for s in range(1, k.high)
        ]
        self.second_near = k.copy(
            self.part.at[pl.ds(self.base + k.second + block, block)],
            self.landing.at[pl.ds(2 * half * (k.high - 1), block)],
            k.near,
        )

    def middle(self):
        k, half, base = self.links, self.links.half, self.base
        steps = half // STEP
        for made in self.first_far:
            made.wait_recv()

        def first(i, _):
            for where in range(2):
                row = where * half + i * STEP
                value = self.part[at(base + row), :].astype(F32)
                for s in range(1, k.high):
                    value = value + self.landing[at(2 * half * (s - 1) + row), :].astype(F32)
                if where == 0:
                    self.total[at(i * STEP), :] = value
                else:
                    self.staged[at(i * STEP), :] = value.astype(BF16)
            return 0

        lax.fori_loop(0, steps, first, 0)
        self.first_near = k.copy(
            self.staged.at[pl.ds(0, half)], self.last.at[pl.ds(0, half)], k.near
        )
        self.second_near.wait_recv()
        landed = 2 * half * (k.high - 1)

        def second(i, _):
            for s in range(k.high):
                row = s * half + i * STEP
                value = self.part[at(base + k.second + row), :].astype(F32)
                value = value + self.landing[at(landed + row), :].astype(F32)
                if s == 0:
                    self.total[at(half + i * STEP), :] = value
                else:
                    self.staged[at(row), :] = value.astype(BF16)
            return 0

        lax.fori_loop(0, steps, second, 0)
        self.second_far = [
            k.copy(
                self.staged.at[pl.ds(half * s, half)], self.last.at[pl.ds(half * s, half)], k.ahead[s]
            )
            for s in range(1, k.high)
        ]
        for made in self.first_far + [self.second_near]:
            made.wait_send()

    def finish(self):
        for made in [self.first_near] + self.second_far:
            made.wait_recv()
            made.wait_send()

    def chunk(self, where, i):
        k, half = self.links, self.links.half
        value = self.total[at(where * half + i * STEP), :]
        if where == 0:
            return value + self.last[at(i * STEP), :].astype(F32)
        for s in range(1, k.high):
            value = value + self.last[at(half * s + i * STEP), :].astype(F32)
        return value


def over_rows(half, body):
    for where in range(2):

        def inner(i, _, where=where):
            body(where, i, where * half + i * STEP)
            return 0

        lax.fori_loop(0, half // STEP, inner, 0)


class Loads:
    def __init__(self, sems):
        self.sems, self.used = sems, 0

    def copy(self, src, dst):
        made = pltpu.make_async_copy(src, dst, self.sems.at[self.used])
        self.used += 1
        made.start()
        return made


def wait_all(*groups):
    for group in groups:
        for made in group if isinstance(group, list) else [group]:
            made.wait()


def columns_in(loads, blocks, flat):
    count, _, width = blocks.shape
    return [loads.copy(blocks.at[j], flat.at[:, pl.ds(j * width, width)]) for j in range(count)]


def halves_out(column, count, make, tile, mine, twin, sems, twin_sem, between=None):
    wide = tile.shape[3]

    def outs(c, slot):
        here = pl.ds(pl.multiple_of(c * wide, wide), wide)
        local = pltpu.make_async_copy(tile.at[slot, 0], mine.at[:, here, :], sems.at[slot])
        away = pltpu.make_async_remote_copy(
            src_ref=tile.at[slot, 1],
            dst_ref=twin.at[:, here, :],
            send_sem=sems.at[2 + slot],
            recv_sem=twin_sem.at[0],
            device_id={"dp": column.twin},
            device_id_type=MESH,
        )
        return local, away

    def body(c, _):
        slot = lax.rem(c, 2)
        local, away = outs(c, slot)

        @pl.when(c >= 2)
        def _():
            local.wait()
            away.wait_send()

        def put(block, value):
            tile[slot, lax.rem(block + column.core, 2), block // 2] = value

        make(c, put)
        local.start()
        away.start()
        return 0

    lax.fori_loop(0, count // 2, body, 0)
    if between is not None:
        between()
    lax.fori_loop(count // 2, count, body, 0)
    for c in range(max(count - 2, 0), count):
        local, away = outs(c, c % 2)
        local.wait()
        away.wait_send()
    all_landed(column, twin, sems, twin_sem)


def blocks_out(column, make, tile, mine, twin, sems, twin_sems, ring):
    def local_copy(i):
        chip = column.chip_at(-1 - i)
        return pltpu.make_async_copy(tile.at[0], mine.at[chip], sems.at[0])

    def away_copy(i):
        return pltpu.make_async_remote_copy(
            src_ref=tile.at[1],
            dst_ref=twin.at[column.chip_at(-1 - i)],
            send_sem=sems.at[1],
            recv_sem=twin_sems.at[i],
            device_id={"dp": column.twin},
            device_id_type=MESH,
        )

    def body(i, _):
        chip, local, away = column.chip_at(-1 - i), local_copy(i), away_copy(i)

        @pl.when(i > 0)
        def _():
            away.wait_send()

        make(2 * chip + 1 - column.core, tile.at[1])
        away.start()

        @pl.when(i > 1)
        def _():
            local.wait()

        make(2 * chip + column.core, tile.at[0])
        local.start()
        return 0

    lax.fori_loop(0, 1, body, 0)
    local_copy(0).wait()
    away_copy(0).wait_recv()
    ring()
    lax.fori_loop(1, column.chips, body, 0)
    for i in range(1, column.chips):
        away_copy(i).wait_recv()
    local_copy(column.chips - 1).wait()
    away_copy(column.chips - 1).wait_send()


def all_landed(column, twin, sems, twin_sem):
    pltpu.make_async_remote_copy(
        src_ref=twin,
        dst_ref=twin,
        send_sem=sems.at[0],
        recv_sem=twin_sem.at[0],
        device_id={"dp": column.twin},
        device_id_type=MESH,
    ).wait_recv()


def normalized(value):
    centred = value - jnp.mean(value, axis=-1, keepdims=True)
    inverse = lax.rsqrt(jnp.mean(centred * centred, axis=-1, keepdims=True) + EPSILON)
    return centred * inverse, inverse


def norm_back(back, normed, inverse, gain):
    scaled = back * gain
    inner = jnp.mean(scaled, axis=-1, keepdims=True)
    along = jnp.mean(scaled * normed, axis=-1, keepdims=True)
    return inverse * (scaled - inner - normed * along)


def softmax_lanes(logits, lanes):
    logits = jnp.where(lanes, logits, MASKED)
    powers = jnp.exp(logits - jnp.max(logits, axis=-1, keepdims=True))
    return jnp.where(lanes, powers / jnp.sum(powers, axis=-1, keepdims=True), 0.0)


def turned(value, cosine, sine):
    return value * cosine + pltpu.roll(value, HD // 2, 1) * sine


def attend_kernel(
    dp_size,
    size,
    heads,
    units,
    tokens,
    cotangent,
    params,
    rates,
    bucket,
    lengths,
    choices,
    mixer,
    merger,
    expand,
    shrink,
    rows_out,
    mix_out,
    out_out,
    mask_hbm,
    cosine_hbm,
    sine_hbm,
    info_hbm,
    own,
    seq_info,
    usage,
    qkv_out,
    heads_out,
    attention_hbm,
    second_out,
    share_out,
    up_out,
    down_out,
    rect_out,
    active_out,
    branch_out,
    mine_out,
    twin_out,
    rows_buf,
    slot_col,
    member_col,
    bucket_col,
    mix,
    out,
    qkv,
    head_rows,
    part,
    landing,
    staged,
    last,
    second_buf,
    up,
    branch_buf,
    tile_out,
    mask,
    cosine,
    sine,
    row_info,
    attention_out,
    send,
    recv,
    load_sems,
    tile_sems,
    twin_sem,
):
    micro, rows, width = tokens.shape
    count = lengths.shape[1]
    rect, active = rows_buf, part
    total = rows * size
    copies, loads = Copies(send, recv), Loads(load_sems)
    links, column = Links(size, rows, copies), Column(dp_size, copies)
    half = links.half
    block = mixer.shape[0]
    greet(*links.peers, *column.ring, *column.pair)
    mix_ring = WeightRing(
        column, loads, mixer, lambda i: mix.at[pl.ds(pl.multiple_of(i * block, block), block)]
    )
    out_ring = WeightRing(
        column,
        loads,
        merger,
        lambda i: out.at[:, pl.ds(pl.multiple_of(i * block, block), block)],
    )
    mix_ring.start()
    first_gathers = []
    for m in range(micro):

        def body(where, i, row, m=m):
            value = tokens[m, at(row), :].astype(F32)
            low = normalized(value)[0] * params[ATTEND : ATTEND + 1, :]
            low = (low + params[ATTEND + 1 : ATTEND + 2, :]).astype(BF16)
            rows_buf[at(m * total + where * links.second + i * STEP), :] = low

        over_rows(links.half, body)
        first_gathers.append(Gather(links, rows_buf, m * total))
        first_gathers[m].start()

    starts = [r * rows for r in links.first_ranks] + [r * rows + half for r in links.second_ranks]

    def slots(shape, dimension):
        index = lax.broadcasted_iota(jnp.int32, shape, dimension)
        offset = jnp.full(shape, starts[0], jnp.int32)
        for k in range(1, len(starts)):
            offset = jnp.where(index >= k * half, starts[k] - k * half, offset)
        return index + offset

    def ends(m):
        found, end = [], 0
        for s in range(count):
            end = end + lengths[m, s]
            found.append(end)
        return found

    def members(m, slot):
        member = jnp.zeros(slot.shape, jnp.int32)
        begin = jnp.zeros(slot.shape, jnp.int32)
        for end in ends(m):
            member = member + jnp.where(slot >= end, 1, 0)
            begin = jnp.where(slot >= end, end, begin)
        return member, slot - begin

    def by_member(member, values, other):
        value = jnp.full(member.shape, other)
        for s in range(count):
            value = jnp.where(member == s, values[s], value)
        return value

    chunk = min(128, total)
    lane = lax.broadcasted_iota(jnp.int32, (chunk, LANES), 1)
    slot_row = slots((8, total), 1)
    slot_col[...] = slots((total, LANES), 0)
    member_rows = [members(m, slot_row)[0] for m in range(micro)]
    for m in range(micro):

        def table(c, _, m=m):
            here = pl.ds(pl.multiple_of(c * chunk, chunk), chunk)
            slot = slot_col[here, :]
            member, place = members(m, slot)
            member_col[m, here, :] = member
            seen = (member[:, :1] == member_rows[m][:1, :]) & (slot[:, :1] >= slot_row[:1, :])
            mask[m, here, :] = jnp.where(seen, 0.0, MASKED)
            angle = place.astype(F32) * rates[...]
            turn = jnp.sin(angle)
            cosine[m, here, :] = jnp.cos(angle)
            sine[m, here, :] = jnp.where(lane < HD // 2, -turn, turn)
            natural = lax.broadcasted_iota(jnp.int32, (chunk, total), 1)
            picked = jnp.where(slot[:, :1] == natural, bucket[m : m + 1, :].astype(F32), 0.0)
            bucket_here = jnp.sum(picked, axis=-1, keepdims=True)
            bucket_col[m, here, :] = jnp.broadcast_to(bucket_here, (chunk, LANES))
            used = by_member(member, [H // NHC * (choices[m, s] + 1) for s in range(count)], 0)
            head_on = jnp.where(links.me * heads + lane < used, 1.0, 0.0)
            first_unit = jnp.full(lane.shape, links.me * units, jnp.int32).astype(F32)
            unit_on = jnp.where(first_unit < FF // NB * (bucket_here + 1.0), 1.0, 0.0)
            row_info[m, here, :] = jnp.where(
                lane < heads, head_on, jnp.where(lane == heads, unit_on, 0.0)
            )
            return 0

        lax.fori_loop(0, total // chunk, table, 0)
    for g in first_gathers:
        g.middle()
    mix_ring.advance()
    outs, rows_saves = [], []
    usage[...] = jnp.zeros_like(usage)
    few = lax.broadcasted_iota(jnp.int32, (8, LANES), 1)
    which = lax.broadcasted_iota(jnp.int32, (8, LANES), 0)
    lane_own = lax.broadcasted_iota(jnp.int32, (half, LANES), 1)
    for m, g in enumerate(first_gathers):
        g.finish()
        here = pl.ds(m * total, total)
        rows_saves.append(loads.copy(rows_buf.at[here], rows_out.at[here]))
        sequence = lax.broadcasted_iota(jnp.int32, (8, total), 0)
        hot = jnp.where(member_rows[m] == sequence, 1.0, 0.0).astype(BF16)
        divisor = jnp.maximum(by_member(which, [lengths[m, s] for s in range(count)], 0), 1)
        divisor = divisor.astype(F32)
        chosen = by_member(which, [choices[m, s] for s in range(count)], 0)
        means = dot(hot, rows_buf[here, :]) / divisor[:, :1]
        logits = jnp.full((8, LANES), MASKED)
        for c in range(NHC):
            router = params[HEAD_ROUTER + c : HEAD_ROUTER + c + 1, :]
            logit = jnp.sum(means * router, axis=-1, keepdims=True)
            logits = jnp.where(few == c, logit, logits)
        share = softmax_lanes(logits, few < NHC)
        picked = jnp.sum(jnp.where(few == chosen, share, 0.0), axis=-1, keepdims=True)
        table = jnp.where(few == PICKED, picked, share)
        table = jnp.where(few == DIVISOR, divisor, table)
        seq_info[m] = jnp.where(few == CHOSEN, chosen.astype(F32), table)
        for where in range(2):
            source = pl.ds(where * links.second, half)
            member = member_col[m, source, :]
            gate = by_member(member, [NHC * picked[s : s + 1, :] for s in range(count)], 0.0)
            choice = by_member(member, [choices[m, s] for s in range(count)], -NHC)
            live = jnp.where(member < count, 1.0, 0.0)
            kind = bucket_col[m, source, :].astype(jnp.int32)
            hot = (lane_own == kind) | (lane_own == CHOICE + choice)
            hot = hot | ((lane_own == SEQ + member) & (member < count))
            value = jnp.where(hot & (choice >= -NHC), 1.0, 0.0)
            value = jnp.where(lane_own == GATE, gate, value)
            value = jnp.where(lane_own == LIVE, live, value)
            own[m, pl.ds(where * half, half), :] = value
            usage[0:1, :] += jnp.sum(value * live, axis=0, keepdims=True)
    if column.chips > 2:
        mix_ring.advance()
    out_ring.start()
    mix_ring.advance_all()
    out_ring.advance()
    mix_ring.finish()
    outs.append(loads.copy(mix, mix_out))
    up_ring = WeightRing(
        column, loads, expand, lambda i: up.at[pl.ds(pl.multiple_of(i * block, block), block)]
    )
    down_ring = WeightRing(column, loads, shrink, lambda i: down_out.at[i])
    scale = HD ** (-0.5)
    span = 3 * HD
    tile = min(512, width)
    saves = outs

    def project(m):
        base = m * total
        cos, sin = cosine[m], sine[m]

        def head(h, _):
            mixed = dot(
                rows_buf[pl.ds(base, total), :], mix[:, pl.ds(pl.multiple_of(h * span, HD), span)]
            )
            here = pl.ds(pl.multiple_of(h * HD, HD), HD)
            qkv[m, 0, :, here] = turned(mixed[:, :HD], cos, sin).astype(BF16)
            qkv[m, 1, :, here] = turned(mixed[:, HD : 2 * HD], cos, sin).astype(BF16)
            qkv[m, 2, :, here] = mixed[:, 2 * HD :].astype(BF16)
            return 0

        lax.fori_loop(0, heads, head, 0)

    def attend(m):
        base = m * total

        def some(c, _):
            rows_here = pl.ds(pl.multiple_of(c * chunk, chunk), chunk)
            bias_here = mask[m, rows_here, :]
            info = row_info[m, rows_here, :]
            for h in range(heads):
                here = pl.ds(h * HD, HD)
                scores = dot_nt(qkv[m, 0, rows_here, here], qkv[m, 1, :, here]) * scale + bias_here
                peak = jnp.max(scores, axis=-1, keepdims=True)
                powers = jnp.exp(scores - peak)
                share = powers / jnp.sum(powers, axis=-1, keepdims=True)
                value = dot(share.astype(BF16), qkv[m, 2, :, here]).astype(BF16)
                value = value.astype(F32) * info[:, h : h + 1]
                head_rows[pl.ds(pl.multiple_of(base + c * chunk, chunk), chunk), here] = value.astype(
                    BF16
                )
            return 0

        lax.fori_loop(0, total // chunk, some, 0)

    def merge(m):
        base = m * total

        def body(j, _):
            here = pl.ds(pl.multiple_of(j * tile, tile), tile)
            part[pl.ds(base, total), here] = dot(
                head_rows[pl.ds(base, total), :], out[:, here]
            ).astype(BF16)
            return 0

        lax.fori_loop(0, width // tile, body, 0)

    scatters = [
        Scatter(
            links,
            part,
            m * total,
            landing.at[m],
            staged.at[m],
            last.at[m],
            attention_out.at[m],
        )
        for m in range(micro)
    ]
    gathers = [Gather(links, second_buf, m * total) for m in range(micro)]

    def second_norm(m):
        scatter = scatters[m]

        def body(where, i, row):
            attended = scatter.chunk(where, i)
            info = own[m, at(row), :]
            hidden = tokens[m, at(row), :].astype(F32) + info[:, GATE : GATE + 1] * attended
            attention_out[m, at(row), :] = attended
            low = normalized(hidden)[0] * params[FEED : FEED + 1, :]
            low = (low + params[FEED + 1 : FEED + 2, :]).astype(BF16)
            second_buf[at(m * total + where * links.second + i * STEP), :] = low
            low = low.astype(F32)
            lane = lax.broadcasted_iota(jnp.int32, (STEP, LANES), 1)
            logits = jnp.full((STEP, LANES), MASKED)
            for b in range(NB):
                router = params[WIDTH_ROUTER + b : WIDTH_ROUTER + b + 1, :]
                logits = jnp.where(lane == b, jnp.sum(low * router, axis=-1, keepdims=True), logits)
            share = softmax_lanes(logits, lane < NB)
            share_out[m, at(row), :] = share
            gate = NB * jnp.sum(share * info, axis=-1, keepdims=True)
            outer = cotangent[m, at(row), :].astype(F32) * info[:, LIVE : LIVE + 1]
            branch_buf[at(m * total + where * links.second + i * STEP), :] = (gate * outer).astype(
                BF16
            )

        over_rows(half, body)

    for m in range(micro):
        project(m)
        if m == 0:
            if column.chips > 2:
                out_ring.advance()
            up_ring.start()
        attend(m)
        if m == 0:
            out_ring.finish()
            outs.append(loads.copy(out, out_out))
        else:
            scatters[m - 1].middle()
        merge(m)
        scatters[m].start()
    branch_gathers = [Gather(links, branch_buf, m * total) for m in range(micro)]
    up_ring.advance()
    for m in range(micro):
        scatters[m].finish()
        second_norm(m)
        gathers[m].start()
        if m + 1 < micro:
            scatters[m + 1].middle()
            gathers[m].middle()
            if column.chips > 2:
                up_ring.advance()
    down_ring.start()
    saves.append(loads.copy(attention_out, attention_hbm))
    for here, there in (
        (mask, mask_hbm),
        (cosine, cosine_hbm),
        (sine, sine_hbm),
        (row_info, info_hbm),
    ):
        saves.append(loads.copy(here, there))
    saves.append(loads.copy(qkv, qkv_out))
    saves.append(loads.copy(head_rows, heads_out))
    gathers[micro - 1].middle()
    for g in branch_gathers:
        g.start()
    for m in range(micro):
        gathers[m].finish()
        here = pl.ds(m * total, total)
        saves.append(loads.copy(second_buf.at[here], second_out.at[here]))
    up_ring.finish()
    saves.append(loads.copy(up, up_out))
    wait_all(rows_saves)
    step = min(512, units)
    for m in range(micro):

        def widen(j, _, m=m):
            here = pl.ds(pl.multiple_of(j * step, step), step)
            before = dot(second_buf[pl.ds(m * total, total), :], up[:, here])
            kept = jnp.maximum(before, 0.0) * row_info[m, :, heads : heads + 1]
            rect[pl.ds(m * total, total), here] = kept.astype(BF16)
            active[pl.ds(m * total, total), here] = (kept * kept).astype(BF16)
            return 0

        lax.fori_loop(0, units // step, widen, 0)
        here = pl.ds(m * total, total)
        saves.append(loads.copy(rect.at[here, pl.ds(0, units)], rect_out.at[here]))
        saves.append(loads.copy(active.at[here, pl.ds(0, units)], active_out.at[here]))
        if m == 0:
            for g in branch_gathers:
                g.middle()
            down_ring.advance()
    for m, g in enumerate(branch_gathers):
        g.finish()
        here = pl.ds(m * total, total)
        saves.append(loads.copy(branch_buf.at[here], branch_out.at[here]))
    wide = tile_out.shape[3]

    def make(c, put):
        value = dot_tn(active[:, pl.ds(pl.multiple_of(c * wide, wide), wide)], branch_buf[...])
        for j in range(dp_size):
            put(j, value[:, j * block : (j + 1) * block].astype(BF16))

    halves_out(
        column,
        units // wide,
        make,
        tile_out,
        mine_out,
        twin_out,
        tile_sems,
        twin_sem,
        down_ring.advance if column.chips > 2 else None,
    )
    down_ring.finish()
    wait_all(saves)


def narrow_kernel(
    dp_size,
    size,
    down_hbm,
    up_hbm,
    active_hbm,
    rect_hbm,
    branch_hbm,
    second_hbm,
    tokens,
    cotangent,
    attention,
    share,
    own,
    params,
    mine_hbm,
    twin_hbm,
    block_out,
    mine_out,
    twin_out,
    hidden_out,
    back_out,
    stats_out,
    gate_out,
    sum_out,
    landed_out,
    gathered_out,
    down,
    up,
    active,
    rect,
    shared_rows,
    part,
    landing,
    staged,
    last,
    total_rows,
    gate_back,
    tile,
    sum_own,
    sum_other,
    sum_landing,
    sum_staged,
    sum_tile,
    send,
    recv,
    load_sems,
    tile_sems,
    twin_sem,
    sum_sems,
):
    micro, rows, width = tokens.shape
    total = rows * size
    units = up.shape[1]
    copies, loads = Copies(send, recv), Loads(load_sems)
    links, column = Links(size, rows, copies), Column(dp_size, copies)
    half = links.half
    here = [pl.ds(m * total, total) for m in range(micro)]
    ring = SumRing(
        column,
        loads,
        mine_hbm,
        twin_hbm,
        sum_out,
        sum_own,
        sum_other,
        sum_landing,
        sum_staged,
        sum_tile,
        sum_sems,
    )
    ring.load()
    down_copies = columns_in(loads, down_hbm, down)
    active_copies = [loads.copy(active_hbm.at[h], active.at[h]) for h in here]
    branch_copies = [loads.copy(branch_hbm.at[h], shared_rows.at[h]) for h in here]
    rect_copy = loads.copy(rect_hbm.at[here[0]], rect)
    up_copy = loads.copy(up_hbm, up)
    stats_out[...] = jnp.zeros_like(stats_out)
    gate_out[...] = jnp.zeros_like(gate_out)
    greet(*links.peers, *column.ring, *column.pair)
    ring.start()
    step = min(512, units)
    tile_cols = min(512, width)
    outs = [
        Scatter(
            links, part, m * total, landing.at[m], staged.at[m], last.at[m], total_rows.at[m]
        )
        for m in range(micro)
    ]
    backs = [
        Scatter(
            links,
            part,
            m * total,
            landing.at[micro + m],
            staged.at[micro + m],
            last.at[micro + m],
            hidden_out.at[m],
        )
        for m in range(micro)
    ]
    wait_all(down_copies)
    for m in range(micro):
        active_copies[m].wait()

        def body(j, _, m=m):
            cols = pl.ds(pl.multiple_of(j * tile_cols, tile_cols), tile_cols)
            part[here[m], cols] = dot(active[here[m], :], down[:, cols]).astype(BF16)
            return 0

        lax.fori_loop(0, width // tile_cols, body, 0)
        outs[m].start()
    for m in range(micro):
        branch_copies[m].wait()
        rect_copy.wait()

        def body(j, _, m=m):
            cols = pl.ds(pl.multiple_of(j * step, step), step)
            back = dot_nt(shared_rows[here[m], :], down[cols, :])
            active[here[m], cols] = (2.0 * rect[:, cols].astype(F32) * back).astype(BF16)
            return 0

        lax.fori_loop(0, units // step, body, 0)
        if m + 1 < micro:
            rect_copy = loads.copy(rect_hbm.at[here[m + 1]], rect)
        if m == 0:
            up_copy.wait()
    second_copies = [loads.copy(second_hbm.at[h], shared_rows.at[h]) for h in here]
    if column.chips > 2:
        ring.advance()
    for m in range(micro):
        outs[m].middle()

        def body(j, _, m=m):
            cols = pl.ds(pl.multiple_of(j * tile_cols, tile_cols), tile_cols)
            part[here[m], cols] = dot_nt(active[here[m], :], up[cols, :]).astype(BF16)
            return 0

        lax.fori_loop(0, width // tile_cols, body, 0)
        backs[m].start()

    def finish_out(m):
        outs[m].finish()

        def body(where, i, row):
            branch = outs[m].chunk(where, i)
            info = own[m, at(row), :]
            live = info[:, LIVE : LIVE + 1]
            outer = cotangent[m, at(row), :].astype(F32) * live
            hidden = tokens[m, at(row), :].astype(F32)
            hidden = hidden + info[:, GATE : GATE + 1] * attention[m, at(row), :]
            gate = NB * jnp.sum(share[m, at(row), :] * info, axis=-1, keepdims=True)
            block_out[m, at(row), :] = (live * (hidden + gate * branch)).astype(BF16)
            value = jnp.sum(outer * branch, axis=-1, keepdims=True)
            gate_back[m, at(row), :] = jnp.broadcast_to(value, (STEP, LANES))

        over_rows(half, body)

    def finish_back(m):
        backs[m].finish()

        def body(where, i, row):
            back = backs[m].chunk(where, i)
            info = own[m, at(row), :]
            portions = share[m, at(row), :]
            live = info[:, LIVE : LIVE + 1]
            outer = cotangent[m, at(row), :].astype(F32) * live
            hidden = tokens[m, at(row), :].astype(F32)
            attended = attention[m, at(row), :]
            hidden = hidden + info[:, GATE : GATE + 1] * attended
            normed, inverse = normalized(hidden)
            gain = params[FEED : FEED + 1, :]
            low = (normed * gain + params[FEED + 1 : FEED + 2, :]).astype(BF16).astype(F32)
            picked = jnp.sum(portions * info, axis=-1, keepdims=True)
            logit_back = NB * picked * (info - portions) * gate_back[m, at(row), :]
            for b in range(NB):
                column = logit_back[:, b : b + 1]
                back = back + column * params[WIDTH_ROUTER + b : WIDTH_ROUTER + b + 1, :]
                stats_out[2 + b : 3 + b, :] += jnp.sum(column * low, axis=0, keepdims=True)
            stats_out[0:1, :] += jnp.sum(back * normed, axis=0, keepdims=True)
            stats_out[1:2, :] += jnp.sum(back, axis=0, keepdims=True)
            hidden_back = outer + norm_back(back, normed, inverse, gain)
            hidden_out[m, at(row), :] = hidden_back
            attention_back = (info[:, GATE : GATE + 1] * hidden_back).astype(BF16)
            if m == 0:
                shared_rows[at(where * links.second + i * STEP), :] = attention_back
            else:
                back_out[m - 1, at(row), :] = attention_back
            gate_part = jnp.sum(hidden_back * attended, axis=-1, keepdims=True)
            gate_out[m : m + 1, :] += jnp.sum(info * gate_part, axis=0, keepdims=True)

        over_rows(half, body)

    wait_all(second_copies)
    block = mine_out.shape[1]

    def make(c, ref):
        ref[...] = dot_tn(
            shared_rows[:, pl.ds(pl.multiple_of(c * block, block), block)], active[...]
        ).astype(BF16)

    early, other, staged_up = [up.at[pl.ds(i * block, block)] for i in range(3)]
    up_ring = SumRing(
        column, loads, mine_out, twin_out, None, early, other, landed_out, staged_up, None, None
    )

    def start_up():
        up_ring.load()
        up_ring.start(more=False)

    blocks_out(column, make, tile, mine_out, twin_out, tile_sems, twin_sem, start_up)
    if column.chips > 3:
        ring.advance()
    for m in range(micro):
        finish_out(m)
    for m in range(micro):
        backs[m].middle()
    gather = Gather(links, shared_rows, 0)
    for m in range(micro):
        finish_back(m)
        if m == 0:
            gather.start()
    gather.middle()
    ring.finish()
    gather.finish()
    save = loads.copy(shared_rows.at[pl.ds(0, total)], gathered_out)
    up_ring.hop.wait()
    save.wait()


STATS_ONE = 6
STATS_USE = 12
STATS_ROWS = 16
SEQ_COUNT = 4


def attend_back_kernel(
    dp_size,
    size,
    heads,
    back,
    gathered_hbm,
    gate,
    out_hbm,
    qkv_hbm,
    heads_hbm,
    rows_hbm,
    mask_hbm,
    mix_hbm,
    cosine,
    sine,
    row_info,
    mine_hbm,
    twin_hbm,
    landed_hbm,
    tokens,
    hidden_hbm,
    own,
    seq_info,
    params,
    stats_two,
    usage,
    back_out,
    up_sum,
    mix_sum,
    out_sum,
    stats_out,
    mix_mine,
    mix_twin,
    out_mine,
    out_twin,
    buf,
    out,
    qkv,
    head_rows,
    rows_buf,
    mask,
    heads_back,
    mixed_back,
    score_back,
    shares,
    out_tile,
    mix_tile,
    gates,
    mix,
    landing,
    staged,
    last,
    hidden_back,
    *rest,
):
    up_bufs, mix_bufs, out_bufs = rest[:5], rest[5:10], rest[10:15]
    stats, share, pieces, sums, whole = rest[15:20]
    send, recv, load_sems = rest[20:23]
    out_sems, out_twin_sem, mix_sems, mix_twin_sem, up_sum_sems, mix_sum_sems, out_sum_sems = rest[23:]
    micro, rows, width = tokens.shape
    total = rows * size
    copies, loads = Copies(send, recv), Loads(load_sems)
    links, column = Links(size, rows, copies), Column(dp_size, copies)
    half = links.half
    ring = SumRing(column, loads, mine_hbm, twin_hbm, up_sum, *up_bufs, up_sum_sems)
    mix_ring = SumRing(column, loads, mix_mine, mix_twin, mix_sum, *mix_bufs, mix_sum_sems)
    out_ring = SumRing(column, loads, out_mine, out_twin, out_sum, *out_bufs, out_sum_sems)
    ring.prepare(landed_hbm)
    first_copy = loads.copy(gathered_hbm, buf.at[pl.ds(0, total)])
    own_copies = []
    for m in range(1, micro):
        for where in range(2):
            own_copies.append(
                loads.copy(
                    back.at[m - 1, pl.ds(where * half, half)],
                    buf.at[pl.ds(m * total + where * links.second, half)],
                )
            )
    out_copies = [loads.copy(out_hbm, out)]
    qkv_copy = loads.copy(qkv_hbm, qkv)
    mask_copy = loads.copy(mask_hbm, mask)
    heads_copy = loads.copy(heads_hbm, head_rows)
    rows_copy = loads.copy(rows_hbm, rows_buf)
    mix_copy = loads.copy(mix_hbm, mix)
    hidden_copy = loads.copy(hidden_hbm, hidden_back)
    gates[links.me] = gate[...]
    near = [lax.rem(links.me + s, size) for s in range(1, size)]
    far = [lax.rem(column.me + s, dp_size) for s in range(1, dp_size)]
    greet(*[("tensor", to) for to in near], *[("dp", to) for to in far])
    wait_all(own_copies)
    gathers = [Gather(links, buf, m * total) for m in range(1, micro)]
    for g in gathers:
        g.start()
    ring.resume()
    gate_copies = [links.copy(gate, gates.at[links.me], peer) for peer in near]
    stats[...] = jnp.zeros_like(stats)
    stats[0:8, :] = stats_two[...]
    stats[STATS_USE : STATS_USE + 1, 0:LANES] = usage[0:1, :]
    wait_all(out_copies)
    qkv_copy.wait()
    mask_copy.wait()
    scale = HD ** (-0.5)
    chunk = min(128, total)
    block, wide = out_mine.shape[2], out_tile.shape[3]
    here_rows = [pl.ds(m * total, total) for m in range(micro)]
    scatters = [
        Scatter(links, buf, m * total, landing.at[m], staged.at[m], last.at[m], back_out.at[m])
        for m in range(micro)
    ]

    def heads_part(m):
        base = m * total
        every = pl.ds(base, total)
        value = dot_nt(buf[every, :], out[...])
        for h in range(heads):
            here = pl.ds(h * HD, HD)
            heads_back[:, here] = (
                value[:, h * HD : (h + 1) * HD] * row_info[m, :, h : h + 1]
            ).astype(BF16)
        for h in range(heads):
            here = pl.ds(h * HD, HD)

            def some(c, _, m=m, here=here):
                rows_here = pl.ds(pl.multiple_of(c * chunk, chunk), chunk)
                scores = dot_nt(qkv[m, 0, rows_here, here], qkv[m, 1, :, here]) * scale
                scores = scores + mask[m, rows_here, :]
                powers = jnp.exp(scores - jnp.max(scores, axis=-1, keepdims=True))
                share = powers / jnp.sum(powers, axis=-1, keepdims=True)
                share_back = dot_nt(heads_back[rows_here, here], qkv[m, 2, :, here])
                inner = jnp.sum(share * share_back, axis=-1, keepdims=True)
                score_back[rows_here, :] = (share * (share_back - inner)).astype(BF16)
                shares[rows_here, :] = share.astype(BF16)
                return 0

            lax.fori_loop(0, total // chunk, some, 0)
            cos, sin = cosine[m], -sine[m]
            query_back = dot(score_back[...], qkv[m, 1, :, here]) * scale
            keys_back = dot_tn(score_back[...], qkv[m, 0, :, here]) * scale
            values_back = dot_tn(shares[...], heads_back[:, here])
            col = 3 * h * HD
            mixed_back[every, pl.ds(col, HD)] = turned(query_back, cos, sin).astype(BF16)
            mixed_back[every, pl.ds(col + HD, HD)] = turned(keys_back, cos, sin).astype(BF16)
            mixed_back[every, pl.ds(col + 2 * HD, HD)] = values_back.astype(BF16)
            if m == 0 and h == 0:
                for g in gathers:
                    g.middle()

    def make_out(c, put):
        value = dot_tn(head_rows[:, pl.ds(pl.multiple_of(c * wide, wide), wide)], buf[...])
        for j in range(dp_size):
            put(j, value[:, j * block : (j + 1) * block].astype(BF16))

    def make_mix(c, ref):
        ref[...] = dot_tn(
            rows_buf[:, pl.ds(pl.multiple_of(c * block, block), block)], mixed_back[...]
        ).astype(BF16)

    tile = min(512, width)

    def first_part(m):
        def body(j, _):
            cols = pl.ds(pl.multiple_of(j * tile, tile), tile)
            buf[here_rows[m], cols] = dot_nt(mixed_back[here_rows[m], :], mix[cols, :]).astype(BF16)
            return 0

        lax.fori_loop(0, width // tile, body, 0)
        scatters[m].start()

    first_copy.wait()
    heads_part(0)
    for g in gathers:
        g.finish()
    heads_copy.wait()
    halves_out(
        column,
        heads * HD // wide,
        make_out,
        out_tile,
        out_mine,
        out_twin,
        out_sems,
        out_twin_sem,
    )
    if column.chips > 3:
        ring.advance()
    out_ring.load()
    out_ring.start()
    mix_copy.wait()
    hidden_copy.wait()
    first_part(0)
    for m in range(1, micro):
        heads_part(m)
    scatters[0].middle()
    rows_copy.wait()

    def start_mix():
        mix_ring.load()
        mix_ring.start(more=False)

    blocks_out(column, make_mix, mix_tile, mix_mine, mix_twin, mix_sems, mix_twin_sem, start_mix)
    mix_ring.load()
    if column.chips > 2:
        out_ring.advance()
    for m in range(1, micro):
        first_part(m)
    for made in gate_copies:
        made.wait()
    gate_sum = gates[0]
    for r in range(1, size):
        gate_sum = gate_sum + gates[r]

    def last_rows(m):
        s = scatters[m]
        s.finish()
        count = SEQ_COUNT
        lane = lax.broadcasted_iota(jnp.int32, (8, LANES), 1)
        which = lax.broadcasted_iota(jnp.int32, (8, LANES), 0)
        info = seq_info[m]
        gate_back = jnp.where(lane == SEQ + which, gate_sum[m : m + 1, :], 0.0)
        gate_back = jnp.sum(gate_back, axis=-1, keepdims=True)
        chosen = jnp.where(lane == info[:, CHOSEN : CHOSEN + 1].astype(jnp.int32), 1.0, 0.0)
        logit_back = NHC * info[:, PICKED : PICKED + 1] * (chosen - info) * gate_back
        logit_back = logit_back / info[:, DIVISOR : DIVISOR + 1]

        def body(where, i, row):
            back = s.chunk(where, i)
            normed, inverse = normalized(tokens[m, at(row), :].astype(F32))
            gain = params[ATTEND : ATTEND + 1, :]
            low = (normed * gain + params[ATTEND + 1 : ATTEND + 2, :]).astype(BF16).astype(F32)
            rows_info = own[m, at(row), :]
            spread = jnp.zeros((STEP, LANES), F32)
            for q in range(count):
                spread = spread + rows_info[:, SEQ + q : SEQ + q + 1] * logit_back[q : q + 1, :]
            for c in range(NHC):
                part = spread[:, c : c + 1]
                back = back + part * params[HEAD_ROUTER + c : HEAD_ROUTER + c + 1, :]
                at_row = STATS_ONE + 2 + c
                stats[at_row : at_row + 1, :] += jnp.sum(part * low, axis=0, keepdims=True)
            at_row = STATS_ONE
            stats[at_row : at_row + 1, :] += jnp.sum(back * normed, axis=0, keepdims=True)
            stats[at_row + 1 : at_row + 2, :] += jnp.sum(back, axis=0, keepdims=True)
            value = norm_back(back, normed, inverse, gain)
            back_out[m, at(row), :] = hidden_back[m, at(row), :] + value

        over_rows(links.half, body)

    if column.chips > 3:
        out_ring.advance()
    if column.chips > 2:
        mix_ring.advance()
    last_rows(0)
    for s in scatters[1:]:
        s.middle()
    if column.chips > 3:
        mix_ring.advance()
    ring.finish()
    for m in range(1, micro):
        last_rows(m)

    piece = width // size
    mine = pl.ds(pl.multiple_of(links.me * piece, piece), piece)
    sent = [
        links.copy(
            stats.at[:, pl.ds(pl.multiple_of(to * piece, piece), piece)], pieces.at[links.me], to
        )
        for to in near
    ]
    pieces[links.me] = stats[:, mine]
    wait_all(sent)
    value = pieces[0]
    for r in range(1, size):
        value = value + pieces[r]
    share[0] = value
    sums[column.me] = value
    sent = [column.copy(share.at[0], sums.at[column.me], to) for to in far]
    out_ring.finish()
    mix_ring.finish()
    wait_all(sent)
    value = sums[0]
    for r in range(1, dp_size):
        value = value + sums[r]
    share[1] = value
    whole[links.me] = value
    wait_all([links.copy(share.at[1], whole.at[links.me], to) for to in near])
    for r in range(size):
        stats_out[:, r * piece : (r + 1) * piece] = whole[r]


ANY = pl.BlockSpec(memory_space=pl.ANY)
VMEM = pl.BlockSpec(memory_space=pltpu.VMEM)
SMEM = pl.BlockSpec(memory_space=pltpu.SMEM)


def call(kernel, ident, ins, outs, scratch, copies, loads, extra=(), flops=0, limit=56):
    dma = pltpu.SemaphoreType.DMA
    sems = [dma((copies,)), dma((copies,)), dma((loads,))] + [dma((n,)) for n in extra]
    moved = sum(a.size * a.dtype.itemsize for a, _ in ins)
    return pl.pallas_call(
        kernel,
        out_shape=[jax.ShapeDtypeStruct(shape, kind) for shape, kind, _ in outs],
        in_specs=[SMEM if near == "s" else VMEM if near else ANY for _, near in ins],
        out_specs=[VMEM if near else ANY for _, _, near in outs],
        scratch_shapes=[pltpu.VMEM(shape, kind) for shape, kind in scratch] + sems,
        compiler_params=pltpu.CompilerParams(
            collective_id=ident, has_side_effects=True, vmem_limit_bytes=limit * MIB
        ),
        cost_estimate=pl.CostEstimate(flops=flops, bytes_accessed=moved, transcendentals=0),
    )(*[a for a, _ in ins])


def local(
    dp_size,
    size,
    tokens,
    cotangent,
    mixer,
    merger,
    expand,
    shrink,
    attend_gain,
    attend_bias,
    feed_gain,
    feed_bias,
    width_router,
    head_router,
    lengths,
    head_choice,
    width_bucket,
):
    micro, rows, width = tokens.shape
    total = width_bucket.shape[1]
    every = micro * total
    half = rows // 2
    high = size // 2
    heads = merger.shape[0] // HD
    units = expand.shape[1]
    block = width // dp_size
    chips = dp_size // 2
    few = transfers(size)
    ringed = ring_copies(dp_size)

    vectors = jnp.concatenate([attend_gain, attend_bias, feed_gain, feed_bias]).reshape(4, width)
    params = jnp.concatenate(
        [vectors, jnp.concatenate([width_router, head_router], axis=1).T], axis=0
    ).astype(F32)
    rates = jnp.power(10000.0, -2.0 * jnp.arange(HD // 2, dtype=F32) / HD)
    rates = jnp.concatenate([rates, rates])[None]

    tables = (micro, total, LANES)
    lands = half * (2 * (high - 1) + high)
    stages = half * high
    wide_heads = heads * HD
    span = 3 * wide_heads
    buffers = [((micro, lands, width), BF16), ((micro, stages, width), BF16), ((micro, stages, width), BF16)]
    attended = call(
        functools.partial(attend_kernel, dp_size, size, heads, units),
        2,
        [
            (tokens, True),
            (cotangent, True),
            (params, True),
            (rates, True),
            (width_bucket, True),
            (lengths, "s"),
            (head_choice, "s"),
            (mixer, False),
            (merger, False),
            (expand, False),
            (shrink, False),
        ],
        [
            ((every, width), BF16, False),
            ((width, span), BF16, False),
            ((wide_heads, width), BF16, False),
            ((micro, total, total), F32, False),
            (tables, F32, False),
            (tables, F32, False),
            (tables, F32, False),
            ((micro, rows, LANES), F32, True),
            ((micro, 8, LANES), F32, True),
            ((8, LANES), F32, True),
            ((micro, 3, total, wide_heads), BF16, False),
            ((every, wide_heads), BF16, False),
            ((micro, rows, width), F32, False),
            ((every, width), BF16, False),
            ((micro, rows, LANES), F32, True),
            ((width, units), BF16, False),
            ((dp_size, units, block), BF16, False),
            ((every, units), BF16, False),
            ((every, units), BF16, False),
            ((every, width), BF16, False),
            ((chips, units, block), BF16, False),
            ((chips, units, block), BF16, False),
        ],
        [
            ((every, width), BF16),
            ((total, LANES), jnp.int32),
            (tables, jnp.int32),
            (tables, F32),
            ((width, span), BF16),
            ((wide_heads, width), BF16),
            ((micro, 3, total, wide_heads), BF16),
            ((every, wide_heads), BF16),
            ((every, width), BF16),
        ]
        + buffers
        + [
            ((every, width), BF16),
            ((width, units), BF16),
            ((every, width), BF16),
            ((2, 2, chips, min(256, units), block), BF16),
            ((micro, total, total), F32),
            (tables, F32),
            (tables, F32),
            (tables, F32),
            ((micro, rows, width), F32),
        ],
        4 * micro * few + 4 * ringed,
        4 + micro + 2 + 2 + micro + 1 + 3 * micro + 5,
        (4, 1),
        flops=2 * every * width * (span + wide_heads + 2 * units),
        limit=63,
    )
    first_rows, mix_weight, out_weight, mask, cosine, sine, row_info = attended[:7]
    own, seq_info, usage, qkv, head_rows, attention, second_rows = attended[7:14]
    width_share, up_weight, down_weight, rect, active, branch_rows = attended[14:20]
    down_mine, down_twin = attended[20:]

    narrowed = call(
        functools.partial(narrow_kernel, dp_size, size),
        4,
        [
            (down_weight, False),
            (up_weight, False),
            (active, False),
            (rect, False),
            (branch_rows, False),
            (second_rows, False),
            (tokens, True),
            (cotangent, True),
            (attention, True),
            (width_share, True),
            (own, True),
            (params, True),
            (down_mine, False),
            (down_twin, False),
        ],
        [
            ((micro, rows, width), BF16, True),
            ((chips, block, units), BF16, False),
            ((chips, block, units), BF16, False),
            ((micro, rows, width), F32, True),
            ((micro - 1, rows, width), BF16, True),
            ((8, width), F32, True),
            ((8, LANES), F32, True),
            ((units, block), F32, False),
            ((1, block, units), BF16, False),
            ((total, width), BF16, False),
        ],
        [
            ((units, width), BF16),
            ((width, units), BF16),
            ((every, units), BF16),
            ((total, units), BF16),
            ((every, width), BF16),
            ((every, width), BF16),
            ((2 * micro, lands, width), BF16),
            ((2 * micro, stages, width), BF16),
            ((2 * micro, stages, width), BF16),
            ((micro, rows, width), F32),
            ((micro, rows, LANES), F32),
            ((2, block, units), BF16),
        ]
        + sum_scratch(chips, units, block),
        2 * micro * few + few + chips,
        dp_size + 4 * micro + 1 + 2 * chips + 3,
        (2, chips, SUM_TILES),
        flops=8 * every * width * units,
        limit=63,
    )
    block_output, up_mine, up_twin, hidden_back, back_own, stats_two, gate_part = narrowed[:7]
    down_sum, up_landed, back_rows = narrowed[7:]

    out_tile = min(256, wide_heads)
    lasts = call(
        functools.partial(attend_back_kernel, dp_size, size, heads),
        5,
        [
            (back_own, False),
            (back_rows, False),
            (gate_part, True),
            (out_weight, False),
            (qkv, False),
            (head_rows, False),
            (first_rows, False),
            (mask, False),
            (mix_weight, False),
            (cosine, True),
            (sine, True),
            (row_info, True),
            (up_mine, False),
            (up_twin, False),
            (up_landed, False),
            (tokens, True),
            (hidden_back, False),
            (own, True),
            (seq_info, True),
            (params, True),
            (stats_two, True),
            (usage, True),
        ],
        [
            ((micro, rows, width), F32, True),
            ((block, units), F32, False),
            ((block, span), F32, False),
            ((wide_heads, block), F32, False),
            ((STATS_ROWS, width), F32, True),
            ((chips, block, span), BF16, False),
            ((chips, block, span), BF16, False),
            ((chips, wide_heads, block), BF16, False),
            ((chips, wide_heads, block), BF16, False),
        ],
        [
            ((every, width), BF16),
            ((wide_heads, width), BF16),
            ((micro, 3, total, wide_heads), BF16),
            ((every, wide_heads), BF16),
            ((every, width), BF16),
            ((micro, total, total), F32),
            ((total, wide_heads), BF16),
            ((every, span), BF16),
            ((total, total), BF16),
            ((total, total), BF16),
            ((2, 2, chips, out_tile, block), BF16),
            ((2, block, span), BF16),
            ((size, 8, LANES), F32),
            ((width, span), BF16),
        ]
        + buffers
        + [((micro, rows, width), F32)]
        + sum_scratch(chips, block, units)
        + sum_scratch(chips, block, span)
        + sum_scratch(chips, wide_heads, block)
        + [
            ((STATS_ROWS, width), F32),
            ((2, STATS_ROWS, width // size), F32),
            ((size, STATS_ROWS, width // size), F32),
            ((dp_size, STATS_ROWS, width // size), F32),
            ((size, STATS_ROWS, width // size), F32),
        ],
        2 * micro * few + 3 * (size - 1) + dp_size - 1 + 3 * (chips - 1),
        2 * micro + dp_size + 7 + 6 * chips,
        (4, 1, 2, chips, SUM_TILES, SUM_TILES, SUM_TILES),
        flops=4 * every * width * (wide_heads + span) + 20 * heads * micro * total * total * HD,
        limit=63,
    )
    tokens_gradient, up_sum, mix_sum, out_sum, stats = lasts[:5]
    return (
        block_output,
        tokens_gradient,
        mix_sum,
        out_sum,
        up_sum,
        down_sum,
        stats[STATS_ONE],
        stats[STATS_ONE + 1],
        stats[0],
        stats[1],
        stats[2 : 2 + NB].T,
        stats[STATS_ONE + 2 : STATS_ONE + 2 + NHC].T,
        stats[STATS_USE, :NB],
        stats[STATS_USE, CHOICE : CHOICE + NHC],
    )


def solution(mesh):
    def run(*args):
        return local(mesh.shape["dp"], mesh.shape["tensor"], *args)

    rows = P(None, ("dp", "tensor"), None)
    tall, wide = P("dp", "tensor"), P("tensor", "dp")
    weights = (tall, wide, tall, wide)
    return jax.shard_map(
        run,
        mesh=mesh,
        in_specs=(rows, rows) + weights + (P(),) * 6 + (P(None, "dp"),) * 3,
        out_specs=(rows, rows) + weights + (P(),) * 8,
        check_vma=False,
    )
```
